128 devices in a mesh: rows: 16 (over z, y), cols: 8 (over x, core).
Axes of the slice: x: 4, y: 4, z: 4, core: 2. Of those that a mesh axis runs over, the one named last changes fastest.
Arguments:
- start_basis: bfloat16 [65536, 128], P('rows'), may hold values from -6 to 6
- block_values: bfloat16 [16, 8, 32, 256, 256], P('rows', 'cols'), may hold values from -0.15625 to 0.15625
- slot_count: int32 [16, 8], P('rows', 'cols'), may hold values from 1 to 32, as said below
- slot_row: int32 [16, 8, 32], P('rows', 'cols'), may hold values from 0 to 15
- slot_col: int32 [16, 8, 32], P('rows', 'cols'), may hold values from 0 to 255, as said below
Outputs:
- new_basis: float32 [65536, 128], P(('rows', 'cols'))
- triangle: float32 [128, 128], replicated
The draws below stay inside these ranges and needn't reach their ends.
Inputs may be any that keep to these rules, and one draw needn't show every extreme that they name: `slot_count`: exactly one device in every draw holds 32 live slots. `slot_col`: on device (r, c) every slot's block column j has (j % 16) // 2 equal to c; pairs may repeat, and repeated blocks add.
All inputs are finite; a program needn't handle non-finite values.
Results may differ from the reference program's by a relative error of at most 0.0021.
Values may be sent and summed in bfloat16 or wider, within the bound.
A program may use at most 64 MiB of HBM per device.

```python
import jax
import jax.numpy as jnp
from jax import lax

K = 128
BS = 256
RB = 16
MAXB = 32
NB = 256
N = 65536
N_ROWS = 16
N_COLS = 8


def draw_slot_count(key, part):
    key = jax.random.fold_in(key, 11)
    first, second = jax.random.split(key)
    counts = jax.random.randint(first, (N_ROWS * N_COLS,), max(1, MAXB // 10), MAXB // 2 + 1)
    chosen = jax.random.randint(second, (), 0, N_ROWS * N_COLS)
    counts = jnp.where(jnp.arange(N_ROWS * N_COLS) == chosen, MAXB, counts)
    return counts.reshape(N_ROWS, N_COLS).astype(jnp.int32)


def draw_slot_row(key, part):
    key = jax.random.fold_in(key, 23)
    return jax.random.randint(key, (N_ROWS, N_COLS, MAXB), 0, RB).astype(jnp.int32)


def draw_slot_col(key, part):
    key = jax.random.fold_in(key, 37)
    first, second = jax.random.split(key)
    panels = jax.random.randint(first, (N_ROWS, N_COLS, MAXB), 0, N_ROWS)
    within = jax.random.randint(second, (N_ROWS, N_COLS, MAXB), 0, RB // N_COLS)
    column_ids = jnp.arange(N_COLS, dtype=jnp.int32)[None, :, None]
    return (panels * RB + column_ids * (RB // N_COLS) + within).astype(jnp.int32)


def block_scale(rng, shape, cuts, smallest, top_value):
    level = 1.0
    for axis_at, parts in cuts:
        steps = jax.random.uniform(jax.random.fold_in(jax.random.fold_in(rng, 6), axis_at), (parts,), jnp.float32, smallest / len(cuts), top_value / len(cuts))
        level = level * jnp.repeat(jnp.exp(steps), shape[axis_at] // parts).reshape((-1,) + (1,) * (len(shape) - 1 - axis_at))
    return level


def noise(key, extent, spread, limit, cuts=(), kind=jnp.bfloat16):
    level = block_scale(key, extent, cuts, -0.22, 0.18) if cuts else 1.0
    values = jax.random.normal(key, extent, jnp.float32) * spread * level
    return jnp.minimum(jnp.maximum(values, -limit), limit).astype(kind)


def setup_inputs(seed: int = 0) -> dict:
    arg_keys = jax.random.split(jax.random.key(seed), 6)
    return {
        "start_basis": noise(arg_keys[0], (N, K), 1.0, 6.0, ((0, 16),)),
        "block_values": noise(arg_keys[1], (N_ROWS, N_COLS, MAXB, BS, BS), (6 * BS) ** -0.5, 0.15625, ((0, 16), (1, 8))),
        "slot_count": draw_slot_count(jax.random.fold_in(arg_keys[5], 71), 0),
        "slot_row": draw_slot_row(jax.random.fold_in(arg_keys[5], 71), 0),
        "slot_col": draw_slot_col(jax.random.fold_in(arg_keys[5], 71), 0),
    }


def reference(start_basis, block_values, slot_count, slot_row, slot_col):
    basis_blocks = start_basis.reshape(NB, BS, K)
    slot_ids = jnp.arange(MAXB, dtype=jnp.int32)
    live_mask = (slot_ids[None, None, :] < slot_count[:, :, None]).astype(jnp.float32)

    def forward(items):
        values, masks, rowids, colids = items
        values = values.reshape(N_COLS * MAXB, BS, BS).astype(jnp.float32)
        masks = masks.reshape(N_COLS * MAXB)
        rowids = rowids.reshape(N_COLS * MAXB).astype(jnp.int32)
        colids = colids.reshape(N_COLS * MAXB).astype(jnp.int32)
        picked = basis_blocks[colids].astype(jnp.float32)
        terms = jnp.einsum('sab,sbk->sak', values, picked) * masks[:, None, None]
        return jnp.zeros((RB, BS, K), jnp.float32).at[rowids].add(terms)
    image = lax.map(forward, (block_values, live_mask, slot_row, slot_col))
    image = image.astype(jnp.bfloat16)

    def backward(total, items):
        values, masks, rowids, colids, panel = items
        values = values.reshape(N_COLS * MAXB, BS, BS).astype(jnp.float32)
        masks = masks.reshape(N_COLS * MAXB)
        rowids = rowids.reshape(N_COLS * MAXB).astype(jnp.int32)
        colids = colids.reshape(N_COLS * MAXB).astype(jnp.int32)
        picked = panel[rowids].astype(jnp.float32)
        terms = jnp.einsum('sab,sak->sbk', values, picked) * masks[:, None, None]
        return (total.at[colids].add(terms), None)
    gathered, unused = lax.scan(backward, jnp.zeros((NB, BS, K), jnp.float32), (block_values, live_mask, slot_row, slot_col, image))
    gathered = gathered.reshape(N, K)
    ortho, upper = jnp.linalg.qr(gathered)
    signs = jnp.where(jnp.diagonal(upper) < 0, -1.0, 1.0).astype(jnp.float32)
    root = jnp.sqrt(jnp.float32(N))
    return (ortho * signs[None, :] * root, upper * signs[:, None] / root)
```

```python
import functools

import jax
import jax.numpy as jnp
from jax import lax
from jax.experimental import pallas as pl
from jax.experimental.pallas import tpu as pltpu
from jax.sharding import PartitionSpec as P

SUB = 8
VMEM = pl.BlockSpec(memory_space=pltpu.VMEM)
SMEM = pl.BlockSpec(memory_space=pltpu.SMEM)
ANY = pl.BlockSpec(memory_space=pl.ANY)
NT = (((1,), (1,)), ((), ()))


def matmul(a, b, dims):
    return lax.dot_general(
        a, b, dims, precision=lax.Precision.HIGHEST, preferred_element_type=jnp.float32
    )


def fetch_live(count, values, tiles, sems):
    def start(slot, carry):
        pltpu.make_async_copy(values.at[slot], tiles.at[slot], sems.at[slot]).start()
        return carry

    lax.fori_loop(0, count, start, 0)


def forward_kernel(count_ref, row_ref, col_ref, basis, values, out, tiles, sems):
    count = count_ref[0]
    fetch_live(count, values, tiles, sems)
    out[...] = jnp.zeros_like(out)

    def step(slot, carry):
        pltpu.make_async_copy(values.at[slot], tiles.at[slot], sems.at[slot]).wait()
        term = jnp.dot(tiles[slot], basis[col_ref[slot]], preferred_element_type=jnp.float32)
        out[row_ref[slot]] += term
        return carry

    lax.fori_loop(0, count, step, 0)


def backward_kernel(count_ref, row_ref, col_ref, image, values, out, tiles, flipped, sems):
    count = count_ref[0]
    fetch_live(count, values, tiles, sems)
    out[...] = jnp.zeros_like(out)

    def flip(row, carry):
        flipped[row] = image[row].T
        return carry

    lax.fori_loop(0, image.shape[0], flip, 0)

    def step(slot, carry):
        pltpu.make_async_copy(values.at[slot], tiles.at[slot], sems.at[slot]).wait()
        term = jnp.dot(flipped[row_ref[slot]], tiles[slot], preferred_element_type=jnp.float32)
        out[col_ref[slot]] += term
        return carry

    lax.fori_loop(0, count, step, 0)


def forward(count, rows, cols, basis, values, panel_blocks):
    slots, width, _ = values.shape
    depth = basis.shape[2]
    return pl.pallas_call(
        forward_kernel,
        out_shape=jax.ShapeDtypeStruct((panel_blocks, width, depth), jnp.float32),
        in_specs=[SMEM, SMEM, SMEM, VMEM, ANY],
        out_specs=VMEM,
        scratch_shapes=[
            pltpu.VMEM((slots, width, width), values.dtype),
            pltpu.SemaphoreType.DMA((slots,)),
        ],
        compiler_params=pltpu.CompilerParams(vmem_limit_bytes=32 << 20),
    )(count, rows, cols, basis, values)


def backward(count, rows, cols, image, values, total_blocks):
    slots, width, _ = values.shape
    panel_blocks, _, depth = image.shape
    return pl.pallas_call(
        backward_kernel,
        out_shape=jax.ShapeDtypeStruct((total_blocks, depth, width), jnp.float32),
        in_specs=[SMEM, SMEM, SMEM, VMEM, ANY],
        out_specs=VMEM,
        scratch_shapes=[
            pltpu.VMEM((slots, width, width), values.dtype),
            pltpu.VMEM((panel_blocks, depth, width), image.dtype),
            pltpu.SemaphoreType.DMA((slots,)),
        ],
        compiler_params=pltpu.CompilerParams(vmem_limit_bytes=32 << 20),
    )(count, rows, cols, image, values)


def factor(gram, upper_ref, inverse_ref):
    order = gram.shape[0]
    lead = gram
    tail = (
        lax.broadcasted_iota(jnp.int32, (order, order), 0)
        == lax.broadcasted_iota(jnp.int32, (order, order), 1)
    ).astype(jnp.float32)
    for base in range(0, order, SUB):
        left = order - base
        columns = [
            jnp.broadcast_to(lead[:, base + k : base + k + 1], (left, order)) for k in range(SUB)
        ]
        position = lax.broadcasted_iota(jnp.int32, (left, order), 0)
        top = lax.broadcasted_iota(jnp.int32, (SUB, order), 0)
        lane = lax.broadcasted_iota(jnp.int32, (SUB, order), 1)
        pivots = jnp.zeros((SUB, order), jnp.float32)
        for k in range(SUB):
            pivot = columns[k][k : k + 1, :]
            pivots = jnp.where(top == k, pivot, pivots)
            ratio = jnp.where(position > k, columns[k] * (1.0 / pivot), 0.0)
            lead = lead - ratio * lead[k : k + 1, :]
            tail = tail - ratio * tail[k : k + 1, :]
            for j in range(k + 1, SUB):
                columns[j] = columns[j] - ratio * columns[j][k : k + 1, :]
        scale = 1.0 / jnp.sqrt(pivots)
        upper_ref[base : base + SUB, :] = jnp.where(lane >= base + top, lead[:SUB] * scale, 0.0)
        inverse_ref[base : base + SUB, :] = tail[:SUB] * scale
        lead = lead[SUB:]
        tail = tail[SUB:]


def first_kernel(gram_ref, x_ref, upper_ref, q_ref, part_ref, inverse):
    factor(gram_ref[...], upper_ref, inverse)
    for s in range(x_ref.shape[0]):
        q_ref[s] = matmul(inverse[...], x_ref[s], (((1,), (0,)), ((), ())))
    part_ref[...] = matmul(q_ref[0], q_ref[0], NT)
    for s in range(1, x_ref.shape[0]):
        part_ref[...] += matmul(q_ref[s], q_ref[s], NT)


def last_kernel(root, gram_ref, upper_ref, q_ref, basis_ref, triangle_ref, second, inverse):
    factor(gram_ref[...], second, inverse)
    width = q_ref.shape[2]
    for s in range(q_ref.shape[0]):
        done = matmul(inverse[...], q_ref[s], (((1,), (0,)), ((), ())))
        basis_ref[s * width : (s + 1) * width, :] = done.T * root
    triangle_ref[...] = matmul(second[...], upper_ref[...], (((1,), (0,)), ((), ()))) / root


def gram_kernel(x_ref, part_ref):
    part_ref[...] = matmul(x_ref[0], x_ref[0], NT)
    for s in range(1, x_ref.shape[0]):
        part_ref[...] += matmul(x_ref[s], x_ref[s], NT)


def body(start_basis, block_values, slot_count, slot_row, slot_col):
    depth = start_basis.shape[1]
    width = block_values.shape[-1]
    panel_blocks = start_basis.shape[0] // width
    sub_blocks = panel_blocks // lax.axis_size("cols")
    col_index = lax.axis_index("cols")
    own_part = lax.dynamic_slice_in_dim(
        start_basis, col_index * sub_blocks * width, sub_blocks * width, 0
    )
    basis_parts = lax.all_gather(own_part, "rows", axis=0, tiled=True).reshape(-1, width, depth)
    values = block_values[0, 0]
    count = slot_count[0]
    row_ids = slot_row[0, 0]
    col_ids = slot_col[0, 0]
    local_cols = col_ids // panel_blocks * sub_blocks + col_ids % sub_blocks
    image_part = forward(count, row_ids, local_cols, basis_parts, values, panel_blocks)
    image = lax.psum(image_part, "cols").astype(jnp.bfloat16)
    back_part = backward(count, row_ids, local_cols, image, values, basis_parts.shape[0])
    mine = lax.psum_scatter(back_part, "rows", scatter_dimension=0, tiled=True)

    square = jax.ShapeDtypeStruct((depth, depth), jnp.float32)
    room = pltpu.VMEM((depth, depth), jnp.float32)
    part = pl.pallas_call(gram_kernel, out_shape=square, in_specs=[VMEM], out_specs=VMEM)(mine)
    gram = lax.psum(part, ("rows", "cols"))
    upper, interim, part = pl.pallas_call(
        first_kernel,
        out_shape=[square, jax.ShapeDtypeStruct(mine.shape, jnp.float32), square],
        in_specs=[VMEM] * 2,
        out_specs=[VMEM] * 3,
        scratch_shapes=[room],
    )(gram, mine)
    gram = lax.psum(part, ("rows", "cols"))
    root = float(lax.axis_size("rows") * panel_blocks * width) ** 0.5
    return pl.pallas_call(
        functools.partial(last_kernel, root),
        out_shape=[jax.ShapeDtypeStruct((sub_blocks * width, depth), jnp.float32), square],
        in_specs=[VMEM] * 3,
        out_specs=[VMEM] * 2,
        scratch_shapes=[room, room],
    )(gram, upper, interim)


def solution(mesh):
    return jax.shard_map(
        body,
        mesh=mesh,
        in_specs=(
            P("rows", None),
            P("rows", "cols", None, None, None),
            P("rows", "cols"),
            P("rows", "cols", None),
            P("rows", "cols", None),
        ),
        out_specs=(P(("rows", "cols"), None), P()),
        check_vma=False,
    )
```

```python
import functools

import jax
import jax.numpy as jnp
from jax import lax
from jax.experimental import pallas as pl
from jax.experimental.pallas import tpu as pltpu
from jax.sharding import PartitionSpec as P

SUB = 8
RING = 4
VMEM = pl.BlockSpec(memory_space=pltpu.VMEM)
SMEM = pl.BlockSpec(memory_space=pltpu.SMEM)
ANY = pl.BlockSpec(memory_space=pl.ANY)
NN = (((1,), (0,)), ((), ()))
NT = (((1,), (1,)), ((), ()))


def matmul(a, b, dims):
    return lax.dot_general(
        a, b, dims, precision=lax.Precision.HIGHEST, preferred_element_type=jnp.float32
    )


class Wires:
    def __init__(self, send, recv):
        self.send, self.recv, self.used = send, recv, []

    def start(self, src, dst, device):
        at = len(self.used)
        copy = pltpu.make_async_remote_copy(
            src_ref=src,
            dst_ref=dst,
            send_sem=self.send.at[at],
            recv_sem=self.recv.at[at],
            device_id=device,
            device_id_type=pl.DeviceIdType.MESH,
        )
        copy.start()
        self.used.append(copy)
        return copy

    def drain(self):
        for copy in self.used:
            copy.wait_send()


def greet(peers):
    barrier = pltpu.get_barrier_semaphore()
    for peer in peers:
        pl.semaphore_signal(
            barrier, inc=1, device_id=peer, device_id_type=pl.DeviceIdType.MESH
        )
    pl.semaphore_wait(barrier, len(peers))


def shifted(at, offset):
    return lax.rem(at + offset % RING, RING)


class Plane:
    def __init__(self):
        row = lax.axis_index("rows")
        self.col = lax.axis_index("cols")
        self.z, self.y = row // RING, lax.rem(row, RING)

    def row(self, half, first, second):
        along_y, along_z = (first, second) if half == 0 else (second, first)
        return shifted(self.z, along_z) * RING + shifted(self.y, along_y)

    def device(self, half, first, second):
        return (self.row(half, first, second), self.col)

    def neighbours(self):
        return [self.device(0, 1, 0), self.device(0, 3, 0), self.device(0, 0, 1), self.device(0, 0, 3)]


GATHER_COPIES = 40


def gather_kernel(own, out, send, recv, local):
    plane = Plane()
    wires = Wires(send, recv)
    me = plane.row(0, 0, 0)
    keep = pltpu.make_async_copy(own, out.at[me], local)
    keep.start()
    greet(plane.neighbours())
    cut = own.shape[1] // 2
    upper, lower = pl.ds(0, cut), pl.ds(cut, cut)

    def both_ways(half, first, axis, src):
        dst = out.at[plane.row(half, first, 0), half]
        if axis == 0:
            return [wires.start(src, dst, plane.device(half, s, 0)) for s in (1, 3)]
        return [wires.start(src, dst, plane.device(half, 0, s)) for s in (1, 3)]

    along_first = [both_ways(h, 0, 0, own.at[h]) for h in (0, 1)]
    along_second = {(h, 0): both_ways(h, 0, 1, own.at[h]) for h in (0, 1)}
    relays = []
    for h in (0, 1):
        pair = []
        for at, (come_from, part, onward) in enumerate(((3, upper, 1), (1, lower, 3))):
            along_first[h][at].wait_recv()
            piece = out.at[plane.row(h, come_from, 0), h, part]
            pair.append(wires.start(piece, piece, plane.device(h, onward, 0)))
        relays.append(pair)
    for h in (0, 1):
        for f in (3, 1):
            along_second[h, f] = both_ways(h, f, 1, out.at[plane.row(h, f, 0), h])
    last = []

    def pass_on(h, f):
        for at, (come_from, part, onward) in enumerate(((3, upper, 1), (1, lower, 3))):
            along_second[h, f][at].wait_recv()
            piece = out.at[plane.row(h, f, come_from), h, part]
            last.append(wires.start(piece, piece, plane.device(h, 0, onward)))

    for h in (0, 1):
        pass_on(h, 0)
    for h in (0, 1):
        for copy in relays[h]:
            copy.wait_recv()
        along_second[h, 2] = both_ways(h, 2, 1, out.at[plane.row(h, 2, 0), h])
    for f in (3, 1, 2):
        for h in (0, 1):
            pass_on(h, f)
    for copy in last:
        copy.wait_recv()
    keep.wait()
    wires.drain()


def gather(own, rows):
    return pl.pallas_call(
        gather_kernel,
        out_shape=jax.ShapeDtypeStruct((rows,) + own.shape, own.dtype),
        in_specs=[VMEM],
        out_specs=VMEM,
        scratch_shapes=[
            pltpu.SemaphoreType.DMA((GATHER_COPIES,)),
            pltpu.SemaphoreType.DMA((GATHER_COPIES,)),
            pltpu.SemaphoreType.DMA,
        ],
        compiler_params=pltpu.CompilerParams(
            collective_id=0, has_side_effects=True, vmem_limit_bytes=32 << 20
        ),
    )(own)


IMAGE_COPIES = 24


def image_kernel(part, image, sibling, total, relayed, merged, final, send, recv):
    row, col = lax.axis_index("rows"), lax.axis_index("cols")
    x, core = col // 2, lax.rem(col, 2)
    twin = (row, x * 2 + 1 - core)
    right, left = ((row, shifted(x, s) * 2 + core) for s in (1, 3))
    wires = Wires(send, recv)
    greet([twin, right, left])
    sub = image.shape[0] // 8

    def chunk(offset, which):
        return pl.ds((shifted(x, offset) * 2 + which) * sub, sub)

    order = (2, 1, 3, 0)
    swap = {
        o: wires.start(part.at[chunk(o, 1 - core)], sibling.at[o], twin) for o in order
    }
    for o in order:
        swap[o].wait_recv()
        total[o] = part[chunk(o, core)] + sibling[o]
        if o == 2:
            up = wires.start(total.at[2, 0], relayed.at[0], right)
            down = wires.start(total.at[2, 1], relayed.at[1], left)
        elif o == 1:
            right_plain = wires.start(total.at[1, 1], final.at[0, 1], right)
        elif o == 3:
            left_plain = wires.start(total.at[3, 0], final.at[1, 0], left)
    up.wait_recv()
    merged[0] = total[1, 0] + relayed[0]
    right_sum = wires.start(merged.at[0], final.at[0, 0], right)
    down.wait_recv()
    merged[1] = total[3, 1] + relayed[1]
    left_sum = wires.start(merged.at[1], final.at[1, 1], left)

    mine = (x * 2 + core) * sub
    left_plain.wait_recv()
    right_sum.wait_recv()
    image[mine] = (total[0, 0] + (final[0, 0] + final[1, 0])).T.astype(image.dtype)
    sends = []
    for b in range(2):
        if b == 1:
            right_plain.wait_recv()
            left_sum.wait_recv()
            image[mine + 1] = (total[0, 1] + (final[0, 1] + final[1, 1])).T.astype(image.dtype)
        block = image.at[mine + b]
        sends.append([wires.start(block, block, peer) for peer in (right, left, twin)])
    hops = []
    for o, at, b_on, onward in ((3, 0, 0, right), (1, 1, 1, left)):
        start = (shifted(x, o) * 2 + core) * sub
        for b in (0, 1):
            sends[b][at].wait_recv()
            block = image.at[start + b]
            if b == b_on:
                hops.append(wires.start(block, block, onward))
        pair = image.at[pl.ds(start, sub)]
        sends.append([wires.start(pair, pair, twin)])
    far = (shifted(x, 2) * 2 + core) * sub
    for b in (0, 1):
        hops[b].wait_recv()
        block = image.at[far + b]
        sends.append([wires.start(block, block, twin)])
    for b in (0, 1):
        sends[b][2].wait_recv()
    for copies in sends[2:]:
        copies[0].wait_recv()
    wires.drain()


def sum_image(part):
    blocks, width, depth = part.shape
    f32 = jnp.float32
    return pl.pallas_call(
        image_kernel,
        out_shape=jax.ShapeDtypeStruct((blocks, depth, width), jnp.bfloat16),
        in_specs=[VMEM],
        out_specs=VMEM,
        scratch_shapes=[
            pltpu.VMEM((RING, 2, width, depth), f32),
            pltpu.VMEM((RING, 2, width, depth), f32),
            pltpu.VMEM((2, width, depth), f32),
            pltpu.VMEM((2, width, depth), f32),
            pltpu.VMEM((2, 2, width, depth), f32),
            pltpu.SemaphoreType.DMA((IMAGE_COPIES,)),
            pltpu.SemaphoreType.DMA((IMAGE_COPIES,)),
        ],
        compiler_params=pltpu.CompilerParams(
            collective_id=1, has_side_effects=True, vmem_limit_bytes=32 << 20
        ),
    )(part)


SCATTER_COPIES = 36


def scatter_sum(plane, wires, part, out, relayed, merged, final, total, hop, joined, close):
    def block(h, first, second):
        return plane.row(h, first, second) * 2 + h

    ups, downs = (2, 1), (3, 0)
    ways = ((0, 1, ups, downs), (1, 3, downs, ups))
    relay, flow = {}, {}
    for h in (0, 1):
        for way, step, onward, plain in ways:
            for slot, s in enumerate(onward):
                relay[h, way, slot] = wires.start(
                    part.at[block(h, 2, s)], relayed.at[h, way, slot], plane.device(h, step, 0)
                )
    for slot in (0, 1):
        for h in (0, 1):
            for way, step, onward, plain in ways:
                s = plain[slot]
                flow[h, way, s] = wires.start(
                    part.at[block(h, step, s)], final.at[h, way, s], plane.device(h, step, 0)
                )
    for slot in (0, 1):
        for h in (0, 1):
            for way, step, onward, plain in ways:
                s = onward[slot]
                relay[h, way, slot].wait_recv()
                merged[h, way, slot] = part[block(h, step, s)] + relayed[h, way, slot]
                flow[h, way, s] = wires.start(
                    merged.at[h, way, slot], final.at[h, way, s], plane.device(h, step, 0)
                )
    cut = out.shape[1] // 2
    low, high = pl.ds(0, cut), pl.ds(cut, cut)
    steps = ((0, 1, low, high), (1, 3, high, low))
    near, direct, ended = {}, {}, {}
    for s in (2, 3, 1, 0):
        for h in (0, 1):
            flow[h, 0, s].wait_recv()
            flow[h, 1, s].wait_recv()
            total[h, s] = part[block(h, 0, s)] + (final[h, 0, s] + final[h, 1, s])
            for way, step, onward, plain in steps:
                if s == 2:
                    near[h, way] = wires.start(
                        total.at[h, 2, onward], hop.at[h, way], plane.device(h, 0, step)
                    )
                elif s == step:
                    direct[h, way] = wires.start(
                        total.at[h, s, plain], close.at[h, way, plain], plane.device(h, 0, step)
                    )
    for h in (0, 1):
        for way, step, onward, plain in steps:
            near[h, way].wait_recv()
            joined[h, way] = total[h, step, onward] + hop[h, way]
            ended[h, way] = wires.start(
                joined.at[h, way], close.at[h, way, onward], plane.device(h, 0, step)
            )
    for h in (0, 1):
        for way in (0, 1):
            direct[h, way].wait_recv()
            ended[h, way].wait_recv()
        out[h] = total[h, 0] + (close[h, 0] + close[h, 1])


def scatter_rooms(depth, width):
    f32 = jnp.float32
    return [
        pltpu.VMEM((2, 2, 2, depth, width), f32),
        pltpu.VMEM((2, 2, 2, depth, width), f32),
        pltpu.VMEM((2, 2, RING, depth, width), f32),
        pltpu.VMEM((2, RING, depth, width), f32),
        pltpu.VMEM((2, 2, depth // 2, width), f32),
        pltpu.VMEM((2, 2, depth // 2, width), f32),
        pltpu.VMEM((2, 2, depth, width), f32),
    ]


SQUARE_COPIES = 7 + 15 + 7


def sum_square(wires, part, out, by_col, by_row, mine):
    rows, cols = lax.axis_size("rows"), lax.axis_size("cols")
    row, col = lax.axis_index("rows"), lax.axis_index("cols")
    share = part.shape[0] // cols

    def span(at):
        return pl.ds(at * share, share)

    first = []
    for o in range(1, cols):
        peer = lax.rem(col + o, cols)
        first.append(wires.start(part.at[span(peer)], by_col.at[col], (row, peer)))
    by_col[col] = part[span(col)]
    for copy in first:
        copy.wait_recv()
    mine[...] = jnp.sum(by_col[...], axis=0)
    second = []
    for o in range(1, rows):
        second.append(wires.start(mine, by_row.at[row], (lax.rem(row + o, rows), col)))
    by_row[row] = mine[...]
    for copy in second:
        copy.wait_recv()
    out[span(col)] = jnp.sum(by_row[...], axis=0)
    third = []
    for o in range(1, cols):
        third.append(
            wires.start(out.at[span(col)], out.at[span(col)], (row, lax.rem(col + o, cols)))
        )
    for copy in third:
        copy.wait_recv()


def square_rooms(order, rows, cols):
    share = order // cols
    return [
        pltpu.VMEM((cols, share, order), jnp.float32),
        pltpu.VMEM((rows, share, order), jnp.float32),
        pltpu.VMEM((share, order), jnp.float32),
    ]


def all_peers():
    rows, cols = lax.axis_size("rows"), lax.axis_size("cols")
    row, col = lax.axis_index("rows"), lax.axis_index("cols")
    return [(lax.rem(row + o, rows), col) for o in range(1, rows)] + [
        (row, lax.rem(col + o, cols)) for o in range(1, cols)
    ]


def fetch_live(count, values, tiles, sems):
    def start(slot, carry):
        pltpu.make_async_copy(values.at[slot], tiles.at[slot], sems.at[slot]).start()
        return carry

    lax.fori_loop(0, count, start, 0)


def forward_kernel(count_ref, row_ref, col_ref, basis, values, out, tiles, sems):
    count = count_ref[0]
    fetch_live(count, values, tiles, sems)
    out[...] = jnp.zeros_like(out)

    def step(slot, carry):
        pltpu.make_async_copy(values.at[slot], tiles.at[slot], sems.at[slot]).wait()
        term = jnp.dot(tiles[slot], basis[col_ref[slot]], preferred_element_type=jnp.float32)
        out[row_ref[slot]] += term
        return carry

    lax.fori_loop(0, count, step, 0)


def backward_kernel(count_ref, row_ref, col_ref, image, values, out, tiles, sems):
    count = count_ref[0]
    fetch_live(count, values, tiles, sems)
    out[...] = jnp.zeros_like(out)

    def step(slot, carry):
        pltpu.make_async_copy(values.at[slot], tiles.at[slot], sems.at[slot]).wait()
        term = jnp.dot(image[row_ref[slot]], tiles[slot], preferred_element_type=jnp.float32)
        out[col_ref[slot]] += term
        return carry

    lax.fori_loop(0, count, step, 0)


def products(kernel, out_shape, count, rows, cols, panels, values):
    return pl.pallas_call(
        kernel,
        out_shape=jax.ShapeDtypeStruct(out_shape, jnp.float32),
        in_specs=[SMEM, SMEM, SMEM, VMEM, ANY],
        out_specs=VMEM,
        scratch_shapes=[
            pltpu.VMEM(values.shape, values.dtype),
            pltpu.SemaphoreType.DMA((values.shape[0],)),
        ],
        compiler_params=pltpu.CompilerParams(vmem_limit_bytes=32 << 20),
    )(count, rows, cols, panels, values)


def factor(gram, upper_ref, inverse_ref):
    order = gram.shape[0]
    lead = gram
    tail = (
        lax.broadcasted_iota(jnp.int32, (order, order), 0)
        == lax.broadcasted_iota(jnp.int32, (order, order), 1)
    ).astype(jnp.float32)
    for base in range(0, order, SUB):
        left = order - base
        columns = [
            jnp.broadcast_to(lead[:, base + k : base + k + 1], (left, order)) for k in range(SUB)
        ]
        position = lax.broadcasted_iota(jnp.int32, (left, order), 0)
        top = lax.broadcasted_iota(jnp.int32, (SUB, order), 0)
        lane = lax.broadcasted_iota(jnp.int32, (SUB, order), 1)
        pivots = jnp.zeros((SUB, order), jnp.float32)
        for k in range(SUB):
            pivot = columns[k][k : k + 1, :]
            pivots = jnp.where(top == k, pivot, pivots)
            ratio = jnp.where(position > k, columns[k] * (1.0 / pivot), 0.0)
            lead = lead - ratio * lead[k : k + 1, :]
            tail = tail - ratio * tail[k : k + 1, :]
            for j in range(k + 1, SUB):
                columns[j] = columns[j] - ratio * columns[j][k : k + 1, :]
        scale = 1.0 / jnp.sqrt(pivots)
        upper_ref[base : base + SUB, :] = jnp.where(lane >= base + top, lead[:SUB] * scale, 0.0)
        inverse_ref[base : base + SUB, :] = tail[:SUB] * scale
        lead = lead[SUB:]
        tail = tail[SUB:]


def inner(x_ref, out):
    out[...] = matmul(x_ref[0], x_ref[0], NT) + matmul(x_ref[1], x_ref[1], NT)


def basis_kernel(
    root, part, basis_ref, triangle_ref, x_ref, square, gram, upper, second, inverse, *rest
):
    rooms, (by_col, by_row, mine, by_col2, by_row2, mine2, send, recv) = rest[:7], rest[7:]
    plane = Plane()
    wires = Wires(send, recv)
    greet(all_peers())
    scatter_sum(plane, wires, part, x_ref, *rooms)
    inner(x_ref, square)
    sum_square(wires, square, gram, by_col, by_row, mine)
    factor(gram[...], upper, inverse)
    for s in range(2):
        x_ref[s] = matmul(inverse[...], x_ref[s], NN)
    wires.drain()
    wires = Wires(send, recv)
    wires.send = send.at[pl.ds(SCATTER_COPIES + SQUARE_COPIES, SQUARE_COPIES)]
    wires.recv = recv.at[pl.ds(SCATTER_COPIES + SQUARE_COPIES, SQUARE_COPIES)]
    inner(x_ref, square)
    sum_square(wires, square, gram, by_col2, by_row2, mine2)
    factor(gram[...], second, inverse)
    width = x_ref.shape[2]
    for s in range(2):
        basis_ref[s * width : (s + 1) * width, :] = matmul(inverse[...], x_ref[s], NN).T * root
    triangle_ref[...] = matmul(second[...], upper[...], NN) / root
    wires.drain()


def orthonormalize(root, part):
    _, depth, width = part.shape
    rows, cols = lax.axis_size("rows"), lax.axis_size("cols")
    copies = SCATTER_COPIES + 2 * SQUARE_COPIES
    f32 = jnp.float32
    square = pltpu.VMEM((depth, depth), f32)
    return pl.pallas_call(
        functools.partial(basis_kernel, root),
        out_shape=[
            jax.ShapeDtypeStruct((2 * width, depth), f32),
            jax.ShapeDtypeStruct((depth, depth), f32),
        ],
        in_specs=[VMEM],
        out_specs=[VMEM] * 2,
        scratch_shapes=[pltpu.VMEM((2, depth, width), f32)]
        + [square] * 5
        + scatter_rooms(depth, width)
        + square_rooms(depth, rows, cols) * 2
        + [pltpu.SemaphoreType.DMA((copies,)), pltpu.SemaphoreType.DMA((copies,))],
        compiler_params=pltpu.CompilerParams(
            collective_id=2, has_side_effects=True, vmem_limit_bytes=40 << 20
        ),
    )(part)


def body(start_basis, block_values, slot_count, slot_row, slot_col):
    depth = start_basis.shape[1]
    width = block_values.shape[-1]
    panel_blocks = start_basis.shape[0] // width
    rows, cols = lax.axis_size("rows"), lax.axis_size("cols")
    sub_blocks = panel_blocks // cols
    own = lax.dynamic_slice_in_dim(
        start_basis.reshape(panel_blocks, width, depth),
        lax.axis_index("cols") * sub_blocks,
        sub_blocks,
        0,
    )
    basis_parts = gather(own, rows).reshape(rows * sub_blocks, width, depth)
    values = block_values[0, 0]
    count = slot_count[0]
    row_ids = slot_row[0, 0]
    col_ids = slot_col[0, 0]
    local_cols = col_ids // panel_blocks * sub_blocks + col_ids % sub_blocks
    image_part = products(
        forward_kernel, (panel_blocks, width, depth), count, row_ids, local_cols, basis_parts, values
    )
    image = sum_image(image_part)
    back_part = products(
        backward_kernel, (rows * sub_blocks, depth, width), count, row_ids, local_cols, image, values
    )
    return tuple(orthonormalize(float(rows * panel_blocks * width) ** 0.5, back_part))


def solution(mesh):
    return jax.shard_map(
        body,
        mesh=mesh,
        in_specs=(
            P("rows", None),
            P("rows", "cols", None, None, None),
            P("rows", "cols"),
            P("rows", "cols", None),
            P("rows", "cols", None),
        ),
        out_specs=(P(("rows", "cols"), None), P()),
        check_vma=False,
    )
```

```python
import functools

import jax
import jax.numpy as jnp
from jax import lax
from jax.experimental import pallas as pl
from jax.experimental.pallas import tpu as pltpu
from jax.sharding import PartitionSpec as P

SUB = 8
RING = 4
VMEM = pl.BlockSpec(memory_space=pltpu.VMEM)
SMEM = pl.BlockSpec(memory_space=pltpu.SMEM)
HBM = pl.BlockSpec(memory_space=pltpu.HBM)
NN = (((1,), (0,)), ((), ()))
NT = (((1,), (1,)), ((), ()))


def matmul(a, b, dims):
    return lax.dot_general(
        a, b, dims, precision=lax.Precision.HIGHEST, preferred_element_type=jnp.float32
    )


class Wires:
    def __init__(self, send, recv):
        self.send, self.recv, self.used = send, recv, 0

    def start(self, src, dst, device, at=None):
        if at is None:
            at = self.used
            self.used += 1
        copy = pltpu.make_async_remote_copy(
            src_ref=src,
            dst_ref=dst,
            send_sem=self.send,
            recv_sem=self.recv.at[at],
            device_id=device,
            device_id_type=pl.DeviceIdType.MESH,
        )
        copy.start()
        return copy

    def drain(self, *refs):
        for ref in refs:
            pltpu.make_async_copy(ref, ref, self.send).wait()


def greet(peers):
    barrier = pltpu.get_barrier_semaphore()
    for peer in peers:
        pl.semaphore_signal(
            barrier, inc=1, device_id=peer, device_id_type=pl.DeviceIdType.MESH
        )
    pl.semaphore_wait(barrier, len(peers))


def shifted(at, offset):
    return lax.rem(at + offset % RING, RING)


class Plane:
    def __init__(self):
        row = lax.axis_index("rows")
        self.col = lax.axis_index("cols")
        self.z, self.y = row // RING, lax.rem(row, RING)

    def row(self, half, first, second):
        along_y, along_z = (first, second) if half == 0 else (second, first)
        return shifted(self.z, along_z) * RING + shifted(self.y, along_y)

    def device(self, half, first, second):
        return (self.row(half, first, second), self.col)

    def neighbours(self):
        return [self.device(0, 1, 0), self.device(0, 3, 0), self.device(0, 0, 1), self.device(0, 0, 3)]


GATHER_COPIES = 24


def gather_kernel(basis, values, out, tiles, send, recv, local):
    plane = Plane()
    wires = Wires(send, recv)
    load = pltpu.make_async_copy(basis.at[pl.ds(plane.col * 2, 2)], out.at[:, 0, 0], local.at[0])
    load.start()
    keep = pltpu.make_async_copy(values, tiles, local.at[1])
    keep.start()
    greet(plane.neighbours())
    load.wait()
    cut = out.shape[3] // 2
    upper, lower = pl.ds(0, cut), pl.ds(cut, cut)
    near, own, rest, relay, far, ends = {}, {}, {}, {}, {}, {}
    for h in (0, 1):
        src = out.at[h, 0, 0]
        near[h] = [
            wires.start(src, out.at[h, 3, 0], plane.device(h, 1, 0)),
            wires.start(src, out.at[h, 1, 0], plane.device(h, 3, 0)),
        ]
    for h in (0, 1):
        src = out.at[h, 0, 0]
        own[h] = [
            wires.start(src, out.at[h, 0, 3], plane.device(h, 0, 1)),
            wires.start(src, out.at[h, 0, 1], plane.device(h, 0, 3)),
        ]
    for h in (0, 1):
        near[h][0].wait_recv()
        up = wires.start(out.at[h, 3, 0, upper], out.at[h, 2, 0, upper], plane.device(h, 1, 0))
        near[h][1].wait_recv()
        down = wires.start(out.at[h, 1, 0, lower], out.at[h, 2, 0, lower], plane.device(h, 3, 0))
        relay[h] = [up, down]
    for h in (0, 1):
        own[h][0].wait_recv()
        up = wires.start(out.at[h, 0, 3, upper], out.at[h, 0, 2, upper], plane.device(h, 0, 1))
        own[h][1].wait_recv()
        down = wires.start(out.at[h, 0, 1, lower], out.at[h, 0, 2, lower], plane.device(h, 0, 3))
        far[h] = [up, down]
    three = pl.ds(1, 3)
    for h in (0, 1):
        relay[h][0].wait_recv()
        relay[h][1].wait_recv()
        src = out.at[h, three, 0]
        rest[h] = [
            wires.start(src, out.at[h, three, 3], plane.device(h, 0, 1)),
            wires.start(src, out.at[h, three, 1], plane.device(h, 0, 3)),
        ]
    for h in (0, 1):
        rest[h][0].wait_recv()
        up = wires.start(
            out.at[h, three, 3, upper], out.at[h, three, 2, upper], plane.device(h, 0, 1)
        )
        rest[h][1].wait_recv()
        down = wires.start(
            out.at[h, three, 1, lower], out.at[h, three, 2, lower], plane.device(h, 0, 3)
        )
        ends[h] = [up, down]
    for h in (0, 1):
        for copy in far[h] + ends[h]:
            copy.wait_recv()
    keep.wait()
    wires.drain(out.at[0], out.at[1, pl.ds(0, 3)], out.at[1, 3, pl.ds(0, 2)])


def gather(basis, values, rows):
    return pl.pallas_call(
        gather_kernel,
        out_shape=[
            jax.ShapeDtypeStruct((2, rows // RING, RING) + basis.shape[1:], basis.dtype),
            jax.ShapeDtypeStruct(values.shape, values.dtype),
        ],
        in_specs=[HBM, HBM],
        out_specs=[VMEM, VMEM],
        scratch_shapes=[
            pltpu.SemaphoreType.DMA,
            pltpu.SemaphoreType.DMA((GATHER_COPIES,)),
            pltpu.SemaphoreType.DMA((2,)),
        ],
        compiler_params=pltpu.CompilerParams(
            collective_id=0, has_side_effects=True, vmem_limit_bytes=44 << 20
        ),
    )(basis, values)


IMAGE_COPIES = 24


def image_kernel(part, image, sibling, total, relayed, merged, final, send, recv, send2):
    row, col = lax.axis_index("rows"), lax.axis_index("cols")
    x, core = col // 2, lax.rem(col, 2)
    twin = (row, x * 2 + 1 - core)
    right, left = ((row, shifted(x, s) * 2 + core) for s in (1, 3))
    wires = Wires(send, recv)
    greet([twin, right, left])
    sub = image.shape[0] // 8

    def chunk(offset, which):
        return pl.ds((shifted(x, offset) * 2 + which) * sub, sub)

    order = (2, 1, 3, 0)
    swap = {
        o: wires.start(part.at[chunk(o, 1 - core)], sibling.at[o], twin) for o in order
    }
    for o in order:
        swap[o].wait_recv()
        total[o] = part[chunk(o, core)] + sibling[o]
        if o == 2:
            up = wires.start(total.at[2, 0], relayed.at[0], right)
            down = wires.start(total.at[2, 1], relayed.at[1], left)
        elif o == 1:
            right_plain = wires.start(total.at[1, 1], final.at[0, 1], right)
        elif o == 3:
            left_plain = wires.start(total.at[3, 0], final.at[1, 0], left)
    up.wait_recv()
    merged[0] = total[1, 0] + relayed[0]
    right_sum = wires.start(merged.at[0], final.at[0, 0], right)
    down.wait_recv()
    merged[1] = total[3, 1] + relayed[1]
    left_sum = wires.start(merged.at[1], final.at[1, 1], left)

    wires.send = send2
    mine = (x * 2 + core) * sub
    left_plain.wait_recv()
    right_sum.wait_recv()
    image[mine] = (total[0, 0] + (final[0, 0] + final[1, 0])).T.astype(image.dtype)
    sends = []
    for b in range(2):
        if b == 1:
            right_plain.wait_recv()
            left_sum.wait_recv()
            image[mine + 1] = (total[0, 1] + (final[0, 1] + final[1, 1])).T.astype(image.dtype)
        block = image.at[mine + b]
        sends.append([wires.start(block, block, peer) for peer in (right, left, twin)])
    hops = []
    for o, at, b_on, onward in ((3, 0, 0, right), (1, 1, 1, left)):
        start = (shifted(x, o) * 2 + core) * sub
        for b in (0, 1):
            sends[b][at].wait_recv()
            block = image.at[start + b]
            if b == b_on:
                hops.append(wires.start(block, block, onward))
        pair = image.at[pl.ds(start, sub)]
        sends.append([wires.start(pair, pair, twin)])
    far = (shifted(x, 2) * 2 + core) * sub
    for b in (0, 1):
        hops[b].wait_recv()
        block = image.at[far + b]
        sends.append([wires.start(block, block, twin)])
    for b in (0, 1):
        sends[b][2].wait_recv()
    for copies in sends[2:]:
        copies[0].wait_recv()
    wires.drain(image.at[pl.ds(0, 14)])
    wires.send = send
    wires.drain(part.at[pl.ds(0, 14)])


def sum_image(part):
    blocks, width, depth = part.shape
    f32 = jnp.float32
    return pl.pallas_call(
        image_kernel,
        out_shape=jax.ShapeDtypeStruct((blocks, depth, width), jnp.bfloat16),
        in_specs=[VMEM],
        out_specs=VMEM,
        scratch_shapes=[
            pltpu.VMEM((RING, 2, width, depth), f32),
            pltpu.VMEM((RING, 2, width, depth), f32),
            pltpu.VMEM((2, width, depth), f32),
            pltpu.VMEM((2, width, depth), f32),
            pltpu.VMEM((2, 2, width, depth), f32),
            pltpu.SemaphoreType.DMA,
            pltpu.SemaphoreType.DMA((IMAGE_COPIES,)),
            pltpu.SemaphoreType.DMA,
        ],
        compiler_params=pltpu.CompilerParams(
            collective_id=1, has_side_effects=True, vmem_limit_bytes=32 << 20
        ),
    )(part)


SCATTER_COPIES = 36


def scatter_sum(plane, wires, part, out, relayed, merged, final, total, hop, joined, close):
    def block(h, first, second):
        return (h * RING + first) * RING + second

    ups, downs = (2, 1), (3, 0)
    ways = ((0, 1, ups, downs), (1, 3, downs, ups))
    relay, flow = {}, {}
    for h in (0, 1):
        for way, step, onward, plain in ways:
            for slot, s in enumerate(onward):
                relay[h, way, slot] = wires.start(
                    part.at[block(h, 2, s)], relayed.at[h, way, slot], plane.device(h, step, 0)
                )
    for slot in (0, 1):
        for h in (0, 1):
            for way, step, onward, plain in ways:
                s = plain[slot]
                flow[h, way, s] = wires.start(
                    part.at[block(h, step, s)], final.at[h, way, s], plane.device(h, step, 0)
                )
    for slot in (0, 1):
        for h in (0, 1):
            for way, step, onward, plain in ways:
                s = onward[slot]
                relay[h, way, slot].wait_recv()
                merged[h, way, slot] = part[block(h, step, s)] + relayed[h, way, slot]
                flow[h, way, s] = wires.start(
                    merged.at[h, way, slot], final.at[h, way, s], plane.device(h, step, 0)
                )
    cut = out.shape[1] // 2
    low, high = pl.ds(0, cut), pl.ds(cut, cut)
    steps = ((0, 1, low, high), (1, 3, high, low))
    near, direct, ended = {}, {}, {}
    for s in (2, 3, 1, 0):
        for h in (0, 1):
            flow[h, 0, s].wait_recv()
            flow[h, 1, s].wait_recv()
            total[h, s] = part[block(h, 0, s)] + (final[h, 0, s] + final[h, 1, s])
            for way, step, onward, plain in steps:
                if s == 2:
                    near[h, way] = wires.start(
                        total.at[h, 2, onward], hop.at[h, way], plane.device(h, 0, step)
                    )
                elif s == step:
                    direct[h, way] = wires.start(
                        total.at[h, s, plain], close.at[h, way, plain], plane.device(h, 0, step)
                    )
    for h in (0, 1):
        for way, step, onward, plain in steps:
            near[h, way].wait_recv()
            joined[h, way] = total[h, step, onward] + hop[h, way]
            ended[h, way] = wires.start(
                joined.at[h, way], close.at[h, way, onward], plane.device(h, 0, step)
            )
    for h in (0, 1):
        for way in (0, 1):
            direct[h, way].wait_recv()
            ended[h, way].wait_recv()
        out[h] = total[h, 0] + (close[h, 0] + close[h, 1])


def scatter_rooms(depth, width):
    f32 = jnp.float32
    return [
        pltpu.VMEM((2, 2, 2, depth, width), f32),
        pltpu.VMEM((2, 2, 2, depth, width), f32),
        pltpu.VMEM((2, 2, RING, depth, width), f32),
        pltpu.VMEM((2, RING, depth, width), f32),
        pltpu.VMEM((2, 2, depth // 2, width), f32),
        pltpu.VMEM((2, 2, depth // 2, width), f32),
        pltpu.VMEM((2, 2, depth, width), f32),
    ]


SQUARE_STEPS = 3


def sum_square(wires, part, out, by_col, by_row, mine):
    rows, cols = lax.axis_size("rows"), lax.axis_size("cols")
    row, col = lax.axis_index("rows"), lax.axis_index("cols")
    share = part.shape[0] // cols
    at = wires.used
    wires.used += SQUARE_STEPS

    def span(at):
        return pl.ds(at * share, share)

    def arrived(ref, step):
        pltpu.make_async_copy(ref, ref, wires.recv.at[at + step]).wait()

    for o in range(1, cols):
        peer = lax.rem(col + o, cols)
        wires.start(part.at[span(peer)], by_col.at[col], (row, peer), at)
    by_col[col] = part[span(col)]
    arrived(by_col.at[pl.ds(0, cols - 1)], 0)
    mine[...] = jnp.sum(by_col[...], axis=0)
    for o in range(1, rows):
        wires.start(mine, by_row.at[row], (lax.rem(row + o, rows), col), at + 1)
    by_row[row] = mine[...]
    arrived(by_row.at[pl.ds(0, rows - 1)], 1)
    out[span(col)] = jnp.sum(by_row[...], axis=0)
    for o in range(1, cols):
        wires.start(
            out.at[span(col)], out.at[span(col)], (row, lax.rem(col + o, cols)), at + 2
        )
    arrived(out.at[pl.ds(0, (cols - 1) * share)], 2)
    wires.drain(
        by_col.at[pl.ds(0, cols - 1)],
        by_row.at[pl.ds(0, rows - 1)],
        out.at[pl.ds(0, (cols - 1) * share)],
    )


def square_rooms(order, rows, cols):
    share = order // cols
    return [
        pltpu.VMEM((cols, share, order), jnp.float32),
        pltpu.VMEM((rows, share, order), jnp.float32),
        pltpu.VMEM((share, order), jnp.float32),
    ]


def all_peers():
    rows, cols = lax.axis_size("rows"), lax.axis_size("cols")
    row, col = lax.axis_index("rows"), lax.axis_index("cols")
    return [(lax.rem(row + o, rows), col) for o in range(1, rows)] + [
        (row, lax.rem(col + o, cols)) for o in range(1, cols)
    ]


GROUP = 8


def local_column(column):
    row = lax.axis_index("rows")
    panel, half = column // 16, lax.rem(column, 2)
    along_z = lax.rem(panel // RING + RING - row // RING, RING)
    along_y = lax.rem(lax.rem(panel, RING) + RING - lax.rem(row, RING), RING)
    first = jnp.where(half == 0, along_y, along_z)
    second = jnp.where(half == 0, along_z, along_y)
    return (half * RING + first) * RING + second


def products_kernel(transposed, count_ref, row_ref, col_ref, panels, tiles, out):
    count = count_ref[0, 0]
    out[...] = jnp.zeros_like(out)

    def step(group, carry):
        slots = [group * GROUP + u for u in range(GROUP)]
        rows = [row_ref[0, 0, slot] for slot in slots]
        cols = [local_column(col_ref[0, 0, slot]) for slot in slots]
        if transposed:
            terms = [
                jnp.dot(panels[r], tiles[slot], preferred_element_type=jnp.float32)
                for r, slot in zip(rows, slots)
            ]
        else:
            terms = [
                jnp.dot(tiles[slot], panels[c], preferred_element_type=jnp.float32)
                for c, slot in zip(cols, slots)
            ]
        for slot, term, place in zip(slots, terms, cols if transposed else rows):
            out[place] += jnp.where(slot < count, term, 0.0)
        return carry

    lax.fori_loop(0, (count + GROUP - 1) // GROUP, step, 0)


def products(transposed, out_shape, count, rows, cols, panels, tiles):
    return pl.pallas_call(
        functools.partial(products_kernel, transposed),
        out_shape=jax.ShapeDtypeStruct(out_shape, jnp.float32),
        in_specs=[SMEM, SMEM, SMEM, VMEM, VMEM],
        out_specs=VMEM,
        compiler_params=pltpu.CompilerParams(vmem_limit_bytes=32 << 20),
    )(count, rows, cols, panels, tiles)


def factor(gram, upper_ref, inverse_ref):
    order = gram.shape[0]
    lead = gram
    tail = (
        lax.broadcasted_iota(jnp.int32, (order, order), 0)
        == lax.broadcasted_iota(jnp.int32, (order, order), 1)
    ).astype(jnp.float32)
    for base in range(0, order, SUB):
        left = order - base
        columns = [
            jnp.broadcast_to(lead[:, base + k : base + k + 1], (left, order)) for k in range(SUB)
        ]
        position = lax.broadcasted_iota(jnp.int32, (left, order), 0)
        top = lax.broadcasted_iota(jnp.int32, (SUB, order), 0)
        lane = lax.broadcasted_iota(jnp.int32, (SUB, order), 1)
        pivots = jnp.zeros((SUB, order), jnp.float32)
        for k in range(SUB):
            pivot = columns[k][k : k + 1, :]
            pivots = jnp.where(top == k, pivot, pivots)
            ratio = jnp.where(position > k, columns[k] * (1.0 / pivot), 0.0)
            lead = lead - ratio * lead[k : k + 1, :]
            tail = tail - ratio * tail[k : k + 1, :]
            for j in range(k + 1, SUB):
                columns[j] = columns[j] - ratio * columns[j][k : k + 1, :]
        scale = 1.0 / jnp.sqrt(pivots)
        upper_ref[base : base + SUB, :] = jnp.where(lane >= base + top, lead[:SUB] * scale, 0.0)
        inverse_ref[base : base + SUB, :] = tail[:SUB] * scale
        lead = lead[SUB:]
        tail = tail[SUB:]


def inner(x_ref, out):
    out[...] = matmul(x_ref[0], x_ref[0], NT) + matmul(x_ref[1], x_ref[1], NT)


def basis_kernel(
    root, part, basis_ref, triangle_ref, spread_ref, x_ref, square, gram, inverse, *rest
):
    rooms, (by_col, by_row, mine, send, recv, send2) = rest[:7], rest[7:]
    plane = Plane()
    wires = Wires(send, recv)
    greet(all_peers())
    scatter_sum(plane, wires, part, x_ref, *rooms)
    inner(x_ref, square)
    wires.send = send2
    sum_square(wires, square, gram, by_col, by_row, mine)
    factor(gram[...], triangle_ref, inverse)
    width = x_ref.shape[2]
    for s in range(2):
        basis_ref[s * width : (s + 1) * width, :] = matmul(inverse[...], x_ref[s], NN).T * root
    triangle_ref[...] = triangle_ref[...] / root
    order = gram.shape[0]
    diagonal = lax.broadcasted_iota(jnp.int32, (order, order), 0) == lax.broadcasted_iota(
        jnp.int32, (order, order), 1
    )
    lengths = jnp.sum(jnp.where(diagonal, gram[...], 0.0), axis=0, keepdims=True)
    inverses = jnp.sum(inverse[...] * inverse[...], axis=0, keepdims=True)
    spread = jnp.sum(lengths * inverses, axis=1, keepdims=True)
    spread_ref[...] = jnp.broadcast_to(spread, spread_ref.shape)
    wires.send = send
    wires.drain(part.at[pl.ds(0, 30)])


def orthonormalize(root, part):
    _, depth, width = part.shape
    rows, cols = lax.axis_size("rows"), lax.axis_size("cols")
    f32 = jnp.float32
    square = pltpu.VMEM((depth, depth), f32)
    return pl.pallas_call(
        functools.partial(basis_kernel, root),
        out_shape=[
            jax.ShapeDtypeStruct((2 * width, depth), f32),
            jax.ShapeDtypeStruct((depth, depth), f32),
            jax.ShapeDtypeStruct((SUB, depth), f32),
        ],
        in_specs=[VMEM],
        out_specs=[VMEM] * 3,
        scratch_shapes=[pltpu.VMEM((2, depth, width), f32)]
        + [square] * 3
        + scatter_rooms(depth, width)
        + square_rooms(depth, rows, cols)
        + [
            pltpu.SemaphoreType.DMA,
            pltpu.SemaphoreType.DMA((SCATTER_COPIES + SQUARE_STEPS,)),
            pltpu.SemaphoreType.DMA,
        ],
        compiler_params=pltpu.CompilerParams(
            collective_id=2, has_side_effects=True, vmem_limit_bytes=40 << 20
        ),
    )(part)


def again_kernel(
    root, basis_in, triangle_in, basis_ref, triangle_ref, x, square, gram, upper, inverse, *rest
):
    by_col, by_row, mine, send, recv = rest
    wires = Wires(send, recv)
    greet(all_peers())
    x[...] = basis_in[...].T / root
    square[...] = matmul(x[...], x[...], NT)
    sum_square(wires, square, gram, by_col, by_row, mine)
    factor(gram[...], upper, inverse)
    basis_ref[...] = matmul(inverse[...], x[...], NN).T * root
    triangle_ref[...] = matmul(upper[...], triangle_in[...], NN)


def second_pass(root, basis, triangle):
    size, depth = basis.shape
    f32 = jnp.float32
    return pl.pallas_call(
        functools.partial(again_kernel, root),
        out_shape=[
            jax.ShapeDtypeStruct(basis.shape, f32),
            jax.ShapeDtypeStruct(triangle.shape, f32),
        ],
        in_specs=[VMEM] * 2,
        out_specs=[VMEM] * 2,
        scratch_shapes=[pltpu.VMEM((depth, size), f32)]
        + [pltpu.VMEM((depth, depth), f32)] * 4
        + square_rooms(depth, lax.axis_size("rows"), lax.axis_size("cols"))
        + [pltpu.SemaphoreType.DMA, pltpu.SemaphoreType.DMA((SQUARE_STEPS,))],
        compiler_params=pltpu.CompilerParams(
            collective_id=3, has_side_effects=True, vmem_limit_bytes=32 << 20
        ),
    )(basis, triangle)


def body(start_basis, block_values, slot_count, slot_row, slot_col):
    depth = start_basis.shape[1]
    width = block_values.shape[-1]
    panel_blocks = start_basis.shape[0] // width
    rows, cols = lax.axis_size("rows"), lax.axis_size("cols")
    column_blocks = rows * panel_blocks // cols
    basis_parts, tiles = gather(
        start_basis.reshape(panel_blocks, width, depth),
        block_values.reshape(block_values.shape[2:]),
        rows,
    )
    image_part = products(
        False,
        (panel_blocks, width, depth),
        slot_count,
        slot_row,
        slot_col,
        basis_parts.reshape(column_blocks, width, depth),
        tiles,
    )
    image = sum_image(image_part)
    back_part = products(
        True, (column_blocks, depth, width), slot_count, slot_row, slot_col, image, tiles
    )
    root = float(rows * panel_blocks * width) ** 0.5
    basis, triangle, spread = orthonormalize(root, back_part)
    return lax.cond(
        spread[0, 0] <= 2.0 * depth,
        lambda basis, triangle: (basis, triangle),
        functools.partial(second_pass, root),
        basis,
        triangle,
    )


def solution(mesh):
    return jax.shard_map(
        body,
        mesh=mesh,
        in_specs=(
            P("rows", None),
            P("rows", "cols", None, None, None),
            P("rows", "cols"),
            P("rows", "cols", None),
            P("rows", "cols", None),
        ),
        out_specs=(P(("rows", "cols"), None), P()),
        check_vma=False,
    )
```

```python
import functools

import jax
import jax.numpy as jnp
from jax import lax
from jax.experimental import pallas as pl
from jax.experimental.pallas import tpu as pltpu
from jax.sharding import PartitionSpec as P

SUB = 8
RING = 4
TOP = 32000.0
LEAST = 1e-33
VMEM = pl.BlockSpec(memory_space=pltpu.VMEM)
SMEM = pl.BlockSpec(memory_space=pltpu.SMEM)
HBM = pl.BlockSpec(memory_space=pltpu.HBM)
NN = (((1,), (0,)), ((), ()))
NT = (((1,), (1,)), ((), ()))


def matmul(a, b, dims):
    return lax.dot_general(
        a, b, dims, precision=lax.Precision.HIGHEST, preferred_element_type=jnp.float32
    )


class Wires:
    def __init__(self, send, recv):
        self.send, self.recv, self.used = send, recv, 0

    def start(self, src, dst, device, at=None):
        if at is None:
            at = self.used
            self.used += 1
        copy = pltpu.make_async_remote_copy(
            src_ref=src,
            dst_ref=dst,
            send_sem=self.send,
            recv_sem=self.recv.at[at],
            device_id=device,
            device_id_type=pl.DeviceIdType.MESH,
        )
        copy.start()
        return copy

    def drain(self, *refs):
        for ref in refs:
            pltpu.make_async_copy(ref, ref, self.send).wait()


def announce(peers):
    barrier = pltpu.get_barrier_semaphore()
    for peer in peers:
        pl.semaphore_signal(
            barrier, inc=1, device_id=peer, device_id_type=pl.DeviceIdType.MESH
        )


def greet(peers):
    announce(peers)
    pl.semaphore_wait(pltpu.get_barrier_semaphore(), len(peers))


def arrived(ref, sem):
    pltpu.make_async_copy(ref, ref, sem).wait()


def encode(value, inverse):
    return jnp.round(value * inverse).astype(jnp.int32).astype(jnp.int16)


def decode(code, unit):
    return code.astype(jnp.int32).astype(jnp.float32) * unit


def shifted(at, offset):
    return lax.rem(at + offset % RING, RING)


class Plane:
    def __init__(self):
        row = lax.axis_index("rows")
        self.col = lax.axis_index("cols")
        self.z, self.y = row // RING, lax.rem(row, RING)

    def row(self, half, first, second):
        along_y, along_z = (first, second) if half == 0 else (second, first)
        return shifted(self.z, along_z) * RING + shifted(self.y, along_y)

    def device(self, half, first, second):
        return (self.row(half, first, second), self.col)

    def neighbours(self):
        return [self.device(0, 1, 0), self.device(0, 3, 0), self.device(0, 0, 1), self.device(0, 0, 3)]


GATHER_COPIES = 24


def gather_kernel(basis, values, out, tiles, send, recv, local):
    plane = Plane()
    wires = Wires(send, recv)
    load = pltpu.make_async_copy(basis.at[pl.ds(plane.col * 2, 2)], out.at[:, 0, 0], local.at[0])
    load.start()
    keep = pltpu.make_async_copy(values, tiles, local.at[1])
    keep.start()
    greet(plane.neighbours())
    load.wait()
    cut = out.shape[3] // 2
    upper, lower = pl.ds(0, cut), pl.ds(cut, cut)
    near, own, rest, relay, far, ends = {}, {}, {}, {}, {}, {}
    for h in (0, 1):
        src = out.at[h, 0, 0]
        near[h] = [
            wires.start(src, out.at[h, 3, 0], plane.device(h, 1, 0)),
            wires.start(src, out.at[h, 1, 0], plane.device(h, 3, 0)),
        ]
    for h in (0, 1):
        src = out.at[h, 0, 0]
        own[h] = [
            wires.start(src, out.at[h, 0, 3], plane.device(h, 0, 1)),
            wires.start(src, out.at[h, 0, 1], plane.device(h, 0, 3)),
        ]
    for h in (0, 1):
        near[h][0].wait_recv()
        up = wires.start(out.at[h, 3, 0, upper], out.at[h, 2, 0, upper], plane.device(h, 1, 0))
        near[h][1].wait_recv()
        down = wires.start(out.at[h, 1, 0, lower], out.at[h, 2, 0, lower], plane.device(h, 3, 0))
        relay[h] = [up, down]
    for h in (0, 1):
        own[h][0].wait_recv()
        up = wires.start(out.at[h, 0, 3, upper], out.at[h, 0, 2, upper], plane.device(h, 0, 1))
        own[h][1].wait_recv()
        down = wires.start(out.at[h, 0, 1, lower], out.at[h, 0, 2, lower], plane.device(h, 0, 3))
        far[h] = [up, down]
    three = pl.ds(1, 3)
    for h in (0, 1):
        relay[h][0].wait_recv()
        relay[h][1].wait_recv()
        src = out.at[h, three, 0]
        rest[h] = [
            wires.start(src, out.at[h, three, 3], plane.device(h, 0, 1)),
            wires.start(src, out.at[h, three, 1], plane.device(h, 0, 3)),
        ]
    for h in (0, 1):
        rest[h][0].wait_recv()
        up = wires.start(
            out.at[h, three, 3, upper], out.at[h, three, 2, upper], plane.device(h, 0, 1)
        )
        rest[h][1].wait_recv()
        down = wires.start(
            out.at[h, three, 1, lower], out.at[h, three, 2, lower], plane.device(h, 0, 3)
        )
        ends[h] = [up, down]
    for h in (0, 1):
        for copy in far[h] + ends[h]:
            copy.wait_recv()
    keep.wait()
    wires.drain(out.at[0], out.at[1, pl.ds(0, 3)], out.at[1, 3, pl.ds(0, 2)])


def gather(basis, values, rows):
    return pl.pallas_call(
        gather_kernel,
        out_shape=[
            jax.ShapeDtypeStruct((2, rows // RING, RING) + basis.shape[1:], basis.dtype),
            jax.ShapeDtypeStruct(values.shape, values.dtype),
        ],
        in_specs=[HBM, HBM],
        out_specs=[VMEM, VMEM],
        scratch_shapes=[
            pltpu.SemaphoreType.DMA,
            pltpu.SemaphoreType.DMA((GATHER_COPIES,)),
            pltpu.SemaphoreType.DMA((2,)),
        ],
        compiler_params=pltpu.CompilerParams(
            collective_id=0, has_side_effects=True, vmem_limit_bytes=44 << 20
        ),
    )(basis, values)


IMAGE_COPIES = 24


def image_kernel(
    part, image, sibling, total, code, unit, got, units, send, recv, send2, send3
):
    row, col = lax.axis_index("rows"), lax.axis_index("cols")
    x, core = col // 2, lax.rem(col, 2)
    twin = (row, x * 2 + 1 - core)
    peer = {o: (row, shifted(x, o) * 2 + core) for o in (1, 2, 3)}
    wires = Wires(send, recv)
    greet([twin, peer[1], peer[2], peer[3]])
    sub = image.shape[0] // 8

    def chunk(offset, which):
        return pl.ds((shifted(x, offset) * 2 + which) * sub, sub)

    order = (2, 1, 3, 0)
    swap = {
        o: wires.start(part.at[chunk(o, 1 - core)], sibling.at[o], twin) for o in order
    }
    wires.send = send2
    coded, scaled = {}, {}
    for o in order:
        swap[o].wait_recv()
        whole = part[chunk(o, core)] + sibling[o]
        if o == 0:
            total[...] = whole
            continue
        most = jnp.max(jnp.max(jnp.abs(whole), axis=0), axis=0, keepdims=True)
        step = jnp.maximum(most, LEAST) * (1.0 / TOP)
        unit[o - 1] = jnp.broadcast_to(step, unit.shape[1:])
        code[o - 1] = encode(whole, (1.0 / step)[None])
        coded[o] = wires.start(code.at[o - 1], got.at[o - 1], peer[o])
        scaled[o] = wires.start(unit.at[o - 1], units.at[o - 1], peer[o])
    for o in (1, 3, 2):
        coded[o].wait_recv()
        scaled[o].wait_recv()
    wires.send = send3
    mine = (x * 2 + core) * sub
    sends = []
    for b in range(2):
        value = total[b]
        for o in (1, 2, 3):
            value = value + decode(got[o - 1, b], units[o - 1, 0:1])
        image[mine + b] = value.T.astype(image.dtype)
        block = image.at[mine + b]
        sends.append({o: wires.start(block, block, peer[o]) for o in (2, 1, 3)})
    both = image.at[pl.ds(mine, sub)]
    last = [wires.start(both, both, twin)]
    for o in (1, 3, 2):
        for b in (0, 1):
            sends[b][o].wait_recv()
        pair = image.at[pl.ds((shifted(x, RING - o) * 2 + core) * sub, sub)]
        last.append(wires.start(pair, pair, twin))
    for copy in last:
        copy.wait_recv()
    wires.drain(image.at[pl.ds(0, 14)])
    wires.send = send2
    wires.drain(got, units)
    wires.send = send
    wires.drain(part.at[pl.ds(0, 8)])


def sum_image(part):
    blocks, width, depth = part.shape
    f32 = jnp.float32
    return pl.pallas_call(
        image_kernel,
        out_shape=jax.ShapeDtypeStruct((blocks, depth, width), jnp.bfloat16),
        in_specs=[VMEM],
        out_specs=VMEM,
        scratch_shapes=[
            pltpu.VMEM((RING, 2, width, depth), f32),
            pltpu.VMEM((2, width, depth), f32),
            pltpu.VMEM((RING - 1, 2, width, depth), jnp.int16),
            pltpu.VMEM((RING - 1, SUB, depth), f32),
            pltpu.VMEM((RING - 1, 2, width, depth), jnp.int16),
            pltpu.VMEM((RING - 1, SUB, depth), f32),
            pltpu.SemaphoreType.DMA,
            pltpu.SemaphoreType.DMA((IMAGE_COPIES,)),
            pltpu.SemaphoreType.DMA,
            pltpu.SemaphoreType.DMA,
        ],
        compiler_params=pltpu.CompilerParams(
            collective_id=1, has_side_effects=True, vmem_limit_bytes=32 << 20
        ),
    )(part)


SCATTER_STEPS = 14


def tile_of(row):
    return jnp.broadcast_to(row, (row.shape[1], row.shape[1])).T


def scatter_sum(plane, wires, peers, part, out, code, got, line, lines, code2, got2, line2, lines2, own):
    others = (2, 1, 3)
    order = (2, 3, 1, 0)

    def block(h, first, second):
        return (h * RING + first) * RING + second

    def column(tile):
        return jnp.concatenate([tile, tile], axis=1)

    announce(peers)
    most = lax.fori_loop(
        0,
        part.shape[0],
        lambda at, most: jnp.maximum(most, jnp.abs(part[at])),
        jnp.zeros(part.shape[1:], jnp.float32),
    )
    most = jnp.broadcast_to(jnp.max(most, axis=1, keepdims=True), line.shape[1:] * 2)
    unit = jnp.maximum(most, LEAST) * (1.0 / TOP)
    line[...] = unit.T[:SUB]
    inverse = column(1.0 / unit)
    pl.semaphore_wait(pltpu.get_barrier_semaphore(), len(peers))
    for h in (0, 1):
        for o in others:
            wires.start(line, lines.at[h, o - 1], plane.device(h, o, 0), h)
    for at, s in enumerate(order):
        for o in others:
            for h in (0, 1):
                code[h, s, o - 1] = encode(part[block(h, o, s)], inverse)
                wires.start(
                    code.at[h, s, o - 1], got.at[h, s, o - 1], plane.device(h, o, 0), 2 + 2 * at + h
                )
    units, sums = {}, {}
    for h in (0, 1):
        arrived(lines.at[h], wires.recv.at[h])
        units[h] = [tile_of(lines[h, k, 0:1]) for k in range(RING - 1)]
        sums[h] = unit + (units[h][0] + units[h][1] + units[h][2])
        line2[h] = line[...] + (lines[h, 0] + lines[h, 1] + lines[h, 2])
        for s in others:
            wires.start(line2.at[h], lines2.at[h, s - 1], plane.device(h, 0, s), 10 + h)
    for at, s in enumerate(order):
        for h in (0, 1):
            arrived(got.at[h, s], wires.recv.at[2 + 2 * at + h])
            total = part[block(h, 0, s)]
            for k in range(RING - 1):
                total = total + decode(got[h, s, k], column(units[h][k]))
            if s == 0:
                own[h] = total
            else:
                code2[h, s - 1] = encode(total, column(1.0 / sums[h]))
                wires.start(
                    code2.at[h, s - 1], got2.at[h, s - 1], plane.device(h, 0, s), 12 + h
                )
    for h in (0, 1):
        arrived(lines2.at[h], wires.recv.at[10 + h])
        arrived(got2.at[h], wires.recv.at[12 + h])
        total = own[h]
        for k in range(RING - 1):
            total = total + decode(got2[h, k], column(tile_of(lines2[h, k, 0:1])))
        out[h] = total


def scatter_rooms(depth, width):
    f32 = jnp.float32
    i16 = jnp.int16
    others = RING - 1
    return [
        pltpu.VMEM((2, RING, others, depth, width), i16),
        pltpu.VMEM((2, RING, others, depth, width), i16),
        pltpu.VMEM((SUB, depth), f32),
        pltpu.VMEM((2, others, SUB, depth), f32),
        pltpu.VMEM((2, others, depth, width), i16),
        pltpu.VMEM((2, others, depth, width), i16),
        pltpu.VMEM((2, SUB, depth), f32),
        pltpu.VMEM((2, others, SUB, depth), f32),
        pltpu.VMEM((2, depth, width), f32),
    ]


SQUARE_STEPS = 3


def sum_square(wires, at, part, out, by_col, by_row, mine):
    rows, cols = lax.axis_size("rows"), lax.axis_size("cols")
    row, col = lax.axis_index("rows"), lax.axis_index("cols")
    share = part.shape[0] // cols
    x, core = col // 2, lax.rem(col, 2)
    z, y = row // RING, lax.rem(row, RING)

    def span(at):
        return pl.ds(at * share, share)

    far = {0: 0, 1: 1, 2: 2, 3: 1}
    col_peers = [
        shifted(x, o) * 2 + lax.rem(core + c, 2)
        for o, c in ((2, 0), (2, 1), (1, 0), (3, 0), (1, 1), (3, 1), (0, 1))
    ]
    steps = [(a, b) for a in range(RING) for b in range(RING) if a or b]
    row_peers = [
        shifted(z, a) * RING + shifted(y, b)
        for a, b in sorted(steps, key=lambda step: -far[step[0]] - far[step[1]])
    ]
    for peer in col_peers:
        wires.start(part.at[span(peer)], by_col.at[col], (row, peer), at)
    by_col[col] = part[span(col)]
    arrived(by_col.at[pl.ds(0, cols - 1)], wires.recv.at[at])
    mine[...] = jnp.sum(by_col[...], axis=0)
    for peer in row_peers:
        wires.start(mine, by_row.at[row], (peer, col), at + 1)
    by_row[row] = mine[...]
    arrived(by_row.at[pl.ds(0, rows - 1)], wires.recv.at[at + 1])
    out[span(col)] = jnp.sum(by_row[...], axis=0)
    for peer in col_peers:
        wires.start(out.at[span(col)], out.at[span(col)], (row, peer), at + 2)
    arrived(out.at[pl.ds(0, (cols - 1) * share)], wires.recv.at[at + 2])
    wires.drain(
        by_col.at[pl.ds(0, cols - 1)],
        by_row.at[pl.ds(0, rows - 1)],
        out.at[pl.ds(0, (cols - 1) * share)],
    )


def square_rooms(order, rows, cols):
    share = order // cols
    return [
        pltpu.VMEM((cols, share, order), jnp.float32),
        pltpu.VMEM((rows, share, order), jnp.float32),
        pltpu.VMEM((share, order), jnp.float32),
    ]


def all_peers():
    rows, cols = lax.axis_size("rows"), lax.axis_size("cols")
    row, col = lax.axis_index("rows"), lax.axis_index("cols")
    return [(lax.rem(row + o, rows), col) for o in range(1, rows)] + [
        (row, lax.rem(col + o, cols)) for o in range(1, cols)
    ]


GROUP = 8


def local_column(column):
    row = lax.axis_index("rows")
    panel, half = column // 16, lax.rem(column, 2)
    along_z = lax.rem(panel // RING + RING - row // RING, RING)
    along_y = lax.rem(lax.rem(panel, RING) + RING - lax.rem(row, RING), RING)
    first = jnp.where(half == 0, along_y, along_z)
    second = jnp.where(half == 0, along_z, along_y)
    return (half * RING + first) * RING + second


def products_kernel(transposed, count_ref, row_ref, col_ref, panels, tiles, out):
    count = count_ref[0, 0]
    out[...] = jnp.zeros_like(out)

    def step(group, carry):
        slots = [group * GROUP + u for u in range(GROUP)]
        rows = [row_ref[0, 0, slot] for slot in slots]
        cols = [local_column(col_ref[0, 0, slot]) for slot in slots]
        if transposed:
            terms = [
                jnp.dot(panels[r], tiles[slot], preferred_element_type=jnp.float32)
                for r, slot in zip(rows, slots)
            ]
        else:
            terms = [
                jnp.dot(tiles[slot], panels[c], preferred_element_type=jnp.float32)
                for c, slot in zip(cols, slots)
            ]
        for slot, term, place in zip(slots, terms, cols if transposed else rows):
            out[place] += jnp.where(slot < count, term, 0.0)
        return carry

    lax.fori_loop(0, (count + GROUP - 1) // GROUP, step, 0)


def products(transposed, out_shape, count, rows, cols, panels, tiles):
    return pl.pallas_call(
        functools.partial(products_kernel, transposed),
        out_shape=jax.ShapeDtypeStruct(out_shape, jnp.float32),
        in_specs=[SMEM, SMEM, SMEM, VMEM, VMEM],
        out_specs=VMEM,
        compiler_params=pltpu.CompilerParams(vmem_limit_bytes=32 << 20),
    )(count, rows, cols, panels, tiles)


def factor(gram, upper_ref, inverse_ref):
    order = gram.shape[0]
    lead = gram
    tail = (
        lax.broadcasted_iota(jnp.int32, (order, order), 0)
        == lax.broadcasted_iota(jnp.int32, (order, order), 1)
    ).astype(jnp.float32)
    for base in range(0, order, SUB):
        left = order - base
        columns = [
            jnp.broadcast_to(lead[:, base + k : base + k + 1], (left, order)) for k in range(SUB)
        ]
        position = lax.broadcasted_iota(jnp.int32, (left, order), 0)
        top = lax.broadcasted_iota(jnp.int32, (SUB, order), 0)
        lane = lax.broadcasted_iota(jnp.int32, (SUB, order), 1)
        pivots = jnp.zeros((SUB, order), jnp.float32)
        for k in range(SUB):
            pivot = columns[k][k : k + 1, :]
            pivots = jnp.where(top == k, pivot, pivots)
            ratio = jnp.where(position > k, columns[k] * (1.0 / pivot), 0.0)
            lead = lead - ratio * lead[k : k + 1, :]
            tail = tail - ratio * tail[k : k + 1, :]
            for j in range(k + 1, SUB):
                columns[j] = columns[j] - ratio * columns[j][k : k + 1, :]
        scale = 1.0 / jnp.sqrt(pivots)
        upper_ref[base : base + SUB, :] = jnp.where(lane >= base + top, lead[:SUB] * scale, 0.0)
        inverse_ref[base : base + SUB, :] = tail[:SUB] * scale
        lead = lead[SUB:]
        tail = tail[SUB:]


def inner(x_ref, out):
    out[...] = matmul(x_ref[0], x_ref[0], NT) + matmul(x_ref[1], x_ref[1], NT)


def basis_kernel(
    root, part, basis_ref, triangle_ref, spread_ref, x_ref, square, gram, inverse, *rest
):
    rooms, (by_col, by_row, mine, send, recv, send2) = rest[:9], rest[9:]
    plane = Plane()
    wires = Wires(send, recv)
    scatter_sum(plane, wires, all_peers(), part, x_ref, *rooms)
    inner(x_ref, square)
    wires.send = send2
    sum_square(wires, SCATTER_STEPS, square, gram, by_col, by_row, mine)
    factor(gram[...], triangle_ref, inverse)
    width = x_ref.shape[2]
    for s in range(2):
        basis_ref[s * width : (s + 1) * width, :] = matmul(inverse[...], x_ref[s], NN).T * root
    triangle_ref[...] = triangle_ref[...] / root
    order = gram.shape[0]
    diagonal = lax.broadcasted_iota(jnp.int32, (order, order), 0) == lax.broadcasted_iota(
        jnp.int32, (order, order), 1
    )
    lengths = jnp.sum(jnp.where(diagonal, gram[...], 0.0), axis=0, keepdims=True)
    inverses = jnp.sum(inverse[...] * inverse[...], axis=0, keepdims=True)
    spread = jnp.sum(lengths * inverses, axis=1, keepdims=True)
    spread_ref[0, 0] = spread[0, 0]
    wires.send = send
    code, got, line, lines, code2, got2, line2, lines2, own = rooms
    wires.drain(got, got2, lines, lines2)


def orthonormalize(root, part):
    _, depth, width = part.shape
    rows, cols = lax.axis_size("rows"), lax.axis_size("cols")
    f32 = jnp.float32
    square = pltpu.VMEM((depth, depth), f32)
    return pl.pallas_call(
        functools.partial(basis_kernel, root),
        out_shape=[
            jax.ShapeDtypeStruct((2 * width, depth), f32),
            jax.ShapeDtypeStruct((depth, depth), f32),
            jax.ShapeDtypeStruct((1, 1), f32),
        ],
        in_specs=[VMEM],
        out_specs=[VMEM, VMEM, SMEM],
        scratch_shapes=[pltpu.VMEM((2, depth, width), f32)]
        + [square] * 3
        + scatter_rooms(depth, width)
        + square_rooms(depth, rows, cols)
        + [
            pltpu.SemaphoreType.DMA,
            pltpu.SemaphoreType.DMA((SCATTER_STEPS + SQUARE_STEPS,)),
            pltpu.SemaphoreType.DMA,
        ],
        compiler_params=pltpu.CompilerParams(
            collective_id=2, has_side_effects=True, vmem_limit_bytes=40 << 20
        ),
    )(part)


def again_kernel(
    root, basis_in, triangle_in, basis_ref, triangle_ref, x, square, gram, upper, inverse, *rest
):
    by_col, by_row, mine, send, recv = rest
    wires = Wires(send, recv)
    greet(all_peers())
    x[...] = basis_in[...].T / root
    square[...] = matmul(x[...], x[...], NT)
    sum_square(wires, 0, square, gram, by_col, by_row, mine)
    factor(gram[...], upper, inverse)
    basis_ref[...] = matmul(inverse[...], x[...], NN).T * root
    triangle_ref[...] = matmul(upper[...], triangle_in[...], NN)


def second_pass(root, basis, triangle):
    size, depth = basis.shape
    f32 = jnp.float32
    return pl.pallas_call(
        functools.partial(again_kernel, root),
        out_shape=[
            jax.ShapeDtypeStruct(basis.shape, f32),
            jax.ShapeDtypeStruct(triangle.shape, f32),
        ],
        in_specs=[VMEM] * 2,
        out_specs=[VMEM] * 2,
        scratch_shapes=[pltpu.VMEM((depth, size), f32)]
        + [pltpu.VMEM((depth, depth), f32)] * 4
        + square_rooms(depth, lax.axis_size("rows"), lax.axis_size("cols"))
        + [pltpu.SemaphoreType.DMA, pltpu.SemaphoreType.DMA((SQUARE_STEPS,))],
        compiler_params=pltpu.CompilerParams(
            collective_id=3, has_side_effects=True, vmem_limit_bytes=32 << 20
        ),
    )(basis, triangle)


def body(start_basis, block_values, slot_count, slot_row, slot_col):
    depth = start_basis.shape[1]
    width = block_values.shape[-1]
    panel_blocks = start_basis.shape[0] // width
    rows, cols = lax.axis_size("rows"), lax.axis_size("cols")
    column_blocks = rows * panel_blocks // cols
    basis_parts, tiles = gather(
        start_basis.reshape(panel_blocks, width, depth),
        block_values.reshape(block_values.shape[2:]),
        rows,
    )
    image_part = products(
        False,
        (panel_blocks, width, depth),
        slot_count,
        slot_row,
        slot_col,
        basis_parts.reshape(column_blocks, width, depth),
        tiles,
    )
    image = sum_image(image_part)
    back_part = products(
        True, (column_blocks, depth, width), slot_count, slot_row, slot_col, image, tiles
    )
    root = float(rows * panel_blocks * width) ** 0.5
    basis, triangle, spread = orthonormalize(root, back_part)
    return lax.cond(
        spread[0, 0] <= 2.0 * depth,
        lambda basis, triangle: (basis, triangle),
        functools.partial(second_pass, root),
        basis,
        triangle,
    )


def solution(mesh):
    return jax.shard_map(
        body,
        mesh=mesh,
        in_specs=(
            P("rows", None),
            P("rows", "cols", None, None, None),
            P("rows", "cols"),
            P("rows", "cols", None),
            P("rows", "cols", None),
        ),
        out_specs=(P(("rows", "cols"), None), P()),
        check_vma=False,
    )
```

```python
import functools

import jax
import jax.numpy as jnp
from jax import lax
from jax.experimental import pallas as pl
from jax.experimental.pallas import tpu as pltpu
from jax.sharding import PartitionSpec as P

SUB = 8
RING = 4
TOP = 32000.0
LEAST = 1e-33
VMEM = pl.BlockSpec(memory_space=pltpu.VMEM)
SMEM = pl.BlockSpec(memory_space=pltpu.SMEM)
HBM = pl.BlockSpec(memory_space=pltpu.HBM)
NN = (((1,), (0,)), ((), ()))
NT = (((1,), (1,)), ((), ()))


def matmul(a, b, dims):
    return lax.dot_general(
        a, b, dims, precision=lax.Precision.HIGHEST, preferred_element_type=jnp.float32
    )


class Wires:
    def __init__(self, send, recv):
        self.send, self.recv, self.used = send, recv, 0

    def start(self, src, dst, device, at=None):
        if at is None:
            at = self.used
            self.used += 1
        copy = pltpu.make_async_remote_copy(
            src_ref=src,
            dst_ref=dst,
            send_sem=self.send,
            recv_sem=self.recv.at[at],
            device_id=device,
            device_id_type=pl.DeviceIdType.MESH,
        )
        copy.start()
        return copy

    def drain(self, *refs):
        for ref in refs:
            pltpu.make_async_copy(ref, ref, self.send).wait()


def announce(peers):
    barrier = pltpu.get_barrier_semaphore()
    for peer in peers:
        pl.semaphore_signal(
            barrier, inc=1, device_id=peer, device_id_type=pl.DeviceIdType.MESH
        )


def greet(peers):
    announce(peers)
    pl.semaphore_wait(pltpu.get_barrier_semaphore(), len(peers))


def arrived(ref, sem):
    pltpu.make_async_copy(ref, ref, sem).wait()


def encode(value, inverse):
    return jnp.round(value * inverse).astype(jnp.int32).astype(jnp.int16)


def decode(code, unit):
    return code.astype(jnp.int32).astype(jnp.float32) * unit


def shifted(at, offset):
    return lax.rem(at + offset % RING, RING)


class Plane:
    def __init__(self):
        row = lax.axis_index("rows")
        self.col = lax.axis_index("cols")
        self.z, self.y = row // RING, lax.rem(row, RING)

    def row(self, half, first, second):
        along_y, along_z = (first, second) if half == 0 else (second, first)
        return shifted(self.z, along_z) * RING + shifted(self.y, along_y)

    def device(self, half, first, second):
        return (self.row(half, first, second), self.col)

    def neighbours(self):
        return [self.device(0, o, 0) for o in (2, 1, 3)] + [self.device(0, 0, o) for o in (2, 1, 3)]


GATHER_COPIES = 36


def gather_kernel(
    basis, values, rows, cols, out, tiles, rows_out, cols_out, send, recv, local
):
    plane = Plane()
    wires = Wires(send, recv)
    load = pltpu.make_async_copy(basis.at[pl.ds(plane.col * 2, 2)], out.at[:, 0, 0], local.at[0])
    load.start()
    kept = [
        pltpu.make_async_copy(src, dst, local.at[1 + at])
        for at, (src, dst) in enumerate(
            ((values, tiles), (rows, rows_out), (cols, cols_out))
        )
    ]
    for copy in kept:
        copy.start()
    greet(plane.neighbours())
    load.wait()
    cut = out.shape[3] // 2
    upper, lower = pl.ds(0, cut), pl.ds(cut, cut)
    near, own, rest, ends = {}, {}, {}, []
    for o in (1, 3, 2):
        for h in (0, 1):
            near[h, o] = wires.start(
                out.at[h, 0, 0], out.at[h, RING - o, 0], plane.device(h, o, 0)
            )
    for o in (1, 3, 2):
        for h in (0, 1):
            own[h, o] = wires.start(
                out.at[h, 0, 0], out.at[h, 0, RING - o], plane.device(h, 0, o)
            )
    for f in (3, 1, 2):
        for h in (0, 1):
            near[h, RING - f].wait_recv()
            for o in (1, 3):
                rest[h, f, o] = wires.start(
                    out.at[h, f, 0], out.at[h, f, RING - o], plane.device(h, 0, o)
                )
    for f in (3, 1, 2):
        for o, piece in ((1, upper), (3, lower)):
            for h in (0, 1):
                rest[h, f, o].wait_recv()
                ends.append(
                    wires.start(
                        out.at[h, f, RING - o, piece], out.at[h, f, 2, piece], plane.device(h, 0, o)
                    )
                )
    for copy in list(own.values()) + ends:
        copy.wait_recv()
    for copy in kept:
        copy.wait()
    wires.drain(out.at[0], out.at[1, pl.ds(0, 3)], out.at[1, 3, pl.ds(0, 2)])


def gather(basis, values, indices, rows):
    return pl.pallas_call(
        gather_kernel,
        out_shape=[
            jax.ShapeDtypeStruct((2, rows // RING, RING) + basis.shape[1:], basis.dtype),
            jax.ShapeDtypeStruct(values.shape, values.dtype),
        ]
        + [jax.ShapeDtypeStruct(index.shape, index.dtype) for index in indices],
        in_specs=[HBM] * 4,
        out_specs=[VMEM] * 2 + [SMEM] * 2,
        scratch_shapes=[
            pltpu.SemaphoreType.DMA,
            pltpu.SemaphoreType.DMA((GATHER_COPIES,)),
            pltpu.SemaphoreType.DMA((4,)),
        ],
        compiler_params=pltpu.CompilerParams(
            collective_id=0, has_side_effects=True, vmem_limit_bytes=44 << 20
        ),
    )(basis, values, *indices)


IMAGE_COPIES = 24


def image_kernel(
    part, image, sibling, total, code, unit, got, units, send, recv, send2, send3
):
    row, col = lax.axis_index("rows"), lax.axis_index("cols")
    x, core = col // 2, lax.rem(col, 2)
    twin = (row, x * 2 + 1 - core)
    peer = {o: (row, shifted(x, o) * 2 + core) for o in (1, 2, 3)}
    wires = Wires(send, recv)
    greet([twin, peer[1], peer[2], peer[3]])
    sub = image.shape[0] // 8

    def chunk(offset, which):
        return pl.ds((shifted(x, offset) * 2 + which) * sub, sub)

    order = (2, 1, 3, 0)
    swap = {
        o: wires.start(part.at[chunk(o, 1 - core)], sibling.at[o], twin) for o in order
    }
    wires.send = send2
    coded, scaled = {}, {}
    for o in order:
        swap[o].wait_recv()
        whole = part[chunk(o, core)] + sibling[o]
        if o == 0:
            total[...] = whole
            continue
        most = jnp.max(jnp.max(jnp.abs(whole), axis=0), axis=0, keepdims=True)
        step = jnp.maximum(most, LEAST) * (1.0 / TOP)
        unit[o - 1] = jnp.broadcast_to(step, unit.shape[1:])
        code[o - 1] = encode(whole, (1.0 / step)[None])
        scaled[o] = wires.start(unit.at[o - 1], units.at[o - 1], peer[o])
        coded[o, 0] = wires.start(code.at[o - 1, 0], got.at[o - 1, 0], peer[o])
    for o in (2, 1, 3):
        coded[o, 1] = wires.start(code.at[o - 1, 1], got.at[o - 1, 1], peer[o])
    for o in (1, 3, 2):
        scaled[o].wait_recv()
    wires.send = send3
    mine = (x * 2 + core) * sub
    sends = []
    for b in range(2):
        value = total[b]
        for o in (1, 3, 2):
            coded[o, b].wait_recv()
            value = value + decode(got[o - 1, b], units[o - 1, 0:1])
        image[mine + b] = value.T.astype(image.dtype)
        block = image.at[mine + b]
        sends.append({o: wires.start(block, block, peer[o]) for o in (2, 1, 3)})
    both = image.at[pl.ds(mine, sub)]
    last = [wires.start(both, both, twin)]
    for o in (1, 3, 2):
        for b in (0, 1):
            sends[b][o].wait_recv()
        pair = image.at[pl.ds((shifted(x, RING - o) * 2 + core) * sub, sub)]
        last.append(wires.start(pair, pair, twin))
    for copy in last:
        copy.wait_recv()
    wires.drain(image.at[pl.ds(0, 14)])
    wires.send = send2
    wires.drain(got, units)
    wires.send = send
    wires.drain(part.at[pl.ds(0, 8)])


def sum_image(part):
    blocks, width, depth = part.shape
    f32 = jnp.float32
    return pl.pallas_call(
        image_kernel,
        out_shape=jax.ShapeDtypeStruct((blocks, depth, width), jnp.bfloat16),
        in_specs=[VMEM],
        out_specs=VMEM,
        scratch_shapes=[
            pltpu.VMEM((RING, 2, width, depth), f32),
            pltpu.VMEM((2, width, depth), f32),
            pltpu.VMEM((RING - 1, 2, width, depth), jnp.int16),
            pltpu.VMEM((RING - 1, SUB, depth), f32),
            pltpu.VMEM((RING - 1, 2, width, depth), jnp.int16),
            pltpu.VMEM((RING - 1, SUB, depth), f32),
            pltpu.SemaphoreType.DMA,
            pltpu.SemaphoreType.DMA((IMAGE_COPIES,)),
            pltpu.SemaphoreType.DMA,
            pltpu.SemaphoreType.DMA,
        ],
        compiler_params=pltpu.CompilerParams(
            collective_id=1, has_side_effects=True, vmem_limit_bytes=32 << 20
        ),
    )(part)


SCATTER_STEPS = 14


def tile_of(row):
    return jnp.broadcast_to(row, (row.shape[1], row.shape[1])).T


def scatter_sum(plane, wires, peers, part, out, code, got, line, lines, code2, got2, line2, lines2, own):
    others = (2, 1, 3)
    order = (2, 3, 1, 0)

    def block(h, first, second):
        return (h * RING + first) * RING + second

    def column(tile):
        return jnp.concatenate([tile, tile], axis=1)

    announce(peers)
    most = lax.fori_loop(
        0,
        part.shape[0],
        lambda at, most: jnp.maximum(most, jnp.abs(part[at])),
        jnp.zeros(part.shape[1:], jnp.float32),
    )
    most = jnp.broadcast_to(jnp.max(most, axis=1, keepdims=True), line.shape[1:] * 2)
    unit = jnp.maximum(most, LEAST) * (1.0 / TOP)
    line[...] = unit.T[:SUB]
    inverse = column(1.0 / unit)
    pl.semaphore_wait(pltpu.get_barrier_semaphore(), len(peers))
    for h in (0, 1):
        for o in others:
            wires.start(line, lines.at[h, o - 1], plane.device(h, o, 0), h)
    for at, s in enumerate(order):
        for o in others:
            for h in (0, 1):
                code[h, s, o - 1] = encode(part[block(h, o, s)], inverse)
                wires.start(
                    code.at[h, s, o - 1], got.at[h, s, o - 1], plane.device(h, o, 0), 2 + 2 * at + h
                )
    units, sums = {}, {}
    for h in (0, 1):
        arrived(lines.at[h], wires.recv.at[h])
        units[h] = [tile_of(lines[h, k, 0:1]) for k in range(RING - 1)]
        sums[h] = unit + (units[h][0] + units[h][1] + units[h][2])
        line2[h] = line[...] + (lines[h, 0] + lines[h, 1] + lines[h, 2])
        for s in others:
            wires.start(line2.at[h], lines2.at[h, s - 1], plane.device(h, 0, s), 10 + h)
    for at, s in enumerate(order):
        for h in (0, 1):
            arrived(got.at[h, s], wires.recv.at[2 + 2 * at + h])
            total = part[block(h, 0, s)]
            for k in range(RING - 1):
                total = total + decode(got[h, s, k], column(units[h][k]))
            if s == 0:
                own[h] = total
            else:
                code2[h, s - 1] = encode(total, column(1.0 / sums[h]))
                wires.start(
                    code2.at[h, s - 1], got2.at[h, s - 1], plane.device(h, 0, s), 12 + h
                )
    for h in (0, 1):
        arrived(lines2.at[h], wires.recv.at[10 + h])
        arrived(got2.at[h], wires.recv.at[12 + h])
        total = own[h]
        for k in range(RING - 1):
            total = total + decode(got2[h, k], column(tile_of(lines2[h, k, 0:1])))
        out[h] = total


def scatter_rooms(depth, width):
    f32 = jnp.float32
    i16 = jnp.int16
    others = RING - 1
    return [
        pltpu.VMEM((2, RING, others, depth, width), i16),
        pltpu.VMEM((2, RING, others, depth, width), i16),
        pltpu.VMEM((SUB, depth), f32),
        pltpu.VMEM((2, others, SUB, depth), f32),
        pltpu.VMEM((2, others, depth, width), i16),
        pltpu.VMEM((2, others, depth, width), i16),
        pltpu.VMEM((2, SUB, depth), f32),
        pltpu.VMEM((2, others, SUB, depth), f32),
        pltpu.VMEM((2, depth, width), f32),
    ]


SQUARE_STEPS = 3


def sum_square(wires, at, part, out, by_col, by_row, mine):
    rows, cols = lax.axis_size("rows"), lax.axis_size("cols")
    row, col = lax.axis_index("rows"), lax.axis_index("cols")
    share = part.shape[0] // cols
    x, core = col // 2, lax.rem(col, 2)
    z, y = row // RING, lax.rem(row, RING)

    def span(at):
        return pl.ds(at * share, share)

    far = {0: 0, 1: 1, 2: 2, 3: 1}
    col_peers = [
        shifted(x, o) * 2 + lax.rem(core + c, 2)
        for o, c in ((2, 0), (2, 1), (1, 0), (3, 0), (1, 1), (3, 1), (0, 1))
    ]
    steps = [(a, b) for a in range(RING) for b in range(RING) if a or b]
    row_peers = [
        shifted(z, a) * RING + shifted(y, b)
        for a, b in sorted(steps, key=lambda step: -far[step[0]] - far[step[1]])
    ]
    for peer in col_peers:
        wires.start(part.at[span(peer)], by_col.at[col], (row, peer), at)
    by_col[col] = part[span(col)]
    arrived(by_col.at[pl.ds(0, cols - 1)], wires.recv.at[at])
    mine[...] = jnp.sum(by_col[...], axis=0)
    for peer in row_peers:
        wires.start(mine, by_row.at[row], (peer, col), at + 1)
    by_row[row] = mine[...]
    arrived(by_row.at[pl.ds(0, rows - 1)], wires.recv.at[at + 1])
    out[span(col)] = jnp.sum(by_row[...], axis=0)
    for peer in col_peers:
        wires.start(out.at[span(col)], out.at[span(col)], (row, peer), at + 2)
    arrived(out.at[pl.ds(0, (cols - 1) * share)], wires.recv.at[at + 2])
    wires.drain(
        by_col.at[pl.ds(0, cols - 1)],
        by_row.at[pl.ds(0, rows - 1)],
        out.at[pl.ds(0, (cols - 1) * share)],
    )


def square_rooms(order, rows, cols):
    share = order // cols
    return [
        pltpu.VMEM((cols, share, order), jnp.float32),
        pltpu.VMEM((rows, share, order), jnp.float32),
        pltpu.VMEM((share, order), jnp.float32),
    ]


def all_peers():
    rows, cols = lax.axis_size("rows"), lax.axis_size("cols")
    row, col = lax.axis_index("rows"), lax.axis_index("cols")
    return [(lax.rem(row + o, rows), col) for o in range(1, rows)] + [
        (row, lax.rem(col + o, cols)) for o in range(1, cols)
    ]


GROUP = 8


def local_column(column):
    row = lax.axis_index("rows")
    panel, half = column // 16, lax.rem(column, 2)
    along_z = lax.rem(panel // RING + RING - row // RING, RING)
    along_y = lax.rem(lax.rem(panel, RING) + RING - lax.rem(row, RING), RING)
    first = jnp.where(half == 0, along_y, along_z)
    second = jnp.where(half == 0, along_z, along_y)
    return (half * RING + first) * RING + second


def products_kernel(transposed, count_ref, row_ref, col_ref, panels, tiles, out):
    count = count_ref[0, 0]
    out[...] = jnp.zeros_like(out)

    def step(group, carry):
        slots = [group * GROUP + u for u in range(GROUP)]
        rows = [row_ref[0, 0, slot] for slot in slots]
        cols = [local_column(col_ref[0, 0, slot]) for slot in slots]
        if transposed:
            terms = [
                jnp.dot(panels[r], tiles[slot], preferred_element_type=jnp.float32)
                for r, slot in zip(rows, slots)
            ]
        else:
            terms = [
                jnp.dot(tiles[slot], panels[c], preferred_element_type=jnp.float32)
                for c, slot in zip(cols, slots)
            ]
        for slot, term, place in zip(slots, terms, cols if transposed else rows):
            out[place] += jnp.where(slot < count, term, 0.0)
        return carry

    lax.fori_loop(0, (count + GROUP - 1) // GROUP, step, 0)


def products(transposed, out_shape, count, rows, cols, panels, tiles):
    return pl.pallas_call(
        functools.partial(products_kernel, transposed),
        out_shape=jax.ShapeDtypeStruct(out_shape, jnp.float32),
        in_specs=[VMEM, SMEM, SMEM, VMEM, VMEM],
        out_specs=VMEM,
        compiler_params=pltpu.CompilerParams(vmem_limit_bytes=32 << 20),
    )(count, rows, cols, panels, tiles)


def factor(gram, upper_ref, inverse_ref):
    order = gram.shape[0]
    lead = gram
    tail = (
        lax.broadcasted_iota(jnp.int32, (order, order), 0)
        == lax.broadcasted_iota(jnp.int32, (order, order), 1)
    ).astype(jnp.float32)
    for base in range(0, order, SUB):
        left = order - base
        columns = [
            jnp.broadcast_to(lead[:, base + k : base + k + 1], (left, order)) for k in range(SUB)
        ]
        position = lax.broadcasted_iota(jnp.int32, (left, order), 0)
        top = lax.broadcasted_iota(jnp.int32, (SUB, order), 0)
        lane = lax.broadcasted_iota(jnp.int32, (SUB, order), 1)
        pivots = jnp.zeros((SUB, order), jnp.float32)
        for k in range(SUB):
            pivot = columns[k][k : k + 1, :]
            pivots = jnp.where(top == k, pivot, pivots)
            ratio = jnp.where(position > k, columns[k] * (1.0 / pivot), 0.0)
            lead = lead - ratio * lead[k : k + 1, :]
            tail = tail - ratio * tail[k : k + 1, :]
            for j in range(k + 1, SUB):
                columns[j] = columns[j] - ratio * columns[j][k : k + 1, :]
        scale = 1.0 / jnp.sqrt(pivots)
        upper_ref[base : base + SUB, :] = jnp.where(lane >= base + top, lead[:SUB] * scale, 0.0)
        inverse_ref[base : base + SUB, :] = tail[:SUB] * scale
        lead = lead[SUB:]
        tail = tail[SUB:]


def inner(x_ref, out):
    out[...] = matmul(x_ref[0], x_ref[0], NT) + matmul(x_ref[1], x_ref[1], NT)


def basis_kernel(
    root, part, basis_ref, triangle_ref, spread_ref, x_ref, square, gram, inverse, *rest
):
    rooms, (by_col, by_row, mine, send, recv, send2) = rest[:9], rest[9:]
    plane = Plane()
    wires = Wires(send, recv)
    scatter_sum(plane, wires, all_peers(), part, x_ref, *rooms)
    inner(x_ref, square)
    wires.send = send2
    sum_square(wires, SCATTER_STEPS, square, gram, by_col, by_row, mine)
    factor(gram[...], triangle_ref, inverse)
    width = x_ref.shape[2]
    for s in range(2):
        basis_ref[s * width : (s + 1) * width, :] = matmul(inverse[...], x_ref[s], NN).T * root
    triangle_ref[...] = triangle_ref[...] / root
    order = gram.shape[0]
    diagonal = lax.broadcasted_iota(jnp.int32, (order, order), 0) == lax.broadcasted_iota(
        jnp.int32, (order, order), 1
    )
    lengths = jnp.sum(jnp.where(diagonal, gram[...], 0.0), axis=0, keepdims=True)
    inverses = jnp.sum(inverse[...] * inverse[...], axis=0, keepdims=True)
    spread = jnp.sum(lengths * inverses, axis=1, keepdims=True)
    spread_ref[0, 0] = spread[0, 0]
    wires.send = send
    code, got, line, lines, code2, got2, line2, lines2, own = rooms
    wires.drain(got, got2, lines, lines2)


def orthonormalize(root, part):
    _, depth, width = part.shape
    rows, cols = lax.axis_size("rows"), lax.axis_size("cols")
    f32 = jnp.float32
    square = pltpu.VMEM((depth, depth), f32)
    return pl.pallas_call(
        functools.partial(basis_kernel, root),
        out_shape=[
            jax.ShapeDtypeStruct((2 * width, depth), f32),
            jax.ShapeDtypeStruct((depth, depth), f32),
            jax.ShapeDtypeStruct((1, 1), f32),
        ],
        in_specs=[VMEM],
        out_specs=[VMEM, VMEM, SMEM],
        scratch_shapes=[pltpu.VMEM((2, depth, width), f32)]
        + [square] * 3
        + scatter_rooms(depth, width)
        + square_rooms(depth, rows, cols)
        + [
            pltpu.SemaphoreType.DMA,
            pltpu.SemaphoreType.DMA((SCATTER_STEPS + SQUARE_STEPS,)),
            pltpu.SemaphoreType.DMA,
        ],
        compiler_params=pltpu.CompilerParams(
            collective_id=2, has_side_effects=True, vmem_limit_bytes=40 << 20
        ),
    )(part)


def again_kernel(
    root, basis_in, triangle_in, basis_ref, triangle_ref, x, square, gram, upper, inverse, *rest
):
    by_col, by_row, mine, send, recv = rest
    wires = Wires(send, recv)
    greet(all_peers())
    x[...] = basis_in[...].T / root
    square[...] = matmul(x[...], x[...], NT)
    sum_square(wires, 0, square, gram, by_col, by_row, mine)
    factor(gram[...], upper, inverse)
    basis_ref[...] = matmul(inverse[...], x[...], NN).T * root
    triangle_ref[...] = matmul(upper[...], triangle_in[...], NN)


def second_pass(root, basis, triangle):
    size, depth = basis.shape
    f32 = jnp.float32
    return pl.pallas_call(
        functools.partial(again_kernel, root),
        out_shape=[
            jax.ShapeDtypeStruct(basis.shape, f32),
            jax.ShapeDtypeStruct(triangle.shape, f32),
        ],
        in_specs=[VMEM] * 2,
        out_specs=[VMEM] * 2,
        scratch_shapes=[pltpu.VMEM((depth, size), f32)]
        + [pltpu.VMEM((depth, depth), f32)] * 4
        + square_rooms(depth, lax.axis_size("rows"), lax.axis_size("cols"))
        + [pltpu.SemaphoreType.DMA, pltpu.SemaphoreType.DMA((SQUARE_STEPS,))],
        compiler_params=pltpu.CompilerParams(
            collective_id=3, has_side_effects=True, vmem_limit_bytes=32 << 20
        ),
    )(basis, triangle)


def body(start_basis, block_values, slot_count, slot_row, slot_col):
    depth = start_basis.shape[1]
    width = block_values.shape[-1]
    panel_blocks = start_basis.shape[0] // width
    rows, cols = lax.axis_size("rows"), lax.axis_size("cols")
    column_blocks = rows * panel_blocks // cols
    held = [
        pltpu.with_memory_space_constraint(array, pltpu.HBM)
        for array in (
            start_basis.reshape(panel_blocks, width, depth),
            block_values.reshape(block_values.shape[2:]),
            slot_row,
            slot_col,
        )
    ]
    basis_parts, tiles, *indices = gather(*held[:2], held[2:], rows)
    image_part = products(
        False,
        (panel_blocks, width, depth),
        slot_count,
        *indices,
        basis_parts.reshape(column_blocks, width, depth),
        tiles,
    )
    image = sum_image(image_part)
    back_part = products(
        True, (column_blocks, depth, width), slot_count, *indices, image, tiles
    )
    root = float(rows * panel_blocks * width) ** 0.5
    basis, triangle, spread = orthonormalize(root, back_part)
    return lax.cond(
        spread[0, 0] <= 2.0 * depth,
        lambda basis, triangle: (basis, triangle),
        functools.partial(second_pass, root),
        basis,
        triangle,
    )


def solution(mesh):
    return jax.shard_map(
        body,
        mesh=mesh,
        in_specs=(
            P("rows", None),
            P("rows", "cols", None, None, None),
            P("rows", "cols"),
            P("rows", "cols", None),
            P("rows", "cols", None),
        ),
        out_specs=(P(("rows", "cols"), None), P()),
        check_vma=False,
    )
```

```python
import functools

import jax
import jax.numpy as jnp
from jax import lax
from jax.experimental import pallas as pl
from jax.experimental.pallas import tpu as pltpu
from jax.sharding import PartitionSpec as P

SUB = 8
RING = 4
TOP = 32000.0
LEAST = 1e-33
VMEM = pl.BlockSpec(memory_space=pltpu.VMEM)
SMEM = pl.BlockSpec(memory_space=pltpu.SMEM)
HBM = pl.BlockSpec(memory_space=pltpu.HBM)
NN = (((1,), (0,)), ((), ()))
NT = (((1,), (1,)), ((), ()))


def matmul(a, b, dims):
    return lax.dot_general(
        a, b, dims, precision=lax.Precision.HIGHEST, preferred_element_type=jnp.float32
    )


class Wires:
    def __init__(self, send, recv):
        self.send, self.recv, self.used = send, recv, 0

    def start(self, src, dst, device, at=None):
        if at is None:
            at = self.used
            self.used += 1
        copy = pltpu.make_async_remote_copy(
            src_ref=src,
            dst_ref=dst,
            send_sem=self.send,
            recv_sem=self.recv.at[at],
            device_id=device,
            device_id_type=pl.DeviceIdType.MESH,
        )
        copy.start()
        return copy

    def drain(self, *refs):
        for ref in refs:
            pltpu.make_async_copy(ref, ref, self.send).wait()


def announce(peers):
    barrier = pltpu.get_barrier_semaphore()
    for peer in peers:
        pl.semaphore_signal(
            barrier, inc=1, device_id=peer, device_id_type=pl.DeviceIdType.MESH
        )


def greet(peers):
    announce(peers)
    pl.semaphore_wait(pltpu.get_barrier_semaphore(), len(peers))


def arrived(ref, sem):
    pltpu.make_async_copy(ref, ref, sem).wait()


def encode(value, inverse):
    return jnp.round(value * inverse).astype(jnp.int32).astype(jnp.int16)


def decode(code, unit):
    return code.astype(jnp.int32).astype(jnp.float32) * unit


def shifted(at, offset):
    return lax.rem(at + offset % RING, RING)


class Plane:
    def __init__(self):
        row = lax.axis_index("rows")
        self.col = lax.axis_index("cols")
        self.z, self.y = row // RING, lax.rem(row, RING)

    def row(self, half, first, second):
        along_y, along_z = (first, second) if half == 0 else (second, first)
        return shifted(self.z, along_z) * RING + shifted(self.y, along_y)

    def device(self, half, first, second):
        return (self.row(half, first, second), self.col)

    def neighbours(self):
        return [self.device(0, o, 0) for o in (2, 1, 3)] + [self.device(0, 0, o) for o in (2, 1, 3)]


GATHER_COPIES = 38


def gather_kernel(
    basis, values, rows, cols, out, tiles, rows_out, cols_out, send, recv, local
):
    plane = Plane()
    wires = Wires(send, recv)
    load = pltpu.make_async_copy(basis.at[pl.ds(plane.col * 2, 2)], out.at[:, 0, 0], local.at[0])
    load.start()
    kept = [
        pltpu.make_async_copy(src, dst, local.at[1 + at])
        for at, (src, dst) in enumerate(
            ((values, tiles), (rows, rows_out), (cols, cols_out))
        )
    ]
    for copy in kept:
        copy.start()
    greet(plane.neighbours())
    load.wait()
    cut = out.shape[3] // 2
    upper, lower = pl.ds(0, cut), pl.ds(cut, cut)
    near, rest, ends = {}, {}, []
    for o in (1, 3, 2):
        for h in (0, 1):
            near[h, o] = wires.start(
                out.at[h, 0, 0], out.at[h, RING - o, 0], plane.device(h, o, 0)
            )
    for o in (1, 3):
        for h in (0, 1):
            rest[h, 0, o] = wires.start(
                out.at[h, 0, 0], out.at[h, 0, RING - o], plane.device(h, 0, o)
            )
    for f in (3, 1, 2):
        for h in (0, 1):
            near[h, RING - f].wait_recv()
            for o in (1, 3):
                rest[h, f, o] = wires.start(
                    out.at[h, f, 0], out.at[h, f, RING - o], plane.device(h, 0, o)
                )
    for f in (0, 3, 1, 2):
        for o, piece in ((1, upper), (3, lower)):
            for h in (0, 1):
                rest[h, f, o].wait_recv()
                ends.append(
                    wires.start(
                        out.at[h, f, RING - o, piece], out.at[h, f, 2, piece], plane.device(h, 0, o)
                    )
                )
    for copy in ends:
        copy.wait_recv()
    for copy in kept:
        copy.wait()
    wires.drain(out.at[0], out.at[1, pl.ds(0, 3)], out.at[1, 3, pl.ds(0, 2)])


def gather(basis, values, indices, rows):
    return pl.pallas_call(
        gather_kernel,
        out_shape=[
            jax.ShapeDtypeStruct((2, rows // RING, RING) + basis.shape[1:], basis.dtype),
            jax.ShapeDtypeStruct(values.shape, values.dtype),
        ]
        + [jax.ShapeDtypeStruct(index.shape, index.dtype) for index in indices],
        in_specs=[HBM] * 4,
        out_specs=[VMEM] * 2 + [SMEM] * 2,
        scratch_shapes=[
            pltpu.SemaphoreType.DMA,
            pltpu.SemaphoreType.DMA((GATHER_COPIES,)),
            pltpu.SemaphoreType.DMA((4,)),
        ],
        compiler_params=pltpu.CompilerParams(
            collective_id=0, has_side_effects=True, vmem_limit_bytes=44 << 20
        ),
    )(basis, values, *indices)


IMAGE_COPIES = 24


def image_kernel(
    part, image, sibling, total, code, unit, got, units, send, recv, send2, send3
):
    row, col = lax.axis_index("rows"), lax.axis_index("cols")
    x, core = col // 2, lax.rem(col, 2)
    twin = (row, x * 2 + 1 - core)
    peer = {o: (row, shifted(x, o) * 2 + core) for o in (1, 2, 3)}
    wires = Wires(send, recv)
    greet([twin, peer[1], peer[2], peer[3]])
    sub = image.shape[0] // 8

    def chunk(offset, which):
        return pl.ds((shifted(x, offset) * 2 + which) * sub, sub)

    order = (2, 1, 3, 0)
    swap = {
        o: wires.start(part.at[chunk(o, 1 - core)], sibling.at[o], twin) for o in order
    }
    wires.send = send2
    coded, scaled = {}, {}
    for o in order:
        swap[o].wait_recv()
        whole = part[chunk(o, core)] + sibling[o]
        if o == 0:
            total[...] = whole
            continue
        most = jnp.max(jnp.max(jnp.abs(whole), axis=0), axis=0, keepdims=True)
        step = jnp.maximum(most, LEAST) * (1.0 / TOP)
        unit[o - 1] = jnp.broadcast_to(step, unit.shape[1:])
        code[o - 1] = encode(whole, (1.0 / step)[None])
        scaled[o] = wires.start(unit.at[o - 1], units.at[o - 1], peer[o])
        coded[o, 0] = wires.start(code.at[o - 1, 0], got.at[o - 1, 0], peer[o])
    for o in (2, 1, 3):
        coded[o, 1] = wires.start(code.at[o - 1, 1], got.at[o - 1, 1], peer[o])
    for o in (1, 3, 2):
        scaled[o].wait_recv()
    wires.send = send3
    mine = (x * 2 + core) * sub
    sends = []
    for b in range(2):
        value = total[b]
        for o in (1, 3, 2):
            coded[o, b].wait_recv()
            value = value + decode(got[o - 1, b], units[o - 1, 0:1])
        image[mine + b] = value.T.astype(image.dtype)
        block = image.at[mine + b]
        sends.append({o: wires.start(block, block, peer[o]) for o in (2, 1, 3)})
    both = image.at[pl.ds(mine, sub)]
    last = [wires.start(both, both, twin)]
    for o in (1, 3, 2):
        for b in (0, 1):
            sends[b][o].wait_recv()
        pair = image.at[pl.ds((shifted(x, RING - o) * 2 + core) * sub, sub)]
        last.append(wires.start(pair, pair, twin))
    for copy in last:
        copy.wait_recv()
    wires.drain(image.at[pl.ds(0, 14)])
    wires.send = send2
    wires.drain(got, units)
    wires.send = send
    wires.drain(part.at[pl.ds(0, 8)])


def sum_image(part):
    blocks, width, depth = part.shape
    f32 = jnp.float32
    return pl.pallas_call(
        image_kernel,
        out_shape=jax.ShapeDtypeStruct((blocks, depth, width), jnp.bfloat16),
        in_specs=[VMEM],
        out_specs=VMEM,
        scratch_shapes=[
            pltpu.VMEM((RING, 2, width, depth), f32),
            pltpu.VMEM((2, width, depth), f32),
            pltpu.VMEM((RING - 1, 2, width, depth), jnp.int16),
            pltpu.VMEM((RING - 1, SUB, depth), f32),
            pltpu.VMEM((RING - 1, 2, width, depth), jnp.int16),
            pltpu.VMEM((RING - 1, SUB, depth), f32),
            pltpu.SemaphoreType.DMA,
            pltpu.SemaphoreType.DMA((IMAGE_COPIES,)),
            pltpu.SemaphoreType.DMA,
            pltpu.SemaphoreType.DMA,
        ],
        compiler_params=pltpu.CompilerParams(
            collective_id=1, has_side_effects=True, vmem_limit_bytes=32 << 20
        ),
    )(part)


SCATTER_STEPS = 14


def tile_of(row):
    return jnp.broadcast_to(row, (row.shape[1], row.shape[1])).T


def scatter_sum(plane, wires, peers, part, out, code, got, line, lines, code2, got2, line2, lines2, own):
    others = (2, 1, 3)
    order = (2, 3, 1, 0)

    def block(h, first, second):
        return (h * RING + first) * RING + second

    def column(tile):
        return jnp.concatenate([tile, tile], axis=1)

    announce(peers)
    most = lax.fori_loop(
        0,
        part.shape[0],
        lambda at, most: jnp.maximum(most, jnp.abs(part[at])),
        jnp.zeros(part.shape[1:], jnp.float32),
    )
    most = jnp.broadcast_to(jnp.max(most, axis=1, keepdims=True), line.shape[1:] * 2)
    unit = jnp.maximum(most, LEAST) * (1.0 / TOP)
    line[...] = unit.T[:SUB]
    inverse = column(1.0 / unit)
    pl.semaphore_wait(pltpu.get_barrier_semaphore(), len(peers))
    for at, s in enumerate(order):
        if at == 1:
            for h in (0, 1):
                for o in others:
                    wires.start(line, lines.at[h, o - 1], plane.device(h, o, 0), h)
        for o in others:
            for h in (0, 1):
                code[h, s, o - 1] = encode(part[block(h, o, s)], inverse)
                wires.start(
                    code.at[h, s, o - 1], got.at[h, s, o - 1], plane.device(h, o, 0), 2 + 2 * at + h
                )
    units, sums = {}, {}
    for h in (0, 1):
        arrived(lines.at[h], wires.recv.at[h])
        units[h] = [tile_of(lines[h, k, 0:1]) for k in range(RING - 1)]
        sums[h] = unit + (units[h][0] + units[h][1] + units[h][2])
        line2[h] = line[...] + (lines[h, 0] + lines[h, 1] + lines[h, 2])
        for s in others:
            wires.start(line2.at[h], lines2.at[h, s - 1], plane.device(h, 0, s), 10 + h)
    for at, s in enumerate(order):
        for h in (0, 1):
            arrived(got.at[h, s], wires.recv.at[2 + 2 * at + h])
            total = part[block(h, 0, s)]
            for k in range(RING - 1):
                total = total + decode(got[h, s, k], column(units[h][k]))
            if s == 0:
                own[h] = total
            else:
                code2[h, s - 1] = encode(total, column(1.0 / sums[h]))
                wires.start(
                    code2.at[h, s - 1], got2.at[h, s - 1], plane.device(h, 0, s), 12 + h
                )
    for h in (0, 1):
        arrived(lines2.at[h], wires.recv.at[10 + h])
        arrived(got2.at[h], wires.recv.at[12 + h])
        total = own[h]
        for k in range(RING - 1):
            total = total + decode(got2[h, k], column(tile_of(lines2[h, k, 0:1])))
        out[h] = total


def scatter_rooms(depth, width):
    f32 = jnp.float32
    i16 = jnp.int16
    others = RING - 1
    return [
        pltpu.VMEM((2, RING, others, depth, width), i16),
        pltpu.VMEM((2, RING, others, depth, width), i16),
        pltpu.VMEM((SUB, depth), f32),
        pltpu.VMEM((2, others, SUB, depth), f32),
        pltpu.VMEM((2, others, depth, width), i16),
        pltpu.VMEM((2, others, depth, width), i16),
        pltpu.VMEM((2, SUB, depth), f32),
        pltpu.VMEM((2, others, SUB, depth), f32),
        pltpu.VMEM((2, depth, width), f32),
    ]


SQUARE_STEPS = 3


def sum_square(wires, at, part, out, by_col, by_row, mine):
    rows, cols = lax.axis_size("rows"), lax.axis_size("cols")
    row, col = lax.axis_index("rows"), lax.axis_index("cols")
    share = part.shape[0] // cols
    x, core = col // 2, lax.rem(col, 2)
    z, y = row // RING, lax.rem(row, RING)

    def span(at):
        return pl.ds(at * share, share)

    far = {0: 0, 1: 1, 2: 2, 3: 1}
    col_peers = [
        shifted(x, o) * 2 + lax.rem(core + c, 2)
        for o, c in ((2, 0), (2, 1), (1, 0), (3, 0), (1, 1), (3, 1), (0, 1))
    ]
    steps = [(a, b) for a in range(RING) for b in range(RING) if a or b]
    row_peers = [
        shifted(z, a) * RING + shifted(y, b)
        for a, b in sorted(steps, key=lambda step: -far[step[0]] - far[step[1]])
    ]
    for peer in col_peers:
        wires.start(part.at[span(peer)], by_col.at[col], (row, peer), at)
    by_col[col] = part[span(col)]
    arrived(by_col.at[pl.ds(0, cols - 1)], wires.recv.at[at])
    mine[...] = jnp.sum(by_col[...], axis=0)
    for peer in row_peers:
        wires.start(mine, by_row.at[row], (peer, col), at + 1)
    by_row[row] = mine[...]
    arrived(by_row.at[pl.ds(0, rows - 1)], wires.recv.at[at + 1])
    out[span(col)] = jnp.sum(by_row[...], axis=0)
    for peer in col_peers:
        wires.start(out.at[span(col)], out.at[span(col)], (row, peer), at + 2)
    arrived(out.at[pl.ds(0, (cols - 1) * share)], wires.recv.at[at + 2])
    wires.drain(
        by_col.at[pl.ds(0, cols - 1)],
        by_row.at[pl.ds(0, rows - 1)],
        out.at[pl.ds(0, (cols - 1) * share)],
    )


def square_rooms(order, rows, cols):
    share = order // cols
    return [
        pltpu.VMEM((cols, share, order), jnp.float32),
        pltpu.VMEM((rows, share, order), jnp.float32),
        pltpu.VMEM((share, order), jnp.float32),
    ]


def all_peers():
    rows, cols = lax.axis_size("rows"), lax.axis_size("cols")
    row, col = lax.axis_index("rows"), lax.axis_index("cols")
    return [(lax.rem(row + o, rows), col) for o in range(1, rows)] + [
        (row, lax.rem(col + o, cols)) for o in range(1, cols)
    ]


GROUP = 16


def local_column(column):
    row = lax.axis_index("rows")
    panel, half = column // 16, lax.rem(column, 2)
    along_z = lax.rem(panel // RING + RING - row // RING, RING)
    along_y = lax.rem(lax.rem(panel, RING) + RING - lax.rem(row, RING), RING)
    first = jnp.where(half == 0, along_y, along_z)
    second = jnp.where(half == 0, along_z, along_y)
    return (half * RING + first) * RING + second


def products_kernel(transposed, count_ref, row_ref, col_ref, panels, tiles, out):
    count = count_ref[0, 0]
    out[...] = jnp.zeros_like(out)

    def step(group, carry):
        slots = [group * GROUP + u for u in range(GROUP)]
        rows = [row_ref[0, 0, slot] for slot in slots]
        cols = [local_column(col_ref[0, 0, slot]) for slot in slots]
        if transposed:
            terms = [
                jnp.dot(panels[r], tiles[slot], preferred_element_type=jnp.float32)
                for r, slot in zip(rows, slots)
            ]
        else:
            terms = [
                jnp.dot(tiles[slot], panels[c], preferred_element_type=jnp.float32)
                for c, slot in zip(cols, slots)
            ]
        for slot, term, place in zip(slots, terms, cols if transposed else rows):
            out[place] += jnp.where(slot < count, term, 0.0)
        return carry

    lax.fori_loop(0, (count + GROUP - 1) // GROUP, step, 0)


def products(transposed, out_shape, count, rows, cols, panels, tiles):
    return pl.pallas_call(
        functools.partial(products_kernel, transposed),
        out_shape=jax.ShapeDtypeStruct(out_shape, jnp.float32),
        in_specs=[VMEM, SMEM, SMEM, VMEM, VMEM],
        out_specs=VMEM,
        compiler_params=pltpu.CompilerParams(vmem_limit_bytes=32 << 20),
    )(count, rows, cols, panels, tiles)


def factor(gram, upper_ref, inverse_ref):
    order = gram.shape[0]
    lead = gram
    tail = (
        lax.broadcasted_iota(jnp.int32, (order, order), 0)
        == lax.broadcasted_iota(jnp.int32, (order, order), 1)
    ).astype(jnp.float32)
    for base in range(0, order, SUB):
        left = order - base
        columns = [
            jnp.broadcast_to(lead[:, base + k : base + k + 1], (left, order)) for k in range(SUB)
        ]
        position = lax.broadcasted_iota(jnp.int32, (left, order), 0)
        top = lax.broadcasted_iota(jnp.int32, (SUB, order), 0)
        lane = lax.broadcasted_iota(jnp.int32, (SUB, order), 1)
        pivots = jnp.zeros((SUB, order), jnp.float32)
        for k in range(SUB):
            pivot = columns[k][k : k + 1, :]
            pivots = jnp.where(top == k, pivot, pivots)
            ratio = jnp.where(position > k, columns[k] * (1.0 / pivot), 0.0)
            lead = lead - ratio * lead[k : k + 1, :]
            tail = tail - ratio * tail[k : k + 1, :]
            for j in range(k + 1, SUB):
                columns[j] = columns[j] - ratio * columns[j][k : k + 1, :]
        scale = 1.0 / jnp.sqrt(pivots)
        upper_ref[base : base + SUB, :] = jnp.where(lane >= base + top, lead[:SUB] * scale, 0.0)
        inverse_ref[base : base + SUB, :] = tail[:SUB] * scale
        lead = lead[SUB:]
        tail = tail[SUB:]


def inner(x_ref, out):
    out[...] = matmul(x_ref[0], x_ref[0], NT) + matmul(x_ref[1], x_ref[1], NT)


def basis_kernel(
    root, part, basis_ref, triangle_ref, spread_ref, x_ref, square, gram, inverse, *rest
):
    rooms, (by_col, by_row, mine, send, recv, send2) = rest[:9], rest[9:]
    plane = Plane()
    wires = Wires(send, recv)
    row, cols = lax.axis_index("rows"), lax.axis_size("cols")
    peers = plane.neighbours() + [
        (row, lax.rem(plane.col + o, cols)) for o in range(1, cols)
    ]
    scatter_sum(plane, wires, peers, part, x_ref, *rooms)
    inner(x_ref, square)
    wires.send = send2
    sum_square(wires, SCATTER_STEPS, square, gram, by_col, by_row, mine)
    factor(gram[...], triangle_ref, inverse)
    width = x_ref.shape[2]
    for s in range(2):
        basis_ref[s * width : (s + 1) * width, :] = matmul(inverse[...], x_ref[s], NN).T * root
    triangle_ref[...] = triangle_ref[...] / root
    order = gram.shape[0]
    diagonal = lax.broadcasted_iota(jnp.int32, (order, order), 0) == lax.broadcasted_iota(
        jnp.int32, (order, order), 1
    )
    lengths = jnp.sum(jnp.where(diagonal, gram[...], 0.0), axis=0, keepdims=True)
    inverses = jnp.sum(inverse[...] * inverse[...], axis=0, keepdims=True)
    spread = jnp.sum(lengths * inverses, axis=1, keepdims=True)
    spread_ref[0, 0] = spread[0, 0]
    wires.send = send
    code, got, line, lines, code2, got2, line2, lines2, own = rooms
    wires.drain(got, got2, lines, lines2)


def orthonormalize(root, part):
    _, depth, width = part.shape
    rows, cols = lax.axis_size("rows"), lax.axis_size("cols")
    f32 = jnp.float32
    square = pltpu.VMEM((depth, depth), f32)
    return pl.pallas_call(
        functools.partial(basis_kernel, root),
        out_shape=[
            jax.ShapeDtypeStruct((2 * width, depth), f32),
            jax.ShapeDtypeStruct((depth, depth), f32),
            jax.ShapeDtypeStruct((1, 1), f32),
        ],
        in_specs=[VMEM],
        out_specs=[VMEM, VMEM, SMEM],
        scratch_shapes=[pltpu.VMEM((2, depth, width), f32)]
        + [square] * 3
        + scatter_rooms(depth, width)
        + square_rooms(depth, rows, cols)
        + [
            pltpu.SemaphoreType.DMA,
            pltpu.SemaphoreType.DMA((SCATTER_STEPS + SQUARE_STEPS,)),
            pltpu.SemaphoreType.DMA,
        ],
        compiler_params=pltpu.CompilerParams(
            collective_id=2, has_side_effects=True, vmem_limit_bytes=40 << 20
        ),
    )(part)


def again_kernel(
    root, basis_in, triangle_in, basis_ref, triangle_ref, x, square, gram, upper, inverse, *rest
):
    by_col, by_row, mine, send, recv = rest
    wires = Wires(send, recv)
    greet(all_peers())
    x[...] = basis_in[...].T / root
    square[...] = matmul(x[...], x[...], NT)
    sum_square(wires, 0, square, gram, by_col, by_row, mine)
    factor(gram[...], upper, inverse)
    basis_ref[...] = matmul(inverse[...], x[...], NN).T * root
    triangle_ref[...] = matmul(upper[...], triangle_in[...], NN)


def second_pass(root, basis, triangle):
    size, depth = basis.shape
    f32 = jnp.float32
    return pl.pallas_call(
        functools.partial(again_kernel, root),
        out_shape=[
            jax.ShapeDtypeStruct(basis.shape, f32),
            jax.ShapeDtypeStruct(triangle.shape, f32),
        ],
        in_specs=[VMEM] * 2,
        out_specs=[VMEM] * 2,
        scratch_shapes=[pltpu.VMEM((depth, size), f32)]
        + [pltpu.VMEM((depth, depth), f32)] * 4
        + square_rooms(depth, lax.axis_size("rows"), lax.axis_size("cols"))
        + [pltpu.SemaphoreType.DMA, pltpu.SemaphoreType.DMA((SQUARE_STEPS,))],
        compiler_params=pltpu.CompilerParams(
            collective_id=3, has_side_effects=True, vmem_limit_bytes=32 << 20
        ),
    )(basis, triangle)


def body(start_basis, block_values, slot_count, slot_row, slot_col):
    depth = start_basis.shape[1]
    width = block_values.shape[-1]
    panel_blocks = start_basis.shape[0] // width
    rows, cols = lax.axis_size("rows"), lax.axis_size("cols")
    column_blocks = rows * panel_blocks // cols
    held = [
        pltpu.with_memory_space_constraint(array, pltpu.HBM)
        for array in (
            start_basis.reshape(panel_blocks, width, depth),
            block_values.reshape(block_values.shape[2:]),
            slot_row,
            slot_col,
        )
    ]
    basis_parts, tiles, *indices = gather(*held[:2], held[2:], rows)
    image_part = products(
        False,
        (panel_blocks, width, depth),
        slot_count,
        *indices,
        basis_parts.reshape(column_blocks, width, depth),
        tiles,
    )
    image = sum_image(image_part)
    back_part = products(
        True, (column_blocks, depth, width), slot_count, *indices, image, tiles
    )
    root = float(rows * panel_blocks * width) ** 0.5
    basis, triangle, spread = orthonormalize(root, back_part)
    return lax.cond(
        spread[0, 0] <= 2.0 * depth,
        lambda basis, triangle: (basis, triangle),
        functools.partial(second_pass, root),
        basis,
        triangle,
    )


def solution(mesh):
    return jax.shard_map(
        body,
        mesh=mesh,
        in_specs=(
            P("rows", None),
            P("rows", "cols", None, None, None),
            P("rows", "cols"),
            P("rows", "cols", None),
            P("rows", "cols", None),
        ),
        out_specs=(P(("rows", "cols"), None), P()),
        check_vma=False,
    )
```

```python
import functools

import jax
import jax.numpy as jnp
from jax import lax
from jax.experimental import pallas as pl
from jax.experimental.pallas import tpu as pltpu
from jax.sharding import PartitionSpec as P

SUB = 8
RING = 4
TOP = 32000.0
LEAST = 1e-33
VMEM = pl.BlockSpec(memory_space=pltpu.VMEM)
SMEM = pl.BlockSpec(memory_space=pltpu.SMEM)
HBM = pl.BlockSpec(memory_space=pltpu.HBM)
NN = (((1,), (0,)), ((), ()))
NT = (((1,), (1,)), ((), ()))


def matmul(a, b, dims):
    return lax.dot_general(
        a, b, dims, precision=lax.Precision.HIGHEST, preferred_element_type=jnp.float32
    )


class Wires:
    def __init__(self, send, recv):
        self.send, self.recv, self.used = send, recv, 0

    def start(self, src, dst, device, at=None):
        if at is None:
            at = self.used
            self.used += 1
        copy = pltpu.make_async_remote_copy(
            src_ref=src,
            dst_ref=dst,
            send_sem=self.send,
            recv_sem=self.recv.at[at],
            device_id=device,
            device_id_type=pl.DeviceIdType.MESH,
        )
        copy.start()
        return copy

    def drain(self, *refs):
        for ref in refs:
            pltpu.make_async_copy(ref, ref, self.send).wait()


def announce(peers):
    barrier = pltpu.get_barrier_semaphore()
    for peer in peers:
        pl.semaphore_signal(
            barrier, inc=1, device_id=peer, device_id_type=pl.DeviceIdType.MESH
        )


def greet(peers):
    announce(peers)
    pl.semaphore_wait(pltpu.get_barrier_semaphore(), len(peers))


def arrived(ref, sem):
    pltpu.make_async_copy(ref, ref, sem).wait()


def encode(value, inverse):
    return jnp.round(value * inverse).astype(jnp.int32).astype(jnp.int16)


def decode(code, unit):
    return code.astype(jnp.int32).astype(jnp.float32) * unit


def shifted(at, offset):
    return lax.rem(at + offset % RING, RING)


class Plane:
    def __init__(self):
        row = lax.axis_index("rows")
        self.col = lax.axis_index("cols")
        self.z, self.y = row // RING, lax.rem(row, RING)

    def row(self, half, first, second):
        along_y, along_z = (first, second) if half == 0 else (second, first)
        return shifted(self.z, along_z) * RING + shifted(self.y, along_y)

    def device(self, half, first, second):
        return (self.row(half, first, second), self.col)

    def neighbours(self):
        return [self.device(0, o, 0) for o in (2, 1, 3)] + [self.device(0, 0, o) for o in (2, 1, 3)]


GATHER_COPIES = 38


def gather_kernel(
    basis, values, rows, cols, out, tiles, rows_out, cols_out, send, recv, local
):
    plane = Plane()
    wires = Wires(send, recv)
    load = pltpu.make_async_copy(basis.at[pl.ds(plane.col * 2, 2)], out.at[:, 0, 0], local.at[0])
    load.start()
    kept = [
        pltpu.make_async_copy(src, dst, local.at[1 + at])
        for at, (src, dst) in enumerate(
            ((values, tiles), (rows, rows_out), (cols, cols_out))
        )
    ]
    for copy in kept:
        copy.start()
    greet(plane.neighbours())
    load.wait()
    cut = out.shape[3] // 2
    upper, lower = pl.ds(0, cut), pl.ds(cut, cut)
    near, rest, ends = {}, {}, []
    for o in (1, 3, 2):
        for h in (0, 1):
            near[h, o] = wires.start(
                out.at[h, 0, 0], out.at[h, RING - o, 0], plane.device(h, o, 0)
            )
    for o in (1, 3):
        for h in (0, 1):
            rest[h, 0, o] = wires.start(
                out.at[h, 0, 0], out.at[h, 0, RING - o], plane.device(h, 0, o)
            )
    for f in (3, 1, 2):
        for h in (0, 1):
            near[h, RING - f].wait_recv()
            for o in (1, 3):
                rest[h, f, o] = wires.start(
                    out.at[h, f, 0], out.at[h, f, RING - o], plane.device(h, 0, o)
                )
    for f in (0, 3, 1, 2):
        for o, piece in ((1, upper), (3, lower)):
            for h in (0, 1):
                rest[h, f, o].wait_recv()
                ends.append(
                    wires.start(
                        out.at[h, f, RING - o, piece], out.at[h, f, 2, piece], plane.device(h, 0, o)
                    )
                )
    for copy in ends:
        copy.wait_recv()
    for copy in kept:
        copy.wait()
    wires.drain(out.at[0], out.at[1, pl.ds(0, 3)], out.at[1, 3, pl.ds(0, 2)])


def gather(basis, values, indices, rows):
    return pl.pallas_call(
        gather_kernel,
        out_shape=[
            jax.ShapeDtypeStruct((2, rows // RING, RING) + basis.shape[1:], basis.dtype),
            jax.ShapeDtypeStruct(values.shape, values.dtype),
        ]
        + [jax.ShapeDtypeStruct(index.shape, index.dtype) for index in indices],
        in_specs=[HBM] * 4,
        out_specs=[VMEM] * 2 + [SMEM] * 2,
        scratch_shapes=[
            pltpu.SemaphoreType.DMA,
            pltpu.SemaphoreType.DMA((GATHER_COPIES,)),
            pltpu.SemaphoreType.DMA((4,)),
        ],
        compiler_params=pltpu.CompilerParams(
            collective_id=0, has_side_effects=True, vmem_limit_bytes=44 << 20
        ),
    )(basis, values, *indices)


IMAGE_COPIES = 24


def image_kernel(
    part, image, sibling, total, code, unit, got, units, send, recv, send2, send3
):
    row, col = lax.axis_index("rows"), lax.axis_index("cols")
    x, core = col // 2, lax.rem(col, 2)
    twin = (row, x * 2 + 1 - core)
    peer = {o: (row, shifted(x, o) * 2 + core) for o in (1, 2, 3)}
    wires = Wires(send, recv)
    greet([twin, peer[1], peer[2], peer[3]])
    sub = image.shape[0] // 8

    def chunk(offset, which):
        return pl.ds((shifted(x, offset) * 2 + which) * sub, sub)

    order = (2, 1, 3, 0)
    swap = {
        o: wires.start(part.at[chunk(o, 1 - core)], sibling.at[o], twin) for o in order
    }
    wires.send = send2
    coded, scaled = {}, {}
    for o in order:
        swap[o].wait_recv()
        whole = part[chunk(o, core)] + sibling[o]
        if o == 0:
            total[...] = whole
            continue
        most = jnp.max(jnp.max(jnp.abs(whole), axis=0), axis=0, keepdims=True)
        step = jnp.maximum(most, LEAST) * (1.0 / TOP)
        unit[o - 1] = jnp.broadcast_to(step, unit.shape[1:])
        code[o - 1] = encode(whole, (1.0 / step)[None])
        scaled[o] = wires.start(unit.at[o - 1], units.at[o - 1], peer[o])
        coded[o, 0] = wires.start(code.at[o - 1, 0], got.at[o - 1, 0], peer[o])
    for o in (2, 1, 3):
        coded[o, 1] = wires.start(code.at[o - 1, 1], got.at[o - 1, 1], peer[o])
    for o in (1, 3, 2):
        scaled[o].wait_recv()
    wires.send = send3
    mine = (x * 2 + core) * sub
    sends = []
    for b in range(2):
        value = total[b]
        for o in (1, 3, 2):
            coded[o, b].wait_recv()
            value = value + decode(got[o - 1, b], units[o - 1, 0:1])
        image[mine + b] = value.T.astype(image.dtype)
        block = image.at[mine + b]
        sends.append({o: wires.start(block, block, peer[o]) for o in (2, 1, 3)})
    both = image.at[pl.ds(mine, sub)]
    last = [wires.start(both, both, twin)]
    for o in (1, 3, 2):
        for b in (0, 1):
            sends[b][o].wait_recv()
        pair = image.at[pl.ds((shifted(x, RING - o) * 2 + core) * sub, sub)]
        last.append(wires.start(pair, pair, twin))
    for copy in last:
        copy.wait_recv()
    wires.drain(image.at[pl.ds(0, 14)])
    wires.send = send2
    wires.drain(got, units)
    wires.send = send
    wires.drain(part.at[pl.ds(0, 8)])


def sum_image(part):
    blocks, width, depth = part.shape
    f32 = jnp.float32
    return pl.pallas_call(
        image_kernel,
        out_shape=jax.ShapeDtypeStruct((blocks, depth, width), jnp.bfloat16),
        in_specs=[VMEM],
        out_specs=VMEM,
        scratch_shapes=[
            pltpu.VMEM((RING, 2, width, depth), f32),
            pltpu.VMEM((2, width, depth), f32),
            pltpu.VMEM((RING - 1, 2, width, depth), jnp.int16),
            pltpu.VMEM((RING - 1, SUB, depth), f32),
            pltpu.VMEM((RING - 1, 2, width, depth), jnp.int16),
            pltpu.VMEM((RING - 1, SUB, depth), f32),
            pltpu.SemaphoreType.DMA,
            pltpu.SemaphoreType.DMA((IMAGE_COPIES,)),
            pltpu.SemaphoreType.DMA,
            pltpu.SemaphoreType.DMA,
        ],
        compiler_params=pltpu.CompilerParams(
            collective_id=1, has_side_effects=True, vmem_limit_bytes=32 << 20
        ),
    )(part)


SCATTER_STEPS = 22


def tile_of(row):
    return jnp.broadcast_to(row, (row.shape[1], row.shape[1])).T


def scatter_sum(plane, wires, peers, part, out, early, hop, code, got, line, lines, code2, got2, line2, lines2, own):
    others = (2, 1, 3)
    order = (2, 3, 1, 0)

    def block(h, first, second):
        return (h * RING + first) * RING + second

    def column(tile):
        return jnp.concatenate([tile, tile], axis=1)

    announce(peers)
    most = lax.fori_loop(
        0,
        part.shape[0],
        lambda at, most: jnp.maximum(most, jnp.abs(part[at])),
        jnp.zeros(part.shape[1:], jnp.float32),
    )
    most = jnp.broadcast_to(jnp.max(most, axis=1, keepdims=True), line.shape[1:] * 2)
    unit = jnp.maximum(most, LEAST) * (1.0 / TOP)
    line[...] = unit.T[:SUB]
    inverse = column(1.0 / unit)
    pl.semaphore_wait(pltpu.get_barrier_semaphore(), len(peers))
    for h in (0, 1):
        for o in others:
            wires.start(line, lines.at[h, o - 1], plane.device(h, o, 0), h)
    way = {2: 0, 1: 0, 3: 1, 0: 1}
    offset = (1, 3)
    for at, s in enumerate(order):
        for h in (0, 1):
            early[h, s] = encode(part[block(h, 2, s)], inverse)
            wires.start(
                early.at[h, s], hop.at[h, s], plane.device(h, offset[way[s]], 0), 14 + 2 * at + h
            )
    for at, s in enumerate(order):
        w = 1 - way[s]
        for h in (0, 1):
            code[h, s, w] = encode(part[block(h, offset[w], s)], inverse)
            wires.start(
                code.at[h, s, w], got.at[h, s, w], plane.device(h, offset[w], 0), 2 + 2 * at + h
            )
    units, sums = {}, {}
    for h in (0, 1):
        arrived(lines.at[h], wires.recv.at[h])
        units[h] = [tile_of(lines[h, k, 0:1]) for k in range(RING - 1)]
        sums[h] = unit + (units[h][0] + units[h][1] + units[h][2])
        line2[h] = line[...] + (lines[h, 0] + lines[h, 1] + lines[h, 2])
        for s in others:
            wires.start(line2.at[h], lines2.at[h, s - 1], plane.device(h, 0, s), 10 + h)
    for at, s in enumerate(order):
        w = way[s]
        for h in (0, 1):
            near = units[h][offset[w] - 1]
            arrived(hop.at[h, s], wires.recv.at[14 + 2 * at + h])
            merged = part[block(h, offset[w], s)] + decode(hop[h, s], column(near))
            code[h, s, w] = encode(merged, column(1.0 / (unit + near)))
            wires.start(
                code.at[h, s, w], got.at[h, s, w], plane.device(h, offset[w], 0), 2 + 2 * at + h
            )
    for at, s in enumerate(order):
        w = way[s]
        for h in (0, 1):
            arrived(got.at[h, s], wires.recv.at[2 + 2 * at + h])
            both = units[h][offset[w] - 1] + units[h][1]
            total = part[block(h, 0, s)] + decode(got[h, s, w], column(both))
            total = total + decode(got[h, s, 1 - w], column(units[h][offset[1 - w] - 1]))
            if s == 0:
                own[h] = total
            else:
                code2[h, s - 1] = encode(total, column(1.0 / sums[h]))
                wires.start(
                    code2.at[h, s - 1], got2.at[h, s - 1], plane.device(h, 0, s), 12 + h
                )
    for h in (0, 1):
        arrived(lines2.at[h], wires.recv.at[10 + h])
        arrived(got2.at[h], wires.recv.at[12 + h])
        total = own[h]
        for k in range(RING - 1):
            total = total + decode(got2[h, k], column(tile_of(lines2[h, k, 0:1])))
        out[h] = total


def scatter_rooms(depth, width):
    f32 = jnp.float32
    i16 = jnp.int16
    others = RING - 1
    return [
        pltpu.VMEM((2, RING, depth, width), i16),
        pltpu.VMEM((2, RING, depth, width), i16),
        pltpu.VMEM((2, RING, 2, depth, width), i16),
        pltpu.VMEM((2, RING, 2, depth, width), i16),
        pltpu.VMEM((SUB, depth), f32),
        pltpu.VMEM((2, others, SUB, depth), f32),
        pltpu.VMEM((2, others, depth, width), i16),
        pltpu.VMEM((2, others, depth, width), i16),
        pltpu.VMEM((2, SUB, depth), f32),
        pltpu.VMEM((2, others, SUB, depth), f32),
        pltpu.VMEM((2, depth, width), f32),
    ]


SQUARE_STEPS = 3


def sum_square(wires, at, part, out, by_col, by_row, mine):
    rows, cols = lax.axis_size("rows"), lax.axis_size("cols")
    row, col = lax.axis_index("rows"), lax.axis_index("cols")
    share = part.shape[0] // cols
    x, core = col // 2, lax.rem(col, 2)
    z, y = row // RING, lax.rem(row, RING)

    def span(at):
        return pl.ds(at * share, share)

    far = {0: 0, 1: 1, 2: 2, 3: 1}
    col_peers = [
        shifted(x, o) * 2 + lax.rem(core + c, 2)
        for o, c in ((2, 0), (2, 1), (1, 0), (3, 0), (1, 1), (3, 1), (0, 1))
    ]
    steps = [(a, b) for a in range(RING) for b in range(RING) if a or b]
    row_peers = [
        shifted(z, a) * RING + shifted(y, b)
        for a, b in sorted(steps, key=lambda step: -far[step[0]] - far[step[1]])
    ]
    for peer in col_peers:
        wires.start(part.at[span(peer)], by_col.at[col], (row, peer), at)
    by_col[col] = part[span(col)]
    arrived(by_col.at[pl.ds(0, cols - 1)], wires.recv.at[at])
    mine[...] = jnp.sum(by_col[...], axis=0)
    for peer in row_peers:
        wires.start(mine, by_row.at[row], (peer, col), at + 1)
    by_row[row] = mine[...]
    arrived(by_row.at[pl.ds(0, rows - 1)], wires.recv.at[at + 1])
    out[span(col)] = jnp.sum(by_row[...], axis=0)
    for peer in col_peers:
        wires.start(out.at[span(col)], out.at[span(col)], (row, peer), at + 2)
    arrived(out.at[pl.ds(0, (cols - 1) * share)], wires.recv.at[at + 2])
    wires.drain(
        by_col.at[pl.ds(0, cols - 1)],
        by_row.at[pl.ds(0, rows - 1)],
        out.at[pl.ds(0, (cols - 1) * share)],
    )


def square_rooms(order, rows, cols):
    share = order // cols
    return [
        pltpu.VMEM((cols, share, order), jnp.float32),
        pltpu.VMEM((rows, share, order), jnp.float32),
        pltpu.VMEM((share, order), jnp.float32),
    ]


def all_peers():
    rows, cols = lax.axis_size("rows"), lax.axis_size("cols")
    row, col = lax.axis_index("rows"), lax.axis_index("cols")
    return [(lax.rem(row + o, rows), col) for o in range(1, rows)] + [
        (row, lax.rem(col + o, cols)) for o in range(1, cols)
    ]


GROUP = 16


def local_column(column):
    row = lax.axis_index("rows")
    panel, half = column // 16, lax.rem(column, 2)
    along_z = lax.rem(panel // RING + RING - row // RING, RING)
    along_y = lax.rem(lax.rem(panel, RING) + RING - lax.rem(row, RING), RING)
    first = jnp.where(half == 0, along_y, along_z)
    second = jnp.where(half == 0, along_z, along_y)
    return (half * RING + first) * RING + second


def products_kernel(transposed, count_ref, row_ref, col_ref, panels, tiles, out):
    count = count_ref[0, 0]
    out[...] = jnp.zeros_like(out)

    def step(group, carry):
        slots = [group * GROUP + u for u in range(GROUP)]
        rows = [row_ref[0, 0, slot] for slot in slots]
        cols = [local_column(col_ref[0, 0, slot]) for slot in slots]
        if transposed:
            terms = [
                jnp.dot(panels[r], tiles[slot], preferred_element_type=jnp.float32)
                for r, slot in zip(rows, slots)
            ]
        else:
            terms = [
                jnp.dot(tiles[slot], panels[c], preferred_element_type=jnp.float32)
                for c, slot in zip(cols, slots)
            ]
        for slot, term, place in zip(slots, terms, cols if transposed else rows):
            out[place] += jnp.where(slot < count, term, 0.0)
        return carry

    lax.fori_loop(0, (count + GROUP - 1) // GROUP, step, 0)


def products(transposed, out_shape, count, rows, cols, panels, tiles):
    return pl.pallas_call(
        functools.partial(products_kernel, transposed),
        out_shape=jax.ShapeDtypeStruct(out_shape, jnp.float32),
        in_specs=[VMEM, SMEM, SMEM, VMEM, VMEM],
        out_specs=VMEM,
        compiler_params=pltpu.CompilerParams(vmem_limit_bytes=32 << 20),
    )(count, rows, cols, panels, tiles)


def factor(gram, upper_ref, inverse_ref):
    order = gram.shape[0]
    lead = gram
    tail = (
        lax.broadcasted_iota(jnp.int32, (order, order), 0)
        == lax.broadcasted_iota(jnp.int32, (order, order), 1)
    ).astype(jnp.float32)
    for base in range(0, order, SUB):
        left = order - base
        columns = [
            jnp.broadcast_to(lead[:, base + k : base + k + 1], (left, order)) for k in range(SUB)
        ]
        position = lax.broadcasted_iota(jnp.int32, (left, order), 0)
        top = lax.broadcasted_iota(jnp.int32, (SUB, order), 0)
        lane = lax.broadcasted_iota(jnp.int32, (SUB, order), 1)
        pivots = jnp.zeros((SUB, order), jnp.float32)
        for k in range(SUB):
            pivot = columns[k][k : k + 1, :]
            pivots = jnp.where(top == k, pivot, pivots)
            ratio = jnp.where(position > k, columns[k] * (1.0 / pivot), 0.0)
            lead = lead - ratio * lead[k : k + 1, :]
            tail = tail - ratio * tail[k : k + 1, :]
            for j in range(k + 1, SUB):
                columns[j] = columns[j] - ratio * columns[j][k : k + 1, :]
        scale = 1.0 / jnp.sqrt(pivots)
        upper_ref[base : base + SUB, :] = jnp.where(lane >= base + top, lead[:SUB] * scale, 0.0)
        inverse_ref[base : base + SUB, :] = tail[:SUB] * scale
        lead = lead[SUB:]
        tail = tail[SUB:]


def inner(x_ref, out):
    out[...] = matmul(x_ref[0], x_ref[0], NT) + matmul(x_ref[1], x_ref[1], NT)


def basis_kernel(
    root, part, basis_ref, triangle_ref, spread_ref, x_ref, square, gram, inverse, *rest
):
    rooms, (by_col, by_row, mine, send, recv, send2) = rest[:11], rest[11:]
    plane = Plane()
    wires = Wires(send, recv)
    row, cols = lax.axis_index("rows"), lax.axis_size("cols")
    peers = plane.neighbours() + [
        (row, lax.rem(plane.col + o, cols)) for o in range(1, cols)
    ]
    scatter_sum(plane, wires, peers, part, x_ref, *rooms)
    inner(x_ref, square)
    wires.send = send2
    sum_square(wires, SCATTER_STEPS, square, gram, by_col, by_row, mine)
    factor(gram[...], triangle_ref, inverse)
    width = x_ref.shape[2]
    for s in range(2):
        basis_ref[s * width : (s + 1) * width, :] = matmul(inverse[...], x_ref[s], NN).T * root
    triangle_ref[...] = triangle_ref[...] / root
    order = gram.shape[0]
    diagonal = lax.broadcasted_iota(jnp.int32, (order, order), 0) == lax.broadcasted_iota(
        jnp.int32, (order, order), 1
    )
    lengths = jnp.sum(jnp.where(diagonal, gram[...], 0.0), axis=0, keepdims=True)
    inverses = jnp.sum(inverse[...] * inverse[...], axis=0, keepdims=True)
    spread = jnp.sum(lengths * inverses, axis=1, keepdims=True)
    spread_ref[0, 0] = spread[0, 0]
    wires.send = send
    early, hop, code, got, line, lines, code2, got2, line2, lines2, own = rooms
    wires.drain(hop, got, got2, lines, lines2)


def orthonormalize(root, part):
    _, depth, width = part.shape
    rows, cols = lax.axis_size("rows"), lax.axis_size("cols")
    f32 = jnp.float32
    square = pltpu.VMEM((depth, depth), f32)
    return pl.pallas_call(
        functools.partial(basis_kernel, root),
        out_shape=[
            jax.ShapeDtypeStruct((2 * width, depth), f32),
            jax.ShapeDtypeStruct((depth, depth), f32),
            jax.ShapeDtypeStruct((1, 1), f32),
        ],
        in_specs=[VMEM],
        out_specs=[VMEM, VMEM, SMEM],
        scratch_shapes=[pltpu.VMEM((2, depth, width), f32)]
        + [square] * 3
        + scatter_rooms(depth, width)
        + square_rooms(depth, rows, cols)
        + [
            pltpu.SemaphoreType.DMA,
            pltpu.SemaphoreType.DMA((SCATTER_STEPS + SQUARE_STEPS,)),
            pltpu.SemaphoreType.DMA,
        ],
        compiler_params=pltpu.CompilerParams(
            collective_id=2, has_side_effects=True, vmem_limit_bytes=40 << 20
        ),
    )(part)


def again_kernel(
    root, basis_in, triangle_in, basis_ref, triangle_ref, x, square, gram, upper, inverse, *rest
):
    by_col, by_row, mine, send, recv = rest
    wires = Wires(send, recv)
    greet(all_peers())
    x[...] = basis_in[...].T / root
    square[...] = matmul(x[...], x[...], NT)
    sum_square(wires, 0, square, gram, by_col, by_row, mine)
    factor(gram[...], upper, inverse)
    basis_ref[...] = matmul(inverse[...], x[...], NN).T * root
    triangle_ref[...] = matmul(upper[...], triangle_in[...], NN)


def second_pass(root, basis, triangle):
    size, depth = basis.shape
    f32 = jnp.float32
    return pl.pallas_call(
        functools.partial(again_kernel, root),
        out_shape=[
            jax.ShapeDtypeStruct(basis.shape, f32),
            jax.ShapeDtypeStruct(triangle.shape, f32),
        ],
        in_specs=[VMEM] * 2,
        out_specs=[VMEM] * 2,
        scratch_shapes=[pltpu.VMEM((depth, size), f32)]
        + [pltpu.VMEM((depth, depth), f32)] * 4
        + square_rooms(depth, lax.axis_size("rows"), lax.axis_size("cols"))
        + [pltpu.SemaphoreType.DMA, pltpu.SemaphoreType.DMA((SQUARE_STEPS,))],
        compiler_params=pltpu.CompilerParams(
            collective_id=3, has_side_effects=True, vmem_limit_bytes=32 << 20
        ),
    )(basis, triangle)


def body(start_basis, block_values, slot_count, slot_row, slot_col):
    depth = start_basis.shape[1]
    width = block_values.shape[-1]
    panel_blocks = start_basis.shape[0] // width
    rows, cols = lax.axis_size("rows"), lax.axis_size("cols")
    column_blocks = rows * panel_blocks // cols
    held = [
        pltpu.with_memory_space_constraint(array, pltpu.HBM)
        for array in (
            start_basis.reshape(panel_blocks, width, depth),
            block_values.reshape(block_values.shape[2:]),
            slot_row,
            slot_col,
        )
    ]
    basis_parts, tiles, *indices = gather(*held[:2], held[2:], rows)
    image_part = products(
        False,
        (panel_blocks, width, depth),
        slot_count,
        *indices,
        basis_parts.reshape(column_blocks, width, depth),
        tiles,
    )
    image = sum_image(image_part)
    back_part = products(
        True, (column_blocks, depth, width), slot_count, *indices, image, tiles
    )
    root = float(rows * panel_blocks * width) ** 0.5
    basis, triangle, spread = orthonormalize(root, back_part)
    return lax.cond(
        spread[0, 0] <= 2.0 * depth,
        lambda basis, triangle: (basis, triangle),
        functools.partial(second_pass, root),
        basis,
        triangle,
    )


def solution(mesh):
    return jax.shard_map(
        body,
        mesh=mesh,
        in_specs=(
            P("rows", None),
            P("rows", "cols", None, None, None),
            P("rows", "cols"),
            P("rows", "cols", None),
            P("rows", "cols", None),
        ),
        out_specs=(P(("rows", "cols"), None), P()),
        check_vma=False,
    )
```

```python
import functools

import jax
import jax.numpy as jnp
from jax import lax
from jax.experimental import pallas as pl
from jax.experimental.pallas import tpu as pltpu
from jax.sharding import PartitionSpec as P

SUB = 8
RING = 4
TOP = 32000.0
LEAST = 1e-33
VMEM = pl.BlockSpec(memory_space=pltpu.VMEM)
SMEM = pl.BlockSpec(memory_space=pltpu.SMEM)
HBM = pl.BlockSpec(memory_space=pltpu.HBM)
NN = (((1,), (0,)), ((), ()))
NT = (((1,), (1,)), ((), ()))


def matmul(a, b, dims):
    return lax.dot_general(
        a, b, dims, precision=lax.Precision.HIGHEST, preferred_element_type=jnp.float32
    )


class Wires:
    def __init__(self, send, recv):
        self.send, self.recv, self.used = send, recv, 0

    def start(self, src, dst, device, at=None):
        if at is None:
            at = self.used
            self.used += 1
        copy = pltpu.make_async_remote_copy(
            src_ref=src,
            dst_ref=dst,
            send_sem=self.send,
            recv_sem=self.recv.at[at],
            device_id=device,
            device_id_type=pl.DeviceIdType.MESH,
        )
        copy.start()
        return copy

    def drain(self, *refs):
        for ref in refs:
            pltpu.make_async_copy(ref, ref, self.send).wait()


def announce(peers):
    barrier = pltpu.get_barrier_semaphore()
    for peer in peers:
        pl.semaphore_signal(
            barrier, inc=1, device_id=peer, device_id_type=pl.DeviceIdType.MESH
        )


def greet(peers):
    announce(peers)
    pl.semaphore_wait(pltpu.get_barrier_semaphore(), len(peers))


def arrived(ref, sem):
    pltpu.make_async_copy(ref, ref, sem).wait()


def encode(value, inverse):
    return jnp.round(value * inverse).astype(jnp.int32).astype(jnp.int16)


def decode(code, unit):
    return code.astype(jnp.int32).astype(jnp.float32) * unit


def shifted(at, offset):
    return lax.rem(at + offset % RING, RING)


class Plane:
    def __init__(self):
        row = lax.axis_index("rows")
        self.col = lax.axis_index("cols")
        self.z, self.y = row // RING, lax.rem(row, RING)

    def row(self, half, first, second):
        along_y, along_z = (first, second) if half == 0 else (second, first)
        return shifted(self.z, along_z) * RING + shifted(self.y, along_y)

    def device(self, half, first, second):
        return (self.row(half, first, second), self.col)

    def neighbours(self):
        return [self.device(0, o, 0) for o in (2, 1, 3)] + [self.device(0, 0, o) for o in (2, 1, 3)]


GATHER_COPIES = 38


def gather_kernel(
    basis, values, rows, cols, out, tiles, rows_out, cols_out, send, recv, local
):
    plane = Plane()
    wires = Wires(send, recv)
    load = pltpu.make_async_copy(basis.at[pl.ds(plane.col * 2, 2)], out.at[:, 0, 0], local.at[0])
    load.start()
    kept = [
        pltpu.make_async_copy(src, dst, local.at[1 + at])
        for at, (src, dst) in enumerate(
            ((values, tiles), (rows, rows_out), (cols, cols_out))
        )
    ]
    for copy in kept:
        copy.start()
    greet(plane.neighbours())
    load.wait()
    cut = out.shape[3] // 2
    upper, lower = pl.ds(0, cut), pl.ds(cut, cut)
    near, rest, ends = {}, {}, []
    for o in (1, 3, 2):
        for h in (0, 1):
            near[h, o] = wires.start(
                out.at[h, 0, 0], out.at[h, RING - o, 0], plane.device(h, o, 0)
            )
    for o in (1, 3):
        for h in (0, 1):
            rest[h, 0, o] = wires.start(
                out.at[h, 0, 0], out.at[h, 0, RING - o], plane.device(h, 0, o)
            )
    for f in (3, 1, 2):
        for h in (0, 1):
            near[h, RING - f].wait_recv()
            for o in (1, 3):
                rest[h, f, o] = wires.start(
                    out.at[h, f, 0], out.at[h, f, RING - o], plane.device(h, 0, o)
                )
    for f in (0, 3, 1, 2):
        for o, piece in ((1, upper), (3, lower)):
            for h in (0, 1):
                rest[h, f, o].wait_recv()
                ends.append(
                    wires.start(
                        out.at[h, f, RING - o, piece], out.at[h, f, 2, piece], plane.device(h, 0, o)
                    )
                )
    for copy in ends:
        copy.wait_recv()
    for copy in kept:
        copy.wait()
    wires.drain(out.at[0], out.at[1, pl.ds(0, 3)], out.at[1, 3, pl.ds(0, 2)])


def gather(basis, values, indices, rows):
    return pl.pallas_call(
        gather_kernel,
        out_shape=[
            jax.ShapeDtypeStruct((2, rows // RING, RING) + basis.shape[1:], basis.dtype),
            jax.ShapeDtypeStruct(values.shape, values.dtype),
        ]
        + [jax.ShapeDtypeStruct(index.shape, index.dtype) for index in indices],
        in_specs=[HBM] * 4,
        out_specs=[VMEM] * 2 + [SMEM] * 2,
        scratch_shapes=[
            pltpu.SemaphoreType.DMA,
            pltpu.SemaphoreType.DMA((GATHER_COPIES,)),
            pltpu.SemaphoreType.DMA((4,)),
        ],
        compiler_params=pltpu.CompilerParams(
            collective_id=0, has_side_effects=True, vmem_limit_bytes=44 << 20
        ),
    )(basis, values, *indices)


IMAGE_COPIES = 24


def image_kernel(
    part, image, sibling, total, code, unit, got, units, send, recv, send2, send3
):
    row, col = lax.axis_index("rows"), lax.axis_index("cols")
    x, core = col // 2, lax.rem(col, 2)
    twin = (row, x * 2 + 1 - core)
    peer = {o: (row, shifted(x, o) * 2 + core) for o in (1, 2, 3)}
    wires = Wires(send, recv)
    greet([twin, peer[1], peer[2], peer[3]])
    sub = image.shape[0] // 8

    def chunk(offset, which):
        return pl.ds((shifted(x, offset) * 2 + which) * sub, sub)

    order = (2, 1, 3, 0)
    swap = {
        o: wires.start(part.at[chunk(o, 1 - core)], sibling.at[o], twin) for o in order
    }
    wires.send = send2
    coded, scaled = {}, {}
    for o in order:
        swap[o].wait_recv()
        whole = part[chunk(o, core)] + sibling[o]
        if o == 0:
            total[...] = whole
            continue
        most = jnp.max(jnp.max(jnp.abs(whole), axis=0), axis=0, keepdims=True)
        step = jnp.maximum(most, LEAST) * (1.0 / TOP)
        unit[o - 1] = jnp.broadcast_to(step, unit.shape[1:])
        code[o - 1] = encode(whole, (1.0 / step)[None])
        scaled[o] = wires.start(unit.at[o - 1], units.at[o - 1], peer[o])
        coded[o, 0] = wires.start(code.at[o - 1, 0], got.at[o - 1, 0], peer[o])
    for o in (2, 1, 3):
        coded[o, 1] = wires.start(code.at[o - 1, 1], got.at[o - 1, 1], peer[o])
    for o in (1, 3, 2):
        scaled[o].wait_recv()
    wires.send = send3
    mine = (x * 2 + core) * sub
    sends = []
    for b in range(2):
        value = total[b]
        for o in (1, 3, 2):
            coded[o, b].wait_recv()
            value = value + decode(got[o - 1, b], units[o - 1, 0:1])
        image[mine + b] = value.T.astype(image.dtype)
        block = image.at[mine + b]
        sends.append({o: wires.start(block, block, peer[o]) for o in (2, 1, 3)})
    both = image.at[pl.ds(mine, sub)]
    last = [wires.start(both, both, twin)]
    for o in (1, 3, 2):
        for b in (0, 1):
            sends[b][o].wait_recv()
        pair = image.at[pl.ds((shifted(x, RING - o) * 2 + core) * sub, sub)]
        last.append(wires.start(pair, pair, twin))
    for copy in last:
        copy.wait_recv()
    wires.drain(image.at[pl.ds(0, 14)])
    wires.send = send2
    wires.drain(got, units)
    wires.send = send
    wires.drain(part.at[pl.ds(0, 8)])


def sum_image(part):
    blocks, width, depth = part.shape
    f32 = jnp.float32
    return pl.pallas_call(
        image_kernel,
        out_shape=jax.ShapeDtypeStruct((blocks, depth, width), jnp.bfloat16),
        in_specs=[VMEM],
        out_specs=VMEM,
        scratch_shapes=[
            pltpu.VMEM((RING, 2, width, depth), f32),
            pltpu.VMEM((2, width, depth), f32),
            pltpu.VMEM((RING - 1, 2, width, depth), jnp.int16),
            pltpu.VMEM((RING - 1, SUB, depth), f32),
            pltpu.VMEM((RING - 1, 2, width, depth), jnp.int16),
            pltpu.VMEM((RING - 1, SUB, depth), f32),
            pltpu.SemaphoreType.DMA,
            pltpu.SemaphoreType.DMA((IMAGE_COPIES,)),
            pltpu.SemaphoreType.DMA,
            pltpu.SemaphoreType.DMA,
        ],
        compiler_params=pltpu.CompilerParams(
            collective_id=1, has_side_effects=True, vmem_limit_bytes=32 << 20
        ),
    )(part)


SCATTER_STEPS = 22


def tile_of(row):
    return jnp.broadcast_to(row, (row.shape[1], row.shape[1])).T


def scatter_sum(plane, wires, peers, part, out, early, hop, code, got, line, lines, code2, got2, line2, lines2, own):
    others = (2, 1, 3)
    order = (2, 3, 1, 0)

    def block(h, first, second):
        return (h * RING + first) * RING + second

    def column(tile):
        return jnp.concatenate([tile, tile], axis=1)

    announce(peers)
    most = lax.fori_loop(
        0,
        part.shape[0],
        lambda at, most: jnp.maximum(most, jnp.abs(part[at])),
        jnp.zeros(part.shape[1:], jnp.float32),
    )
    most = jnp.broadcast_to(jnp.max(most, axis=1, keepdims=True), line.shape[1:] * 2)
    unit = jnp.maximum(most, LEAST) * (1.0 / TOP)
    line[...] = unit.T[:SUB]
    inverse = column(1.0 / unit)
    pl.semaphore_wait(pltpu.get_barrier_semaphore(), len(peers))
    for h in (0, 1):
        for o in others:
            wires.start(line, lines.at[h, o - 1], plane.device(h, o, 0), h)
    way = {2: 0, 1: 0, 3: 1, 0: 1}
    offset = (1, 3)
    for at, s in enumerate(order):
        for h in (0, 1):
            early[h, s] = encode(part[block(h, 2, s)], inverse)
            wires.start(
                early.at[h, s], hop.at[h, s], plane.device(h, offset[way[s]], 0), 14 + 2 * at + h
            )
    for at, s in enumerate(order):
        w = 1 - way[s]
        for h in (0, 1):
            code[h, s, w] = encode(part[block(h, offset[w], s)], inverse)
            wires.start(
                code.at[h, s, w], got.at[h, s, w], plane.device(h, offset[w], 0), 2 + 2 * at + h
            )
    units, sums = {}, {}
    for h in (0, 1):
        arrived(lines.at[h], wires.recv.at[h])
        units[h] = [tile_of(lines[h, k, 0:1]) for k in range(RING - 1)]
        sums[h] = unit + (units[h][0] + units[h][1] + units[h][2])
        line2[h] = line[...] + (lines[h, 0] + lines[h, 1] + lines[h, 2])
        for s in others:
            wires.start(line2.at[h], lines2.at[h, s - 1], plane.device(h, 0, s), 10 + h)
    for at, s in enumerate(order):
        w = way[s]
        for h in (0, 1):
            near = units[h][offset[w] - 1]
            arrived(hop.at[h, s], wires.recv.at[14 + 2 * at + h])
            merged = part[block(h, offset[w], s)] + decode(hop[h, s], column(near))
            code[h, s, w] = encode(merged, column(1.0 / (unit + near)))
            wires.start(
                code.at[h, s, w], got.at[h, s, w], plane.device(h, offset[w], 0), 2 + 2 * at + h
            )
    for at, s in enumerate(order):
        w = way[s]
        for h in (0, 1):
            arrived(got.at[h, s], wires.recv.at[2 + 2 * at + h])
            both = units[h][offset[w] - 1] + units[h][1]
            total = part[block(h, 0, s)] + decode(got[h, s, w], column(both))
            total = total + decode(got[h, s, 1 - w], column(units[h][offset[1 - w] - 1]))
            if s == 0:
                own[h] = total
            else:
                code2[h, s - 1] = encode(total, column(1.0 / sums[h]))
                wires.start(
                    code2.at[h, s - 1], got2.at[h, s - 1], plane.device(h, 0, s), 12 + h
                )
    last = {}
    for h in (0, 1):
        arrived(lines2.at[h], wires.recv.at[10 + h])
        last[h] = [tile_of(lines2[h, k, 0:1]) for k in range(RING - 1)]
    for h in (0, 1):
        arrived(got2.at[h], wires.recv.at[12 + h])
        total = own[h]
        for k in range(RING - 1):
            total = total + decode(got2[h, k], column(last[h][k]))
        out[h] = total


def scatter_rooms(depth, width):
    f32 = jnp.float32
    i16 = jnp.int16
    others = RING - 1
    return [
        pltpu.VMEM((2, RING, depth, width), i16),
        pltpu.VMEM((2, RING, depth, width), i16),
        pltpu.VMEM((2, RING, 2, depth, width), i16),
        pltpu.VMEM((2, RING, 2, depth, width), i16),
        pltpu.VMEM((SUB, depth), f32),
        pltpu.VMEM((2, others, SUB, depth), f32),
        pltpu.VMEM((2, others, depth, width), i16),
        pltpu.VMEM((2, others, depth, width), i16),
        pltpu.VMEM((2, SUB, depth), f32),
        pltpu.VMEM((2, others, SUB, depth), f32),
        pltpu.VMEM((2, depth, width), f32),
    ]


SQUARE_STEPS = 3


def sum_square(wires, at, part, out, by_col, by_row, mine):
    rows, cols = lax.axis_size("rows"), lax.axis_size("cols")
    row, col = lax.axis_index("rows"), lax.axis_index("cols")
    share = part.shape[0] // cols
    x, core = col // 2, lax.rem(col, 2)
    z, y = row // RING, lax.rem(row, RING)

    def span(at):
        return pl.ds(at * share, share)

    far = {0: 0, 1: 1, 2: 2, 3: 1}
    col_peers = [
        shifted(x, o) * 2 + lax.rem(core + c, 2)
        for o, c in ((2, 0), (2, 1), (1, 0), (3, 0), (1, 1), (3, 1), (0, 1))
    ]
    steps = [(a, b) for a in range(RING) for b in range(RING) if a or b]
    row_peers = [
        shifted(z, a) * RING + shifted(y, b)
        for a, b in sorted(steps, key=lambda step: -far[step[0]] - far[step[1]])
    ]
    for peer in col_peers:
        wires.start(part.at[span(peer)], by_col.at[col], (row, peer), at)
    by_col[col] = part[span(col)]
    arrived(by_col.at[pl.ds(0, cols - 1)], wires.recv.at[at])
    mine[...] = jnp.sum(by_col[...], axis=0)
    for peer in row_peers:
        wires.start(mine, by_row.at[row], (peer, col), at + 1)
    by_row[row] = mine[...]
    arrived(by_row.at[pl.ds(0, rows - 1)], wires.recv.at[at + 1])
    out[span(col)] = jnp.sum(by_row[...], axis=0)
    for peer in col_peers:
        wires.start(out.at[span(col)], out.at[span(col)], (row, peer), at + 2)
    arrived(out.at[pl.ds(0, (cols - 1) * share)], wires.recv.at[at + 2])
    wires.drain(
        by_col.at[pl.ds(0, cols - 1)],
        by_row.at[pl.ds(0, rows - 1)],
        out.at[pl.ds(0, (cols - 1) * share)],
    )


def square_rooms(order, rows, cols):
    share = order // cols
    return [
        pltpu.VMEM((cols, share, order), jnp.float32),
        pltpu.VMEM((rows, share, order), jnp.float32),
        pltpu.VMEM((share, order), jnp.float32),
    ]


def all_peers():
    rows, cols = lax.axis_size("rows"), lax.axis_size("cols")
    row, col = lax.axis_index("rows"), lax.axis_index("cols")
    return [(lax.rem(row + o, rows), col) for o in range(1, rows)] + [
        (row, lax.rem(col + o, cols)) for o in range(1, cols)
    ]


GROUP = 16


def local_column(column):
    row = lax.axis_index("rows")
    panel, half = column // 16, lax.rem(column, 2)
    along_z = lax.rem(panel // RING + RING - row // RING, RING)
    along_y = lax.rem(lax.rem(panel, RING) + RING - lax.rem(row, RING), RING)
    first = jnp.where(half == 0, along_y, along_z)
    second = jnp.where(half == 0, along_z, along_y)
    return (half * RING + first) * RING + second


def products_kernel(transposed, count_ref, row_ref, col_ref, panels, tiles, out):
    count = count_ref[0, 0]
    out[...] = jnp.zeros_like(out)

    def step(group, carry):
        slots = [group * GROUP + u for u in range(GROUP)]
        rows = [row_ref[0, 0, slot] for slot in slots]
        cols = [local_column(col_ref[0, 0, slot]) for slot in slots]
        if transposed:
            terms = [
                jnp.dot(panels[r], tiles[slot], preferred_element_type=jnp.float32)
                for r, slot in zip(rows, slots)
            ]
        else:
            terms = [
                jnp.dot(tiles[slot], panels[c], preferred_element_type=jnp.float32)
                for c, slot in zip(cols, slots)
            ]
        for slot, term, place in zip(slots, terms, cols if transposed else rows):
            out[place] += jnp.where(slot < count, term, 0.0)
        return carry

    lax.fori_loop(0, (count + GROUP - 1) // GROUP, step, 0)


def products(transposed, out_shape, count, rows, cols, panels, tiles):
    return pl.pallas_call(
        functools.partial(products_kernel, transposed),
        out_shape=jax.ShapeDtypeStruct(out_shape, jnp.float32),
        in_specs=[VMEM, SMEM, SMEM, VMEM, VMEM],
        out_specs=VMEM,
        compiler_params=pltpu.CompilerParams(vmem_limit_bytes=32 << 20),
    )(count, rows, cols, panels, tiles)


def factor(gram, upper_ref, inverse_ref):
    order = gram.shape[0]
    lead = gram
    tail = (
        lax.broadcasted_iota(jnp.int32, (order, order), 0)
        == lax.broadcasted_iota(jnp.int32, (order, order), 1)
    ).astype(jnp.float32)
    for base in range(0, order, SUB):
        left = order - base
        columns = [
            jnp.broadcast_to(lead[:, base + k : base + k + 1], (left, order)) for k in range(SUB)
        ]
        position = lax.broadcasted_iota(jnp.int32, (left, order), 0)
        top = lax.broadcasted_iota(jnp.int32, (SUB, order), 0)
        lane = lax.broadcasted_iota(jnp.int32, (SUB, order), 1)
        pivots = jnp.zeros((SUB, order), jnp.float32)
        for k in range(SUB):
            pivot = columns[k][k : k + 1, :]
            pivots = jnp.where(top == k, pivot, pivots)
            ratio = jnp.where(position > k, columns[k], 0.0) * (1.0 / pivot)
            lead = lead - ratio * lead[k : k + 1, :]
            tail = tail - ratio * tail[k : k + 1, :]
            for j in range(k + 1, SUB):
                columns[j] = columns[j] - ratio * columns[j][k : k + 1, :]
        scale = 1.0 / jnp.sqrt(pivots)
        upper_ref[base : base + SUB, :] = jnp.where(lane >= base + top, lead[:SUB] * scale, 0.0)
        inverse_ref[base : base + SUB, :] = tail[:SUB] * scale
        lead = lead[SUB:]
        tail = tail[SUB:]


def inner(x_ref, out):
    out[...] = matmul(x_ref[0], x_ref[0], NT) + matmul(x_ref[1], x_ref[1], NT)


def basis_kernel(
    root, part, basis_ref, triangle_ref, spread_ref, x_ref, square, gram, inverse, *rest
):
    rooms, (by_col, by_row, mine, send, recv, send2) = rest[:11], rest[11:]
    plane = Plane()
    wires = Wires(send, recv)
    row, cols = lax.axis_index("rows"), lax.axis_size("cols")
    peers = plane.neighbours() + [
        (row, lax.rem(plane.col + o, cols)) for o in range(1, cols)
    ]
    scatter_sum(plane, wires, peers, part, x_ref, *rooms)
    inner(x_ref, square)
    wires.send = send2
    sum_square(wires, SCATTER_STEPS, square, gram, by_col, by_row, mine)
    factor(gram[...], triangle_ref, inverse)
    width = x_ref.shape[2]
    for s in range(2):
        basis_ref[s * width : (s + 1) * width, :] = matmul(inverse[...], x_ref[s], NN).T * root
    triangle_ref[...] = triangle_ref[...] / root
    order = gram.shape[0]
    diagonal = lax.broadcasted_iota(jnp.int32, (order, order), 0) == lax.broadcasted_iota(
        jnp.int32, (order, order), 1
    )
    lengths = jnp.sum(jnp.where(diagonal, gram[...], 0.0), axis=0, keepdims=True)
    inverses = jnp.sum(inverse[...] * inverse[...], axis=0, keepdims=True)
    spread = jnp.sum(lengths * inverses, axis=1, keepdims=True)
    spread_ref[0, 0] = spread[0, 0]
    wires.send = send
    early, hop, code, got, line, lines, code2, got2, line2, lines2, own = rooms
    wires.drain(hop, got, got2, lines, lines2)


def orthonormalize(root, part):
    _, depth, width = part.shape
    rows, cols = lax.axis_size("rows"), lax.axis_size("cols")
    f32 = jnp.float32
    square = pltpu.VMEM((depth, depth), f32)
    return pl.pallas_call(
        functools.partial(basis_kernel, root),
        out_shape=[
            jax.ShapeDtypeStruct((2 * width, depth), f32),
            jax.ShapeDtypeStruct((depth, depth), f32),
            jax.ShapeDtypeStruct((1, 1), f32),
        ],
        in_specs=[VMEM],
        out_specs=[VMEM, VMEM, SMEM],
        scratch_shapes=[pltpu.VMEM((2, depth, width), f32)]
        + [square] * 3
        + scatter_rooms(depth, width)
        + square_rooms(depth, rows, cols)
        + [
            pltpu.SemaphoreType.DMA,
            pltpu.SemaphoreType.DMA((SCATTER_STEPS + SQUARE_STEPS,)),
            pltpu.SemaphoreType.DMA,
        ],
        compiler_params=pltpu.CompilerParams(
            collective_id=2, has_side_effects=True, vmem_limit_bytes=40 << 20
        ),
    )(part)


def again_kernel(
    root, basis_in, triangle_in, basis_ref, triangle_ref, x, square, gram, upper, inverse, *rest
):
    by_col, by_row, mine, send, recv = rest
    wires = Wires(send, recv)
    greet(all_peers())
    x[...] = basis_in[...].T / root
    square[...] = matmul(x[...], x[...], NT)
    sum_square(wires, 0, square, gram, by_col, by_row, mine)
    factor(gram[...], upper, inverse)
    basis_ref[...] = matmul(inverse[...], x[...], NN).T * root
    triangle_ref[...] = matmul(upper[...], triangle_in[...], NN)


def second_pass(root, basis, triangle):
    size, depth = basis.shape
    f32 = jnp.float32
    return pl.pallas_call(
        functools.partial(again_kernel, root),
        out_shape=[
            jax.ShapeDtypeStruct(basis.shape, f32),
            jax.ShapeDtypeStruct(triangle.shape, f32),
        ],
        in_specs=[VMEM] * 2,
        out_specs=[VMEM] * 2,
        scratch_shapes=[pltpu.VMEM((depth, size), f32)]
        + [pltpu.VMEM((depth, depth), f32)] * 4
        + square_rooms(depth, lax.axis_size("rows"), lax.axis_size("cols"))
        + [pltpu.SemaphoreType.DMA, pltpu.SemaphoreType.DMA((SQUARE_STEPS,))],
        compiler_params=pltpu.CompilerParams(
            collective_id=3, has_side_effects=True, vmem_limit_bytes=32 << 20
        ),
    )(basis, triangle)


def body(start_basis, block_values, slot_count, slot_row, slot_col):
    depth = start_basis.shape[1]
    width = block_values.shape[-1]
    panel_blocks = start_basis.shape[0] // width
    rows, cols = lax.axis_size("rows"), lax.axis_size("cols")
    column_blocks = rows * panel_blocks // cols
    held = [
        pltpu.with_memory_space_constraint(array, pltpu.HBM)
        for array in (
            start_basis.reshape(panel_blocks, width, depth),
            block_values.reshape(block_values.shape[2:]),
            slot_row,
            slot_col,
        )
    ]
    basis_parts, tiles, *indices = gather(*held[:2], held[2:], rows)
    image_part = products(
        False,
        (panel_blocks, width, depth),
        slot_count,
        *indices,
        basis_parts.reshape(column_blocks, width, depth),
        tiles,
    )
    image = sum_image(image_part)
    back_part = products(
        True, (column_blocks, depth, width), slot_count, *indices, image, tiles
    )
    root = float(rows * panel_blocks * width) ** 0.5
    basis, triangle, spread = orthonormalize(root, back_part)
    return lax.cond(
        spread[0, 0] <= 2.0 * depth,
        lambda basis, triangle: (basis, triangle),
        functools.partial(second_pass, root),
        basis,
        triangle,
    )


def solution(mesh):
    return jax.shard_map(
        body,
        mesh=mesh,
        in_specs=(
            P("rows", None),
            P("rows", "cols", None, None, None),
            P("rows", "cols"),
            P("rows", "cols", None),
            P("rows", "cols", None),
        ),
        out_specs=(P(("rows", "cols"), None), P()),
        check_vma=False,
    )
```

```python
import functools

import jax
import jax.numpy as jnp
from jax import lax
from jax.experimental import pallas as pl
from jax.experimental.pallas import tpu as pltpu
from jax.sharding import PartitionSpec as P

SUB = 8
RING = 4
TOP = 32000.0
LEAST = 1e-33
VMEM = pl.BlockSpec(memory_space=pltpu.VMEM)
SMEM = pl.BlockSpec(memory_space=pltpu.SMEM)
HBM = pl.BlockSpec(memory_space=pltpu.HBM)
NN = (((1,), (0,)), ((), ()))
NT = (((1,), (1,)), ((), ()))


def matmul(a, b, dims):
    return lax.dot_general(
        a, b, dims, precision=lax.Precision.HIGHEST, preferred_element_type=jnp.float32
    )


class Wires:
    def __init__(self, send, recv):
        self.send, self.recv, self.used = send, recv, 0

    def start(self, src, dst, device, at=None):
        if at is None:
            at = self.used
            self.used += 1
        copy = pltpu.make_async_remote_copy(
            src_ref=src,
            dst_ref=dst,
            send_sem=self.send,
            recv_sem=self.recv.at[at],
            device_id=device,
            device_id_type=pl.DeviceIdType.MESH,
        )
        copy.start()
        return copy

    def drain(self, *refs):
        for ref in refs:
            pltpu.make_async_copy(ref, ref, self.send).wait()


def announce(peers):
    barrier = pltpu.get_barrier_semaphore()
    for peer in peers:
        pl.semaphore_signal(
            barrier, inc=1, device_id=peer, device_id_type=pl.DeviceIdType.MESH
        )


def greet(peers):
    announce(peers)
    pl.semaphore_wait(pltpu.get_barrier_semaphore(), len(peers))


def arrived(ref, sem):
    pltpu.make_async_copy(ref, ref, sem).wait()


def encode(value, inverse):
    return jnp.round(value * inverse).astype(jnp.int32).astype(jnp.int16)


def decode(code, unit):
    return code.astype(jnp.int32).astype(jnp.float32) * unit


def shifted(at, offset):
    return lax.rem(at + offset % RING, RING)


class Plane:
    def __init__(self):
        row = lax.axis_index("rows")
        self.col = lax.axis_index("cols")
        self.z, self.y = row // RING, lax.rem(row, RING)

    def row(self, half, first, second):
        along_y, along_z = (first, second) if half == 0 else (second, first)
        return shifted(self.z, along_z) * RING + shifted(self.y, along_y)

    def device(self, half, first, second):
        return (self.row(half, first, second), self.col)

    def neighbours(self):
        return [self.device(0, o, 0) for o in (2, 1, 3)] + [self.device(0, 0, o) for o in (2, 1, 3)]


GATHER_COPIES = 38


def gather_kernel(
    basis, values, rows, cols, out, tiles, rows_out, cols_out, send, recv, local
):
    plane = Plane()
    wires = Wires(send, recv)
    load = pltpu.make_async_copy(basis.at[pl.ds(plane.col * 2, 2)], out.at[:, 0, 0], local.at[0])
    load.start()
    kept = [
        pltpu.make_async_copy(src, dst, local.at[1 + at])
        for at, (src, dst) in enumerate(
            ((values, tiles), (rows, rows_out), (cols, cols_out))
        )
    ]
    for copy in kept:
        copy.start()
    greet(plane.neighbours())
    load.wait()
    cut = out.shape[3] // 2
    upper, lower = pl.ds(0, cut), pl.ds(cut, cut)
    near, rest, ends = {}, {}, []
    for o in (1, 3, 2):
        for h in (0, 1):
            near[h, o] = wires.start(
                out.at[h, 0, 0], out.at[h, RING - o, 0], plane.device(h, o, 0)
            )
    for o in (1, 3):
        for h in (0, 1):
            rest[h, 0, o] = wires.start(
                out.at[h, 0, 0], out.at[h, 0, RING - o], plane.device(h, 0, o)
            )
    for f in (3, 1, 2):
        for h in (0, 1):
            near[h, RING - f].wait_recv()
            for o in (1, 3):
                rest[h, f, o] = wires.start(
                    out.at[h, f, 0], out.at[h, f, RING - o], plane.device(h, 0, o)
                )
    for f in (0, 3, 1, 2):
        for o, piece in ((1, upper), (3, lower)):
            for h in (0, 1):
                rest[h, f, o].wait_recv()
                ends.append(
                    wires.start(
                        out.at[h, f, RING - o, piece], out.at[h, f, 2, piece], plane.device(h, 0, o)
                    )
                )
    for copy in ends:
        copy.wait_recv()
    for copy in kept:
        copy.wait()
    wires.drain(out.at[0], out.at[1, pl.ds(0, 3)], out.at[1, 3, pl.ds(0, 2)])


def gather(basis, values, indices, rows):
    return pl.pallas_call(
        gather_kernel,
        out_shape=[
            jax.ShapeDtypeStruct((2, rows // RING, RING) + basis.shape[1:], basis.dtype),
            jax.ShapeDtypeStruct(values.shape, values.dtype),
        ]
        + [jax.ShapeDtypeStruct(index.shape, index.dtype) for index in indices],
        in_specs=[HBM] * 4,
        out_specs=[VMEM] * 2 + [SMEM] * 2,
        scratch_shapes=[
            pltpu.SemaphoreType.DMA,
            pltpu.SemaphoreType.DMA((GATHER_COPIES,)),
            pltpu.SemaphoreType.DMA((4,)),
        ],
        compiler_params=pltpu.CompilerParams(
            collective_id=0, has_side_effects=True, vmem_limit_bytes=44 << 20
        ),
    )(basis, values, *indices)


IMAGE_COPIES = 24


def image_kernel(
    part, image, sibling, total, code, unit, got, units, send, recv, send2, send3
):
    row, col = lax.axis_index("rows"), lax.axis_index("cols")
    x, core = col // 2, lax.rem(col, 2)
    twin = (row, x * 2 + 1 - core)
    peer = {o: (row, shifted(x, o) * 2 + core) for o in (1, 2, 3)}
    wires = Wires(send, recv)
    greet([twin, peer[1], peer[2], peer[3]])
    sub = image.shape[0] // 8

    def chunk(offset, which):
        return pl.ds((shifted(x, offset) * 2 + which) * sub, sub)

    order = (2, 1, 3, 0)
    swap = {
        o: wires.start(part.at[chunk(o, 1 - core)], sibling.at[o], twin) for o in order
    }
    wires.send = send2
    coded, scaled = {}, {}
    for o in order[:3]:
        swap[o].wait_recv()
        whole = part[chunk(o, core)] + sibling[o]
        most = jnp.max(jnp.max(jnp.abs(whole), axis=0), axis=0, keepdims=True)
        step = jnp.maximum(most, LEAST) * (1.0 / TOP)
        inverse = 1.0 / step
        code[o - 1, 0] = encode(whole[0], inverse)
        coded[o, 0] = wires.start(code.at[o - 1, 0], got.at[o - 1, 0], peer[o])
        unit[o - 1] = jnp.broadcast_to(step, unit.shape[1:])
        scaled[o] = wires.start(unit.at[o - 1], units.at[o - 1], peer[o])
        code[o - 1, 1] = encode(whole[1], inverse)
    for o in (2, 1, 3):
        coded[o, 1] = wires.start(code.at[o - 1, 1], got.at[o - 1, 1], peer[o])
    swap[0].wait_recv()
    total[...] = part[chunk(0, core)] + sibling[0]
    for o in (1, 3, 2):
        scaled[o].wait_recv()
    wires.send = send3
    mine = (x * 2 + core) * sub
    sends = []
    for b in range(2):
        value = total[b]
        for o in (1, 3, 2):
            coded[o, b].wait_recv()
            value = value + decode(got[o - 1, b], units[o - 1, 0:1])
        image[mine + b] = value.T.astype(image.dtype)
        block = image.at[mine + b]
        sends.append({o: wires.start(block, block, peer[o]) for o in (2, 1, 3)})
    both = image.at[pl.ds(mine, sub)]
    last = [wires.start(both, both, twin)]
    for o in (1, 3, 2):
        for b in (0, 1):
            sends[b][o].wait_recv()
        pair = image.at[pl.ds((shifted(x, RING - o) * 2 + core) * sub, sub)]
        last.append(wires.start(pair, pair, twin))
    for copy in last:
        copy.wait_recv()
    wires.drain(image.at[pl.ds(0, 14)])
    wires.send = send2
    wires.drain(got, units)
    wires.send = send
    wires.drain(part.at[pl.ds(0, 8)])


def sum_image(part):
    blocks, width, depth = part.shape
    f32 = jnp.float32
    return pl.pallas_call(
        image_kernel,
        out_shape=jax.ShapeDtypeStruct((blocks, depth, width), jnp.bfloat16),
        in_specs=[VMEM],
        out_specs=VMEM,
        scratch_shapes=[
            pltpu.VMEM((RING, 2, width, depth), f32),
            pltpu.VMEM((2, width, depth), f32),
            pltpu.VMEM((RING - 1, 2, width, depth), jnp.int16),
            pltpu.VMEM((RING - 1, SUB, depth), f32),
            pltpu.VMEM((RING - 1, 2, width, depth), jnp.int16),
            pltpu.VMEM((RING - 1, SUB, depth), f32),
            pltpu.SemaphoreType.DMA,
            pltpu.SemaphoreType.DMA((IMAGE_COPIES,)),
            pltpu.SemaphoreType.DMA,
            pltpu.SemaphoreType.DMA,
        ],
        compiler_params=pltpu.CompilerParams(
            collective_id=1, has_side_effects=True, vmem_limit_bytes=32 << 20
        ),
    )(part)


SCATTER_STEPS = 22


def tile_of(row):
    return jnp.broadcast_to(row, (row.shape[1], row.shape[1])).T


def scatter_sum(plane, wires, peers, part, out, early, hop, code, got, line, lines, code2, got2, line2, lines2, own):
    others = (2, 1, 3)
    order = (2, 3, 1, 0)

    def block(h, first, second):
        return (h * RING + first) * RING + second

    def column(tile):
        return jnp.concatenate([tile, tile], axis=1)

    announce(peers)
    most = lax.fori_loop(
        0,
        part.shape[0],
        lambda at, most: jnp.maximum(most, jnp.abs(part[at])),
        jnp.zeros(part.shape[1:], jnp.float32),
    )
    most = jnp.broadcast_to(jnp.max(most, axis=1, keepdims=True), line.shape[1:] * 2)
    unit = jnp.maximum(most, LEAST) * (1.0 / TOP)
    line[...] = unit.T[:SUB]
    inverse = column(1.0 / unit)
    pl.semaphore_wait(pltpu.get_barrier_semaphore(), len(peers))
    for h in (0, 1):
        for o in others:
            wires.start(line, lines.at[h, o - 1], plane.device(h, o, 0), h)
    way = {2: 0, 1: 0, 3: 1, 0: 1}
    offset = (1, 3)
    for at, s in enumerate(order):
        for h in (0, 1):
            early[h, s] = encode(part[block(h, 2, s)], inverse)
            wires.start(
                early.at[h, s], hop.at[h, s], plane.device(h, offset[way[s]], 0), 14 + 2 * at + h
            )
    for at, s in enumerate(order):
        w = 1 - way[s]
        for h in (0, 1):
            code[h, s, w] = encode(part[block(h, offset[w], s)], inverse)
            wires.start(
                code.at[h, s, w], got.at[h, s, w], plane.device(h, offset[w], 0), 2 + 2 * at + h
            )
    units, sums = {}, {}
    for h in (0, 1):
        arrived(lines.at[h], wires.recv.at[h])
        units[h] = [tile_of(lines[h, k, 0:1]) for k in range(RING - 1)]
        sums[h] = unit + (units[h][0] + units[h][1] + units[h][2])
        line2[h] = line[...] + (lines[h, 0] + lines[h, 1] + lines[h, 2])
        for s in others:
            wires.start(line2.at[h], lines2.at[h, s - 1], plane.device(h, 0, s), 10 + h)
    for at, s in enumerate(order):
        w = way[s]
        for h in (0, 1):
            near = units[h][offset[w] - 1]
            arrived(hop.at[h, s], wires.recv.at[14 + 2 * at + h])
            merged = part[block(h, offset[w], s)] + decode(hop[h, s], column(near))
            code[h, s, w] = encode(merged, column(1.0 / (unit + near)))
            wires.start(
                code.at[h, s, w], got.at[h, s, w], plane.device(h, offset[w], 0), 2 + 2 * at + h
            )
    for at, s in enumerate(order):
        w = way[s]
        for h in (0, 1):
            arrived(got.at[h, s], wires.recv.at[2 + 2 * at + h])
            both = units[h][offset[w] - 1] + units[h][1]
            total = part[block(h, 0, s)] + decode(got[h, s, w], column(both))
            total = total + decode(got[h, s, 1 - w], column(units[h][offset[1 - w] - 1]))
            if s == 0:
                own[h] = total
            else:
                code2[h, s - 1] = encode(total, column(1.0 / sums[h]))
                wires.start(
                    code2.at[h, s - 1], got2.at[h, s - 1], plane.device(h, 0, s), 12 + h
                )
    for h in (0, 1):
        arrived(lines2.at[h], wires.recv.at[10 + h])
        arrived(got2.at[h], wires.recv.at[12 + h])
        total = own[h]
        for k in range(RING - 1):
            total = total + decode(got2[h, k], column(tile_of(lines2[h, k, 0:1])))
        out[h] = total


def scatter_rooms(depth, width):
    f32 = jnp.float32
    i16 = jnp.int16
    others = RING - 1
    return [
        pltpu.VMEM((2, RING, depth, width), i16),
        pltpu.VMEM((2, RING, depth, width), i16),
        pltpu.VMEM((2, RING, 2, depth, width), i16),
        pltpu.VMEM((2, RING, 2, depth, width), i16),
        pltpu.VMEM((SUB, depth), f32),
        pltpu.VMEM((2, others, SUB, depth), f32),
        pltpu.VMEM((2, others, depth, width), i16),
        pltpu.VMEM((2, others, depth, width), i16),
        pltpu.VMEM((2, SUB, depth), f32),
        pltpu.VMEM((2, others, SUB, depth), f32),
        pltpu.VMEM((2, depth, width), f32),
    ]


SQUARE_STEPS = 3


def sum_square(wires, at, part, out, by_col, by_row, mine):
    rows, cols = lax.axis_size("rows"), lax.axis_size("cols")
    row, col = lax.axis_index("rows"), lax.axis_index("cols")
    share = part.shape[0] // cols
    x, core = col // 2, lax.rem(col, 2)
    z, y = row // RING, lax.rem(row, RING)

    def span(at):
        return pl.ds(at * share, share)

    far = {0: 0, 1: 1, 2: 2, 3: 1}
    col_peers = [
        shifted(x, o) * 2 + lax.rem(core + c, 2)
        for o, c in ((2, 0), (2, 1), (1, 0), (3, 0), (1, 1), (3, 1), (0, 1))
    ]
    steps = [(a, b) for a in range(RING) for b in range(RING) if a or b]
    row_peers = [
        shifted(z, a) * RING + shifted(y, b)
        for a, b in sorted(steps, key=lambda step: -far[step[0]] - far[step[1]])
    ]
    for peer in col_peers:
        wires.start(part.at[span(peer)], by_col.at[col], (row, peer), at)
    by_col[col] = part[span(col)]
    arrived(by_col.at[pl.ds(0, cols - 1)], wires.recv.at[at])
    mine[...] = jnp.sum(by_col[...], axis=0)
    for peer in row_peers:
        wires.start(mine, by_row.at[row], (peer, col), at + 1)
    by_row[row] = mine[...]
    arrived(by_row.at[pl.ds(0, rows - 1)], wires.recv.at[at + 1])
    out[span(col)] = jnp.sum(by_row[...], axis=0)
    for peer in col_peers:
        wires.start(out.at[span(col)], out.at[span(col)], (row, peer), at + 2)
    arrived(out.at[pl.ds(0, (cols - 1) * share)], wires.recv.at[at + 2])
    wires.drain(
        by_col.at[pl.ds(0, cols - 1)],
        by_row.at[pl.ds(0, rows - 1)],
        out.at[pl.ds(0, (cols - 1) * share)],
    )


def square_rooms(order, rows, cols):
    share = order // cols
    return [
        pltpu.VMEM((cols, share, order), jnp.float32),
        pltpu.VMEM((rows, share, order), jnp.float32),
        pltpu.VMEM((share, order), jnp.float32),
    ]


def all_peers():
    rows, cols = lax.axis_size("rows"), lax.axis_size("cols")
    row, col = lax.axis_index("rows"), lax.axis_index("cols")
    return [(lax.rem(row + o, rows), col) for o in range(1, rows)] + [
        (row, lax.rem(col + o, cols)) for o in range(1, cols)
    ]


GROUP = 16


def local_column(column):
    row = lax.axis_index("rows")
    panel, half = column // 16, lax.rem(column, 2)
    along_z = lax.rem(panel // RING + RING - row // RING, RING)
    along_y = lax.rem(lax.rem(panel, RING) + RING - lax.rem(row, RING), RING)
    first = jnp.where(half == 0, along_y, along_z)
    second = jnp.where(half == 0, along_z, along_y)
    return (half * RING + first) * RING + second


def products_kernel(transposed, count_ref, row_ref, col_ref, panels, tiles, out):
    count = count_ref[0, 0]
    out[...] = jnp.zeros_like(out)

    def step(group, carry):
        slots = [group * GROUP + u for u in range(GROUP)]
        rows = [row_ref[0, 0, slot] for slot in slots]
        cols = [local_column(col_ref[0, 0, slot]) for slot in slots]
        if transposed:
            terms = [
                jnp.dot(panels[r], tiles[slot], preferred_element_type=jnp.float32)
                for r, slot in zip(rows, slots)
            ]
        else:
            terms = [
                jnp.dot(tiles[slot], panels[c], preferred_element_type=jnp.float32)
                for c, slot in zip(cols, slots)
            ]
        for slot, term, place in zip(slots, terms, cols if transposed else rows):
            out[place] += jnp.where(slot < count, term, 0.0)
        return carry

    lax.fori_loop(0, (count + GROUP - 1) // GROUP, step, 0)


def products(transposed, out_shape, count, rows, cols, panels, tiles):
    return pl.pallas_call(
        functools.partial(products_kernel, transposed),
        out_shape=jax.ShapeDtypeStruct(out_shape, jnp.float32),
        in_specs=[VMEM, SMEM, SMEM, VMEM, VMEM],
        out_specs=VMEM,
        compiler_params=pltpu.CompilerParams(vmem_limit_bytes=32 << 20),
    )(count, rows, cols, panels, tiles)


def factor(gram, upper_ref, inverse_ref):
    order = gram.shape[0]
    lead = gram
    tail = (
        lax.broadcasted_iota(jnp.int32, (order, order), 0)
        == lax.broadcasted_iota(jnp.int32, (order, order), 1)
    ).astype(jnp.float32)
    for base in range(0, order, SUB):
        left = order - base
        columns = [
            jnp.broadcast_to(lead[:, base + k : base + k + 1], (left, order)) for k in range(SUB)
        ]
        position = lax.broadcasted_iota(jnp.int32, (left, order), 0)
        top = lax.broadcasted_iota(jnp.int32, (SUB, order), 0)
        lane = lax.broadcasted_iota(jnp.int32, (SUB, order), 1)
        pivots = jnp.zeros((SUB, order), jnp.float32)
        for k in range(SUB):
            pivot = columns[k][k : k + 1, :]
            pivots = jnp.where(top == k, pivot, pivots)
            ratio = jnp.where(position > k, columns[k] * (1.0 / pivot), 0.0)
            lead = lead - ratio * lead[k : k + 1, :]
            tail = tail - ratio * tail[k : k + 1, :]
            for j in range(k + 1, SUB):
                columns[j] = columns[j] - ratio * columns[j][k : k + 1, :]
        scale = 1.0 / jnp.sqrt(pivots)
        upper_ref[base : base + SUB, :] = jnp.where(lane >= base + top, lead[:SUB] * scale, 0.0)
        inverse_ref[base : base + SUB, :] = tail[:SUB] * scale
        lead = lead[SUB:]
        tail = tail[SUB:]


def inner(x_ref, out):
    out[...] = matmul(x_ref[0], x_ref[0], NT) + matmul(x_ref[1], x_ref[1], NT)


def basis_kernel(
    root, part, basis_ref, triangle_ref, spread_ref, x_ref, square, gram, inverse, *rest
):
    rooms, (by_col, by_row, mine, send, recv, send2) = rest[:11], rest[11:]
    plane = Plane()
    wires = Wires(send, recv)
    row, cols = lax.axis_index("rows"), lax.axis_size("cols")
    peers = plane.neighbours() + [
        (row, lax.rem(plane.col + o, cols)) for o in range(1, cols)
    ]
    scatter_sum(plane, wires, peers, part, x_ref, *rooms)
    inner(x_ref, square)
    wires.send = send2
    sum_square(wires, SCATTER_STEPS, square, gram, by_col, by_row, mine)
    factor(gram[...], triangle_ref, inverse)
    width = x_ref.shape[2]
    for s in range(2):
        basis_ref[s * width : (s + 1) * width, :] = matmul(inverse[...], x_ref[s], NN).T * root
    triangle_ref[...] = triangle_ref[...] / root
    order = gram.shape[0]
    diagonal = lax.broadcasted_iota(jnp.int32, (order, order), 0) == lax.broadcasted_iota(
        jnp.int32, (order, order), 1
    )
    lengths = jnp.sum(jnp.where(diagonal, gram[...], 0.0), axis=0, keepdims=True)
    inverses = jnp.sum(inverse[...] * inverse[...], axis=0, keepdims=True)
    spread = jnp.sum(lengths * inverses, axis=1, keepdims=True)
    spread_ref[0, 0] = spread[0, 0]
    wires.send = send
    early, hop, code, got, line, lines, code2, got2, line2, lines2, own = rooms
    wires.drain(hop, got, got2, lines, lines2)


def orthonormalize(root, part):
    _, depth, width = part.shape
    rows, cols = lax.axis_size("rows"), lax.axis_size("cols")
    f32 = jnp.float32
    square = pltpu.VMEM((depth, depth), f32)
    return pl.pallas_call(
        functools.partial(basis_kernel, root),
        out_shape=[
            jax.ShapeDtypeStruct((2 * width, depth), f32),
            jax.ShapeDtypeStruct((depth, depth), f32),
            jax.ShapeDtypeStruct((1, 1), f32),
        ],
        in_specs=[VMEM],
        out_specs=[VMEM, VMEM, SMEM],
        scratch_shapes=[pltpu.VMEM((2, depth, width), f32)]
        + [square] * 3
        + scatter_rooms(depth, width)
        + square_rooms(depth, rows, cols)
        + [
            pltpu.SemaphoreType.DMA,
            pltpu.SemaphoreType.DMA((SCATTER_STEPS + SQUARE_STEPS,)),
            pltpu.SemaphoreType.DMA,
        ],
        compiler_params=pltpu.CompilerParams(
            collective_id=2, has_side_effects=True, vmem_limit_bytes=40 << 20
        ),
    )(part)


def again_kernel(
    root, basis_in, triangle_in, basis_ref, triangle_ref, x, square, gram, upper, inverse, *rest
):
    by_col, by_row, mine, send, recv = rest
    wires = Wires(send, recv)
    greet(all_peers())
    x[...] = basis_in[...].T / root
    square[...] = matmul(x[...], x[...], NT)
    sum_square(wires, 0, square, gram, by_col, by_row, mine)
    factor(gram[...], upper, inverse)
    basis_ref[...] = matmul(inverse[...], x[...], NN).T * root
    triangle_ref[...] = matmul(upper[...], triangle_in[...], NN)


def second_pass(root, basis, triangle):
    size, depth = basis.shape
    f32 = jnp.float32
    return pl.pallas_call(
        functools.partial(again_kernel, root),
        out_shape=[
            jax.ShapeDtypeStruct(basis.shape, f32),
            jax.ShapeDtypeStruct(triangle.shape, f32),
        ],
        in_specs=[VMEM] * 2,
        out_specs=[VMEM] * 2,
        scratch_shapes=[pltpu.VMEM((depth, size), f32)]
        + [pltpu.VMEM((depth, depth), f32)] * 4
        + square_rooms(depth, lax.axis_size("rows"), lax.axis_size("cols"))
        + [pltpu.SemaphoreType.DMA, pltpu.SemaphoreType.DMA((SQUARE_STEPS,))],
        compiler_params=pltpu.CompilerParams(
            collective_id=3, has_side_effects=True, vmem_limit_bytes=32 << 20
        ),
    )(basis, triangle)


def body(start_basis, block_values, slot_count, slot_row, slot_col):
    depth = start_basis.shape[1]
    width = block_values.shape[-1]
    panel_blocks = start_basis.shape[0] // width
    rows, cols = lax.axis_size("rows"), lax.axis_size("cols")
    column_blocks = rows * panel_blocks // cols
    held = [
        pltpu.with_memory_space_constraint(array, pltpu.HBM)
        for array in (
            start_basis.reshape(panel_blocks, width, depth),
            block_values.reshape(block_values.shape[2:]),
            slot_row,
            slot_col,
        )
    ]
    basis_parts, tiles, *indices = gather(*held[:2], held[2:], rows)
    image_part = products(
        False,
        (panel_blocks, width, depth),
        slot_count,
        *indices,
        basis_parts.reshape(column_blocks, width, depth),
        tiles,
    )
    image = sum_image(image_part)
    back_part = products(
        True, (column_blocks, depth, width), slot_count, *indices, image, tiles
    )
    root = float(rows * panel_blocks * width) ** 0.5
    basis, triangle, spread = orthonormalize(root, back_part)
    return lax.cond(
        spread[0, 0] <= 2.0 * depth,
        lambda basis, triangle: (basis, triangle),
        functools.partial(second_pass, root),
        basis,
        triangle,
    )


def solution(mesh):
    return jax.shard_map(
        body,
        mesh=mesh,
        in_specs=(
            P("rows", None),
            P("rows", "cols", None, None, None),
            P("rows", "cols"),
            P("rows", "cols", None),
            P("rows", "cols", None),
        ),
        out_specs=(P(("rows", "cols"), None), P()),
        check_vma=False,
    )
```
